128 devices in a mesh: seq: 8 (over z, x_hi), fsdp: 16 (over x_lo, y, core).
Axes of the slice: x: 4 (x_hi: 2, x_lo: 2; x = x_hi * 2 + x_lo), y: 4, z: 4, core: 2. Of those that a mesh axis runs over, the one named last changes fastest.
Arguments:
- tokens: bfloat16 [16384, 1024], P(('fsdp', 'seq')), may hold values from -6 to 6
- segments: int32 [16384], replicated, may hold values from 0 to 3, as said below
- cotangent: bfloat16 [16384, 1024], P(('fsdp', 'seq')), may hold values from -6 to 6
- attention_gain: bfloat16 [1024], P('fsdp'), may hold values from 0.5 to 1.5
- query_gain: bfloat16 [64], P('fsdp'), may hold values from 0.69921875 to 2
- key_gain: bfloat16 [64], P('fsdp'), may hold values from 0.69921875 to 2
- query_weight: bfloat16 [1024, 1024], P('fsdp'), may hold values from -0.1875 to 0.1875
- key_weight: bfloat16 [1024, 512], P('fsdp'), may hold values from -0.1875 to 0.1875
- value_weight: bfloat16 [1024, 512], P('fsdp'), may hold values from -0.1875 to 0.1875
- out_weight: bfloat16 [1024, 1024], P('fsdp'), may hold values from -1.5 to 1.5
- feedforward_gain: bfloat16 [1024], P('fsdp'), may hold values from 0.5 to 1.5
- gate_weight: bfloat16 [1024, 4608], P('fsdp'), may hold values from -0.1875 to 0.1875
- up_weight: bfloat16 [1024, 4608], P('fsdp'), may hold values from -0.1875 to 0.1875
- down_weight: bfloat16 [4608, 1024], P('fsdp'), may hold values from -0.09375 to 0.09375
Outputs:
- layer_out: bfloat16 [16384, 1024], P(('fsdp', 'seq'))
- input_grad: float32 [16384, 1024], P(('fsdp', 'seq'))
- grad_attention_gain: float32 [1024], P('fsdp')
- grad_query_gain: float32 [64], P('fsdp')
- grad_key_gain: float32 [64], P('fsdp')
- grad_query_weight: float32 [1024, 1024], P('fsdp')
- grad_key_weight: float32 [1024, 512], P('fsdp')
- grad_value_weight: float32 [1024, 512], P('fsdp')
- grad_out_weight: float32 [1024, 1024], P('fsdp')
- grad_feedforward_gain: float32 [1024], P('fsdp')
- grad_gate_weight: float32 [1024, 4608], P('fsdp')
- grad_up_weight: float32 [1024, 4608], P('fsdp')
- grad_down_weight: float32 [4608, 1024], P('fsdp')
The draws below stay inside these ranges and needn't reach their ends.
Inputs may be any that keep to these rules, and one draw needn't show every extreme that they name: `segments`: segment ids never fall along the stream, every id from 0 to 3 occurs, no document has more than 8192 tokens, and one has exactly 8192.
All inputs are finite; a program needn't handle non-finite values.
Results may differ from the reference program's by a relative error of at most 0.03.
Values may be sent and summed in bfloat16 or wider, within the bound.
A program may use at most 192 MiB of HBM per device.

```python
import math
import jax
import jax.numpy as jnp
from jax import lax

D = 1024
H = 16
KVH = 8
HD = 64
FF = 4608
TOK_DEV = 128
DOCS = 4
SEQLEN = 16384


def draw_segments(key, part):
    first_key, second_key = jax.random.split(key, 2)
    half = SEQLEN // 2
    doc_start = jax.random.randint(first_key, (), 1, TOK_DEV + 1)
    last_cut = jax.random.randint(second_key, (), doc_start + half + 1, SEQLEN)
    index = jnp.arange(SEQLEN, dtype=jnp.int32)
    return (index >= doc_start).astype(jnp.int32) + (index >= doc_start + half).astype(jnp.int32) + (index >= last_cut).astype(jnp.int32)


def steps_of(rng, shape, cuts, low, largest):
    gain = 1.0
    for position, shards_of in cuts:
        heights = jax.random.uniform(jax.random.fold_in(jax.random.fold_in(rng, 6), position), (shards_of,), jnp.float32, low / len(cuts), largest / len(cuts))
        gain = gain * jnp.repeat(jnp.exp(heights), shape[position] // shards_of).reshape((-1,) + (1,) * (len(shape) - 1 - position))
    return gain


def normal_values(rng, shape, scale, most, cuts=(), held_as=jnp.bfloat16):
    result = scale * jax.random.normal(rng, shape, jnp.float32)
    if cuts:
        result = result * steps_of(rng, shape, cuts, -0.22, 0.18)
    return jnp.clip(result, -most, most).astype(held_as)


def setup_inputs(seed: int = 0) -> dict:
    keys = jax.random.split(jax.random.key(seed), 15)
    return {
        "tokens": normal_values(keys[0], (SEQLEN, D), 1.0, 6.0, ((0, 128),)),
        "segments": draw_segments(jax.random.fold_in(keys[14], 71), 0),
        "cotangent": normal_values(keys[2], (SEQLEN, D), 1.0, 6.0, ((0, 128),)),
        "attention_gain": jnp.clip(1.0 + 0.1 * jax.random.normal(keys[3], (D,), jnp.float32), 0.5, 1.5).astype(jnp.bfloat16),
        "query_gain": jnp.clip(jnp.exp(math.log(2.0) - 1.0509388 * jax.random.uniform(keys[4], (HD,), jnp.float32) ** steps_of(keys[4], (HD,), ((0, 16),), -0.2, 0.2)), 0.69921875, 2.0).astype(jnp.bfloat16),
        "key_gain": jnp.clip(jnp.exp(math.log(2.0) - 1.0509388 * jax.random.uniform(keys[5], (HD,), jnp.float32) ** steps_of(keys[5], (HD,), ((0, 16),), -0.2, 0.2)), 0.69921875, 2.0).astype(jnp.bfloat16),
        "query_weight": normal_values(keys[6], (D, H * HD), D ** -0.5, 0.1875, ((0, 16),)),
        "key_weight": normal_values(keys[7], (D, KVH * HD), D ** -0.5, 0.1875, ((0, 16),)),
        "value_weight": normal_values(keys[8], (D, KVH * HD), D ** -0.5, 0.1875, ((0, 16),)),
        "out_weight": normal_values(keys[9], (H * HD, D), (H * HD // 64) ** -0.5, 1.5, ((0, 16),)),
        "feedforward_gain": jnp.clip(1.0 + 0.1 * jax.random.normal(keys[10], (D,), jnp.float32), 0.5, 1.5).astype(jnp.bfloat16),
        "gate_weight": normal_values(keys[11], (D, FF), D ** -0.5, 0.1875, ((0, 16),)),
        "up_weight": normal_values(keys[12], (D, FF), D ** -0.5, 0.1875, ((0, 16),)),
        "down_weight": normal_values(keys[13], (FF, D), FF ** -0.5, 0.09375, ((0, 16),)),
    }


EPSILON = 1e-06
THETA = 1000000.0

@jax.custom_vjp
def low(v):
    return lax.optimization_barrier(v.astype(jnp.bfloat16)).astype(jnp.float32)

@jax.custom_vjp
def low_back(v):
    return v

def low_keep(v):
    return (low(v), None)

def low_pass(kept, grad):
    return (grad,)

def back_keep(v):
    return (v, None)

def back_low(kept, grad):
    return (low(grad),)
low.defvjp(low_keep, low_pass)
low_back.defvjp(back_keep, back_low)

def matmul(left, right):
    return jnp.dot(left, right, precision=lax.Precision.HIGHEST, preferred_element_type=jnp.float32)

def rms_scale(values):
    return lax.rsqrt(lax.optimization_barrier(jnp.mean(values * values, axis=-1, keepdims=True)) + EPSILON)

def doc_positions(segments, first, count):
    labels = jnp.arange(DOCS, dtype=jnp.int32)
    member = (segments[None, :] == labels[:, None]).astype(jnp.int32)
    lengths = lax.optimization_barrier(jnp.sum(member, axis=1))
    starts = jnp.cumsum(lengths) - lengths
    local_ids = lax.dynamic_slice_in_dim(segments, first, count)
    picked = (local_ids[:, None] == labels[None, :]).astype(jnp.int32)
    index = first + jnp.arange(count, dtype=jnp.int32)
    return index - lax.optimization_barrier(jnp.sum(picked * starts[None, :], axis=1))

def rope_tables(positions, width):
    half = width // 2
    freqs = THETA ** (-2.0 * jnp.arange(half, dtype=jnp.float32) / width)
    angles = positions.astype(jnp.float32)[:, None] * freqs[None, :]
    return (jnp.cos(angles), jnp.sin(angles))

def rotate(values, cosine, sine):
    half = values.shape[-1] // 2
    first_half = values[..., :half]
    second_half = values[..., half:]
    cos_rows = cosine[:, None, :]
    sin_rows = sine[:, None, :]
    return jnp.concatenate([first_half * cos_rows - second_half * sin_rows, second_half * cos_rows + first_half * sin_rows], axis=-1)

def attention(query, key, value, segments, bound):
    total = query.shape[0]
    block = min(512, total)
    query_blocks = query.reshape(total // block, block, KVH, H // KVH, HD)
    starts = block * jnp.arange(total // block, dtype=jnp.int32)
    key_index = jnp.arange(total, dtype=jnp.int32)
    scale = HD ** (-0.5)

    @jax.checkpoint
    def one_block(item):
        query_block, start = item
        raw = jnp.einsum('sgrd,pgd->grsp', query_block, key, precision=lax.Precision.HIGHEST) * scale
        scores = low_back(raw)
        query_index = start + jnp.arange(block, dtype=jnp.int32)
        query_ids = lax.dynamic_slice_in_dim(segments, start, block)
        allowed = (key_index[None, :] <= query_index[:, None]) & (segments[None, :] == query_ids[:, None])
        exps = jnp.where(allowed, jnp.exp(scores - bound), 0.0)
        totals = lax.optimization_barrier(jnp.sum(exps, axis=-1))
        sums = low_back(jnp.einsum('grsp,pgd->sgrd', low(exps), value, precision=lax.Precision.HIGHEST))
        return sums / jnp.transpose(totals, (2, 0, 1))[..., None]
    outputs = lax.map(one_block, (query_blocks, starts))
    return low_back(low(outputs.reshape(total, H * HD)))

def layer(inputs, gain_one, query_scale, key_scale, query_weight, key_weight, value_weight, out_weight, gain_two, gate_weight, up_weight, down_weight, segments, bound):
    total = inputs.shape[0]
    positions = doc_positions(segments, 0, total)
    cosine, sine = rope_tables(positions, HD)
    normed_one = low(inputs * rms_scale(inputs) * gain_one)
    query_pre = low_back(matmul(normed_one, query_weight)).reshape(total, H, HD)
    key_pre = low_back(matmul(normed_one, key_weight)).reshape(total, KVH, HD)
    value = low_back(low(matmul(normed_one, value_weight))).reshape(total, KVH, HD)
    query = low_back(low(rotate(query_pre * rms_scale(query_pre) * query_scale, cosine, sine)))
    key = low_back(low(rotate(key_pre * rms_scale(key_pre) * key_scale, cosine, sine)))
    attended = attention(query, key, value, segments, bound)
    hidden_state = inputs + low_back(matmul(attended, out_weight))
    normed_two = low(hidden_state * rms_scale(hidden_state) * gain_two)
    gate = low_back(matmul(normed_two, gate_weight))
    up_proj = low_back(matmul(normed_two, up_weight))
    activated = low(jax.nn.silu(gate) * up_proj)
    return hidden_state + low_back(matmul(activated, down_weight))

def reference(tokens, segments, cotangent, attention_gain, query_gain, key_gain, query_weight, key_weight, value_weight, out_weight, feedforward_gain, gate_weight, up_weight, down_weight):
    inputs = tokens.astype(jnp.float32)
    gain_one = attention_gain.astype(jnp.float32)
    query_scale = query_gain.astype(jnp.float32)
    key_scale = key_gain.astype(jnp.float32)
    weight_query = query_weight.astype(jnp.float32)
    weight_key = key_weight.astype(jnp.float32)
    weight_value = value_weight.astype(jnp.float32)
    weight_out = out_weight.astype(jnp.float32)
    gain_two = feedforward_gain.astype(jnp.float32)
    weight_gate = gate_weight.astype(jnp.float32)
    weight_up = up_weight.astype(jnp.float32)
    weight_down = down_weight.astype(jnp.float32)
    bound = HD ** (-0.5) * HD * jnp.max(jnp.abs(query_scale)) * jnp.max(jnp.abs(key_scale))

    def forward(inputs, gain_one, query_scale, key_scale, weight_query, weight_key, weight_value, weight_out, gain_two, weight_gate, weight_up, weight_down):
        return layer(inputs, gain_one, query_scale, key_scale, weight_query, weight_key, weight_value, weight_out, gain_two, weight_gate, weight_up, weight_down, segments, bound)
    output, pullback = jax.vjp(forward, inputs, gain_one, query_scale, key_scale, weight_query, weight_key, weight_value, weight_out, gain_two, weight_gate, weight_up, weight_down)
    grads = pullback(cotangent.astype(jnp.float32))
    return (output.astype(jnp.bfloat16), grads[0], grads[1], grads[2], grads[3], grads[4], grads[5], grads[6], grads[7], grads[8], grads[9], grads[10], grads[11])
```

```python
import functools
import math

import jax
import jax.numpy as jnp
from jax import lax
from jax.experimental import pallas as pl
from jax.experimental.pallas import tpu as pltpu
from jax.sharding import PartitionSpec as P

H = 16
KVH = 8
HD = 64
DOCS = 4
EPSILON = 1e-06
THETA = 1000000.0
LOG2E = math.log2(math.e)
F32 = jnp.float32
BF16 = jnp.bfloat16
TILE = 512
KEYS = 512
VMEM = 56 * 1024 * 1024
PIECE = 48


def rms_scale(values):
    return lax.rsqrt(jnp.mean(values * values, axis=-1, keepdims=True) + EPSILON)


def norm_back(values, inverse, gain, grad):
    normalized = values * inverse
    gain_term = jnp.sum(grad * normalized, axis=tuple(range(grad.ndim - 1)))
    weighted = grad * gain
    inner = jnp.mean(weighted * normalized, axis=-1, keepdims=True)
    return (gain_term, inverse * (weighted - normalized * inner))


def doc_starts(segments):
    labels = jnp.arange(DOCS, dtype=jnp.int32)
    member = (segments[None, :] == labels[:, None]).astype(jnp.int32)
    lengths = jnp.sum(member, axis=1)
    return jnp.cumsum(lengths) - lengths


def rotate(values, cosine, sine):
    half = values.shape[-1] // 2
    first, second = values[..., :half], values[..., half:]
    return jnp.concatenate(
        [first * cosine - second * sine, second * cosine + first * sine], axis=-1
    )


def dot_nt(a, b):
    return lax.dot_general(a, b, (((1,), (1,)), ((), ())), preferred_element_type=F32)


def dot_tn(a, b):
    return lax.dot_general(a, b, (((0,), (0,)), ((), ())), preferred_element_type=F32)


def dot_nn(a, b):
    return jnp.dot(a, b, preferred_element_type=F32)


def key_loops(ranges_ref, tile, step):
    low, inner_low, inner_high, high = [ranges_ref[i, tile] for i in range(4)]

    def masked(block, _):
        step(block, True)
        return 0

    def plain(block, _):
        step(block, False)
        return 0

    lax.fori_loop(low, inner_low, masked, 0)
    lax.fori_loop(inner_low, inner_high, plain, 0)
    lax.fori_loop(inner_high, high, masked, 0)


def forward_kernel(ranges_ref, shift_ref, query_ref, first_ref, kv_ref, sums_ref, totals_ref, total):
    tile = pl.program_id(0)
    rows = query_ref.shape[1]
    query = query_ref[...].reshape(2 * rows, 2 * HD)
    first = jnp.concatenate([first_ref[...]] * 2, axis=0)
    index = ranges_ref[4, tile] + lax.broadcasted_iota(jnp.int32, (rows, 1), 0)
    index = jnp.concatenate([index, index], axis=0)
    shift = shift_ref[0]
    ones = jnp.ones((KEYS, 2 * HD), BF16)
    total[...] = jnp.zeros_like(total)

    def step(block, masked):
        start = pl.multiple_of(block * KEYS, KEYS)
        kv = kv_ref[pl.ds(start, KEYS), :]
        exps = jnp.exp2(dot_nt(query, kv) * (LOG2E * HD**-0.5) - shift)
        if masked:
            keys = start + lax.broadcasted_iota(jnp.int32, (2 * rows, KEYS), 1)
            exps = jnp.where((keys >= first) & (keys <= index), exps, 0.0)
        total[...] += dot_nn(exps.astype(BF16), jnp.concatenate([kv, ones], axis=1))

    key_loops(ranges_ref, tile, step)
    sums_ref[...] = total[:, : 2 * HD].reshape(2, rows, 2 * HD)
    totals_ref[...] = total[:, 2 * HD :].reshape(2, rows, 2 * HD)


def forward_attention(ranges, shift, query, first, kv):
    rows = query.shape[1]
    tiles = rows // TILE
    whole = lambda t, *_: (0, 0)
    part = lambda t, *_: (0, t, 0)
    return pl.pallas_call(
        forward_kernel,
        grid_spec=pltpu.PrefetchScalarGridSpec(
            num_scalar_prefetch=2,
            grid=(tiles,),
            in_specs=[
                pl.BlockSpec((2, TILE, 2 * HD), part),
                pl.BlockSpec((TILE, 1), lambda t, *_: (t, 0)),
                pl.BlockSpec(kv.shape, whole),
            ],
            out_specs=[
                pl.BlockSpec((2, TILE, 2 * HD), part),
                pl.BlockSpec((2, TILE, 2 * HD), part),
            ],
            scratch_shapes=[pltpu.VMEM((2 * TILE, 4 * HD), F32)],
        ),
        out_shape=[jax.ShapeDtypeStruct(query.shape, F32)] * 2,
        compiler_params=pltpu.CompilerParams(vmem_limit_bytes=VMEM),
        cost_estimate=pl.CostEstimate(
            flops=8 * 10**9, bytes_accessed=8 * 10**6, transcendentals=16 * 10**6
        ),
        name="attention_forward",
    )(ranges, shift, query, first, kv)


def backward_kernel(
    ranges_ref, shift_ref, query_ref, grad_ref, delta_ref, first_ref, kv_ref, gq_ref, gkv_ref, total
):
    tile = pl.program_id(0)
    rows = query_ref.shape[1]
    query = query_ref[...].reshape(2 * rows, 2 * HD)
    grad = grad_ref[...].reshape(2 * rows, 2 * HD)
    delta = delta_ref[...].reshape(1, 2 * rows)
    first = first_ref[...].reshape(1, 2 * rows)
    index = ranges_ref[4, tile] + lax.broadcasted_iota(jnp.int32, (1, rows), 1)
    index = jnp.concatenate([index, index], axis=1)
    shift = shift_ref[0]

    @pl.when(tile == 0)
    def _():
        total[...] = jnp.zeros_like(total)

    gq_ref[...] = jnp.zeros_like(gq_ref)

    def step(block, masked):
        start = pl.multiple_of(block * KEYS, KEYS)
        kv = kv_ref[pl.ds(start, KEYS), :]
        exps = jnp.exp2(dot_nt(kv, query) * (LOG2E * HD**-0.5) - shift)
        if masked:
            keys = start + lax.broadcasted_iota(jnp.int32, (KEYS, 2 * rows), 0)
            exps = jnp.where((keys >= first) & (keys <= index), exps, 0.0)
        scores = (exps * (dot_nt(kv, grad) - delta)).astype(BF16)
        gq_ref[...] += dot_tn(scores, kv).reshape(gq_ref.shape)
        total[pl.ds(start, KEYS), :] += dot_nn(scores, query) * HD**-0.5 + dot_nn(
            exps.astype(BF16), grad
        )

    key_loops(ranges_ref, tile, step)

    @pl.when(tile == pl.num_programs(0) - 1)
    def _():
        gkv_ref[...] = total[...].astype(BF16)


def backward_attention(ranges, shift, query, grad, delta, first, kv):
    rows = query.shape[1]
    tiles = rows // TILE
    whole = lambda t, *_: (0, 0)
    part = lambda t, *_: (0, t, 0)
    row = lambda t, *_: (t, 0, 0)
    return pl.pallas_call(
        backward_kernel,
        grid_spec=pltpu.PrefetchScalarGridSpec(
            num_scalar_prefetch=2,
            grid=(tiles,),
            in_specs=[
                pl.BlockSpec((2, TILE, 2 * HD), part),
                pl.BlockSpec((2, TILE, 2 * HD), part),
                pl.BlockSpec((1, 1, 2 * TILE), row),
                pl.BlockSpec((1, 1, 2 * TILE), row),
                pl.BlockSpec(kv.shape, whole),
            ],
            out_specs=[
                pl.BlockSpec((2, TILE, 2 * HD), part),
                pl.BlockSpec(kv.shape, whole),
            ],
            scratch_shapes=[pltpu.VMEM(kv.shape, F32)],
        ),
        out_shape=[
            jax.ShapeDtypeStruct(query.shape, F32),
            jax.ShapeDtypeStruct(kv.shape, BF16),
        ],
        compiler_params=pltpu.CompilerParams(vmem_limit_bytes=VMEM),
        cost_estimate=pl.CostEstimate(
            flops=20 * 10**9, bytes_accessed=16 * 10**6, transcendentals=16 * 10**6
        ),
        name="attention_backward",
    )(ranges, shift, query, grad, delta, first, kv)


MESH = pl.DeviceIdType.MESH
HBM = pl.BlockSpec(memory_space=pl.ANY)
IN_VMEM = pl.BlockSpec(memory_space=pltpu.VMEM)
RING = 8


def pair_of(value):
    return value + 1 - 2 * lax.rem(value, 2)


def ring_step(index, steps):
    return lax.div(index, RING) * RING + lax.rem(lax.rem(index, RING) + 2 * steps, RING)


class Copies:
    def __init__(self, send, recv, local):
        self.send, self.recv, self.local = send, recv, local
        self.started, self.locals = [], []

    def remote(self, src, dst, peer):
        i = len(self.started)
        copy = pltpu.make_async_remote_copy(
            src_ref=src,
            dst_ref=dst,
            send_sem=self.send.at[i],
            recv_sem=self.recv.at[i],
            device_id=peer,
            device_id_type=MESH,
        )
        copy.start()
        self.started.append(copy)
        return copy

    def here(self, src, dst):
        copy = pltpu.make_async_copy(src, dst, self.local.at[len(self.locals)])
        copy.start()
        self.locals.append(copy)
        return copy

    def finish(self):
        for copy in self.started:
            copy.wait_send()


def greet(peers):
    barrier = pltpu.get_barrier_semaphore()
    for peer in peers:
        pl.semaphore_signal(barrier, inc=1, device_id=peer, device_id_type=MESH)
    pl.semaphore_wait(barrier, len(peers))


def slot(ref, axis, size, index, split=None, half=0):
    start = index * size
    where = [pl.ds(0, n) for n in ref.shape]
    where[axis] = pl.ds(pl.multiple_of(start, 16), size)
    if split is not None:
        along, cut = split
        whole = size if along == axis else ref.shape[along]
        base = start if along == axis else 0
        begin, count = (0, cut) if half == 0 else (cut, whole - cut)
        offset = base + begin
        where[along] = pl.ds(pl.multiple_of(offset, 16) if along == axis else offset, count)
    return ref.at[tuple(where)]


def gather_stages(copies, src, out, axis, size, split, me, pair, device, sibling):
    plus, minus = ring_step(me, 1), ring_step(me, 3)
    at = functools.partial(slot, out, axis, size)
    halves = lambda index, half: at(index, split, half)
    to_sibling = []

    def pass_on(index):
        if sibling is not None:
            to_sibling.append(copies.remote(at(index), at(index), device(sibling)))

    kept = copies.here(src, at(me))
    first = copies.remote(src, at(me), device(pair))
    up = copies.remote(src, at(me), device(plus))
    down = copies.remote(src, at(me), device(minus))
    if sibling is not None:
        to_sibling.append(copies.remote(src, at(me), device(sibling)))
    yield
    up.wait_recv()
    far = [copies.remote(halves(minus, 0), halves(minus, 0), device(plus))]
    pass_on(minus)
    down.wait_recv()
    far.append(copies.remote(halves(plus, 1), halves(plus, 1), device(minus)))
    pass_on(plus)
    yield
    first.wait_recv()
    up = copies.remote(at(pair), at(pair), device(plus))
    down = copies.remote(at(pair), at(pair), device(minus))
    pass_on(pair)
    yield
    shift = pair - me
    up.wait_recv()
    last = [copies.remote(halves(minus + shift, 0), halves(minus + shift, 0), device(plus))]
    pass_on(minus + shift)
    down.wait_recv()
    last.append(copies.remote(halves(plus + shift, 1), halves(plus + shift, 1), device(minus)))
    pass_on(plus + shift)
    yield
    opposite = ring_step(me, 2)
    for copy in far:
        copy.wait_recv()
    pass_on(opposite)
    yield
    for copy in last:
        copy.wait_recv()
    pass_on(opposite + shift)
    yield
    for copy in to_sibling:
        copy.wait_recv()
    kept.wait()


def run_stages(stages):
    live = list(stages)
    while live:
        live = [stage for stage in live if next(stage, stage) is not stage]


class Places:
    def __init__(self):
        self.seq, self.fsdp = lax.axis_index("seq"), lax.axis_index("fsdp")
        self.core = lax.rem(self.fsdp, 2)
        self.chip = lax.div(self.fsdp, 2)
        self.row = lax.div(self.chip, 4)
        self.col = lax.rem(self.chip, 4)
        self.sibling = pair_of(self.fsdp)
        self.across = lax.rem(self.fsdp + 8, 16)

    def on_seq(self, index):
        return (index, self.fsdp)

    def on_fsdp(self, index):
        return (self.seq, index)

    def other_seq(self, step):
        return lax.rem(self.seq + step, 8)

    def other_chip(self, step):
        return lax.rem(self.row + step // 4, 2) * 4 + lax.rem(self.col + step % 4, 4)

    def gather_peers(self):
        seq = [pair_of(self.seq), ring_step(self.seq, 1), ring_step(self.seq, 3)]
        fsdp = [self.across, ring_step(self.fsdp, 1), ring_step(self.fsdp, 3), self.sibling]
        return [self.on_seq(i) for i in seq] + [self.on_fsdp(i) for i in fsdp]

    def scatter_peers(self):
        seq = [self.on_seq(self.other_seq(d)) for d in range(1, 8)]
        fsdp = [self.on_fsdp(self.other_chip(d) * 2 + self.core) for d in range(1, 8)]
        return seq + fsdp + [self.on_fsdp(self.sibling)]


def params(name_id):
    return pltpu.CompilerParams(
        collective_id=name_id, has_side_effects=True, vmem_limit_bytes=VMEM
    )


def semaphores(remote, local):
    return [
        pltpu.SemaphoreType.DMA((remote,)),
        pltpu.SemaphoreType.DMA((remote,)),
        pltpu.SemaphoreType.DMA((local,)),
    ]


def seq_gather(copies, places, src, out, axis, split):
    size = src.shape[axis]
    return gather_stages(
        copies, src, out, axis, size, split, places.seq, pair_of(places.seq), places.on_seq, None
    )


def fsdp_gather(copies, places, src, out, axis, split):
    size = src.shape[axis]
    return gather_stages(
        copies, src, out, axis, size, split, places.fsdp, places.across, places.on_fsdp, places.sibling
    )


def gather(name, name_id, seq_items, fsdp_items):
    items = seq_items + fsdp_items
    count = len(items)

    def kernel(*refs):
        srcs, outs = refs[:count], refs[count : 2 * count]
        copies, places = Copies(*refs[2 * count :]), Places()
        greet(places.gather_peers())
        stages = []
        for i, (_, axis, split) in enumerate(items):
            make = seq_gather if i < len(seq_items) else fsdp_gather
            stages.append(make(copies, places, srcs[i], outs[i], axis, split))
        run_stages(stages)
        copies.finish()

    shapes = []
    for i, (array, axis, _) in enumerate(items):
        shape = list(array.shape)
        shape[axis] *= 8 if i < len(seq_items) else 16
        shapes.append(jax.ShapeDtypeStruct(tuple(shape), array.dtype))
    return pl.pallas_call(
        kernel,
        out_shape=shapes,
        in_specs=[HBM] * count,
        out_specs=[HBM] * count,
        scratch_shapes=semaphores(9 * len(seq_items) + 17 * len(fsdp_items), count),
        compiler_params=params(name_id),
        name=name,
    )(*[item[0] for item in items])


class SeqSum:
    def __init__(self, copies, places, part, held):
        self.held = held
        self.kept = copies.here(part.at[places.seq], held.at[0])
        self.copies = []
        for d in (4, 3, 5, 2, 6, 1, 7):
            peer = places.other_seq(d)
            self.copies.append(copies.remote(part.at[peer], held.at[d], places.on_seq(peer)))

    def total(self):
        self.kept.wait()
        for copy in self.copies:
            copy.wait_recv()
        total = self.held[0].astype(F32)
        for d in range(1, 8):
            total += self.held[d].astype(F32)
        return total


class FsdpSum:
    def __init__(self, copies, places, part, mine, theirs, held):
        self.remote, self.places = copies.remote, places
        self.mine, self.theirs, self.held = mine, theirs, held
        self.other = copies.remote(
            part.at[:, 1 - places.core], theirs, places.on_fsdp(places.sibling)
        )
        self.kept = copies.here(part.at[:, places.core], mine)

    def send(self):
        self.kept.wait()
        self.other.wait_recv()
        self.copies = []
        for d in (2, 6, 4, 5, 7, 1, 3):
            chip = self.places.other_chip(d)
            self.mine[chip] = (
                self.mine[chip].astype(F32) + self.theirs[chip].astype(F32)
            ).astype(BF16)
            peer = self.places.on_fsdp(chip * 2 + self.places.core)
            self.copies.append(self.remote(self.mine.at[chip], self.held.at[d], peer))

    def total(self):
        chip = self.places.chip
        total = self.mine[chip].astype(F32) + self.theirs[chip].astype(F32)
        for copy in self.copies:
            copy.wait_recv()
        for d in range(1, 8):
            total += self.held[d].astype(F32)
        return total


def fsdp_buffers(shape):
    return [pltpu.VMEM((8,) + shape, BF16)] * 3


def unit_rows(values):
    return lax.rsqrt(jnp.mean(values * values, axis=-1, keepdims=True) + EPSILON)


def hidden_kernel(
    part, h1, dy, gain, wo, gate, up, down,
    gh1_ref, gb_ref, term_ref, go_ref, gate_out, up_out, down_out,
    held, go_own, b0, b1, b2, b3, b4, b5, b6, b7, b8, send, recv, local_sem,
):
    copies, places = Copies(send, recv, local_sem), Places()
    greet(places.scatter_peers())
    hidden = SeqSum(copies, places, part, held)
    sums = [
        FsdpSum(copies, places, gate, b0, b1, b2),
        FsdpSum(copies, places, up, b3, b4, b5),
        FsdpSum(copies, places, down, b6, b7, b8),
    ]
    for item in sums:
        item.send()
    gn2 = hidden.total()
    value = h1[...]
    inverse = unit_rows(value)
    normed = value * inverse
    term_ref[...] = jnp.sum(gn2 * normed, axis=0, keepdims=True)
    weighted = gn2 * gain[...]
    inner = jnp.mean(weighted * normed, axis=-1, keepdims=True)
    gh1 = dy[...].astype(F32) + inverse * (weighted - normed * inner)
    gh1_ref[...] = gh1
    gb_ref[...] = gh1.astype(BF16)

    def columns(j, _):
        begin = pl.multiple_of(j * 256, 256)
        go_own[:, pl.ds(begin, 256)] = dot_nt(gb_ref[...], wo[pl.ds(begin, 256), :]).astype(BF16)
        return 0

    lax.fori_loop(0, 4, columns, 0)
    rows = go_own.shape[0]
    mine = go_ref.at[pl.ds(pl.multiple_of(places.seq * rows, 16), rows), :]
    head = lambda index: go_own.at[:, pl.ds(pl.multiple_of(index * 128, 128), 128)]
    kept = copies.here(head(places.seq), mine)
    heads = []
    for d in (4, 3, 5, 2, 6, 1, 7):
        peer = places.other_seq(d)
        heads.append(copies.remote(head(peer), mine, places.on_seq(peer)))
    for item, out in zip(sums, (gate_out, up_out, down_out)):
        out[...] = item.total().astype(BF16)
    kept.wait()
    for copy in heads:
        copy.wait_recv()
    copies.finish()


def scatter_hidden(part, h1, dy, gain, wo, gate, up, down):
    rows, width = h1.shape
    shapes = [a.shape[2:] for a in (gate, up, down)]
    scratch = [pltpu.VMEM((8, rows, width), BF16), pltpu.VMEM((rows, width), BF16)]
    for shape in shapes:
        scratch += fsdp_buffers(shape)
    return pl.pallas_call(
        hidden_kernel,
        out_shape=[
            jax.ShapeDtypeStruct((rows, width), F32),
            jax.ShapeDtypeStruct((rows, width), BF16),
            jax.ShapeDtypeStruct((1, width), F32),
            jax.ShapeDtypeStruct((8 * rows, 128), BF16),
        ]
        + [jax.ShapeDtypeStruct(shape, BF16) for shape in shapes],
        in_specs=[HBM] + [IN_VMEM] * 4 + [HBM] * 3,
        out_specs=[IN_VMEM] * 3 + [HBM] + [IN_VMEM] * 3,
        scratch_shapes=scratch + semaphores(7 + 7 + 3 * 8, 5),
        compiler_params=params(4),
        name="scatter_hidden",
    )(part, h1, dy, gain, wo, gate, up, down)


def keys_kernel(
    branch, h1, gkv, gout, gate, up, down,
    layer_ref, gkv_out, gout_out, gate_all, up_all, down_all,
    held, b0, b1, b2, b3, b4, b5, send, recv, local_sem,
):
    copies, places = Copies(send, recv, local_sem), Places()
    greet(places.scatter_peers())
    sums = [FsdpSum(copies, places, gkv, b0, b1, b2), FsdpSum(copies, places, gout, b3, b4, b5)]
    hidden = SeqSum(copies, places, branch, held)
    stages = [
        seq_gather(copies, places, gate, gate_all, 0, (0, 32)),
        seq_gather(copies, places, up, up_all, 0, (0, 32)),
        seq_gather(copies, places, down, down_all, 0, (0, 16)),
    ]
    for stage in stages:
        next(stage)
    for item in sums:
        item.send()
    run_stages(stages)
    for item, out in zip(sums, (gkv_out, gout_out)):
        out[...] = item.total().astype(BF16)
    layer_ref[...] = (h1[...] + hidden.total()).astype(BF16)
    copies.finish()


def scatter_keys(branch, h1, gkv, gout, gate, up, down):
    rows, width = h1.shape
    shapes = [a.shape[2:] for a in (gkv, gout)]
    scratch = [pltpu.VMEM((8, rows, width), BF16)]
    for shape in shapes:
        scratch += fsdp_buffers(shape)
    wide = [jax.ShapeDtypeStruct((8 * a.shape[0],) + a.shape[1:], BF16) for a in (gate, up, down)]
    return pl.pallas_call(
        keys_kernel,
        out_shape=[jax.ShapeDtypeStruct((rows, width), BF16)]
        + [jax.ShapeDtypeStruct(shape, BF16) for shape in shapes]
        + wide,
        in_specs=[HBM, IN_VMEM] + [HBM] * 5,
        out_specs=[IN_VMEM] * 3 + [HBM] * 3,
        scratch_shapes=scratch + semaphores(7 + 2 * 8 + 27, 6),
        compiler_params=params(5),
        name="scatter_keys",
    )(branch, h1, gkv, gout, gate, up, down)


def input_kernel(
    part, tokens, gain, gh1, pack, gout,
    grad_ref, pack_all, gout_all,
    held, b0, b1, b2, small, send, recv, local_sem,
):
    copies, places = Copies(send, recv, local_sem), Places()
    greet(places.scatter_peers())
    packs = FsdpSum(copies, places, pack, b0, b1, b2)
    hidden = SeqSum(copies, places, part, held)
    packs.send()
    stages = [seq_gather(copies, places, gout, gout_all, 0, (0, 32))]
    next(stages[0])
    small[...] = packs.total().astype(BF16)
    stages.append(seq_gather(copies, places, small, pack_all, 0, (0, 48)))
    run_stages(stages)
    gn1 = hidden.total()
    value = tokens[...].astype(F32)
    inverse = unit_rows(value)
    normed = value * inverse
    weighted = gn1 * gain[...]
    inner = jnp.mean(weighted * normed, axis=-1, keepdims=True)
    grad_ref[...] = gh1[...] + inverse * (weighted - normed * inner)
    copies.finish()


def scatter_input(part, tokens, gain, gh1, pack, gout):
    rows, width = gh1.shape
    shape = pack.shape[2:]
    return pl.pallas_call(
        input_kernel,
        out_shape=[
            jax.ShapeDtypeStruct((rows, width), F32),
            jax.ShapeDtypeStruct((8 * shape[0], shape[1]), BF16),
            jax.ShapeDtypeStruct((8 * gout.shape[0], width), BF16),
        ],
        in_specs=[HBM] + [IN_VMEM] * 3 + [HBM] * 2,
        out_specs=[IN_VMEM] + [HBM] * 2,
        scratch_shapes=[pltpu.VMEM((8, rows, width), BF16)]
        + fsdp_buffers(shape)
        + [pltpu.VMEM(shape, BF16)]
        + semaphores(7 + 8 + 18, 4),
        compiler_params=params(6),
        name="scatter_input",
    )(part, tokens, gain, gh1, pack, gout)


def local(
    tokens,
    segments,
    cotangent,
    attention_gain,
    query_gain,
    key_gain,
    query_weight,
    key_weight,
    value_weight,
    out_weight,
    feedforward_gain,
    gate_weight,
    up_weight,
    down_weight,
):
    seq_count = lax.axis_size("seq")
    fsdp_count = lax.axis_size("fsdp")
    fsdp = lax.axis_index("fsdp")
    seq = lax.axis_index("seq")
    rows, width = tokens.shape
    block = rows * seq_count
    hidden = gate_weight.shape[1]
    part = hidden // seq_count
    per_head = (H // KVH) * HD
    block_start = fsdp * block
    take = lax.dynamic_slice_in_dim

    ratio = fsdp_count // seq_count
    pairs = [
        (
            f % seq_count * fsdp_count + ratio * s + f // (fsdp_count // ratio),
            s * fsdp_count + f,
        )
        for f in range(fsdp_count)
        for s in range(seq_count)
    ]
    back_pairs = [(b, a) for a, b in pairs]
    both = ("seq", "fsdp")

    gains = jnp.concatenate([attention_gain, feedforward_gain, query_gain, key_gain])
    heads_weight = jnp.concatenate(
        [
            take(query_weight, seq * per_head, per_head, 1),
            take(key_weight, seq * HD, HD, 1),
            take(value_weight, seq * HD, HD, 1),
        ],
        axis=1,
    )
    gains = jnp.pad(gains[None, :], ((0, 15), (0, heads_weight.shape[1] - gains.shape[0])))
    pieces = down_weight.shape[0] // seq_count
    down_piece = lax.ppermute(take(down_weight, seq * pieces, pieces, 0), both, pairs)
    down_piece = jnp.pad(down_piece, ((0, PIECE - pieces), (0, 0)))
    gate_up = jnp.stack(
        [take(gate_weight, seq * part, part, 1), take(up_weight, seq * part, part, 1)]
    )
    x_block, packs, wo = gather(
        "gather_inputs",
        1,
        [(tokens, 0, (0, 64))],
        [(jnp.concatenate([heads_weight, gains]), 0, (0, 48)), (out_weight, 0, (0, 32))],
    )
    packs = packs.reshape(fsdp_count, -1, packs.shape[1])
    heads_weight = packs[:, : width // fsdp_count].reshape(width, -1)
    gains = packs[:, width // fsdp_count].astype(F32)

    shard = width // fsdp_count
    gain_one = gains[:, :shard].reshape(width)
    gain_two = gains[:, shard : 2 * shard].reshape(width)
    qshard = HD // fsdp_count
    gain_q = gains[:, 2 * shard : 2 * shard + qshard].reshape(HD)
    gain_k = gains[:, 2 * shard + qshard : 2 * shard + 2 * qshard].reshape(HD)

    starts = doc_starts(segments)
    ids = take(segments, block_start, block)
    picked = (ids[:, None] == jnp.arange(DOCS, dtype=jnp.int32)[None, :]).astype(jnp.int32)
    first = jnp.sum(picked * starts[None, :], axis=1)
    index = block_start + jnp.arange(block, dtype=jnp.int32)
    freqs = THETA ** (-2.0 * jnp.arange(HD // 2, dtype=F32) / HD)
    angles = (index - first).astype(F32)[:, None] * freqs[None, :]
    cosine, sine = jnp.cos(angles), jnp.sin(angles)
    shift = (HD**0.5 * LOG2E) * jnp.max(jnp.abs(gain_q)) * jnp.max(jnp.abs(gain_k))
    shift = shift.reshape(1)

    tiles = block // TILE
    q_first = block_start + TILE * jnp.arange(tiles, dtype=jnp.int32)
    tile_first = first.reshape(tiles, TILE)
    low = tile_first[:, 0] // KEYS
    high = (q_first + TILE - 1) // KEYS + 1
    inner_low = jnp.minimum((tile_first[:, TILE - 1] + KEYS - 1) // KEYS, high)
    inner_high = jnp.maximum((q_first + 1) // KEYS, inner_low)
    ranges = jnp.stack([low, inner_low, inner_high, high, q_first])

    x = x_block.astype(F32)
    inverse_one = rms_scale(x)
    n1 = (x * inverse_one * gain_one).astype(BF16)
    pre = dot_nn(n1, heads_weight)
    qp = pre[:, :per_head].reshape(block, H // KVH, HD)
    kp = pre[:, per_head : per_head + HD]
    value = pre[:, per_head + HD :].astype(BF16)
    inverse_q = rms_scale(qp)
    inverse_k = rms_scale(kp)
    q = rotate(qp * inverse_q * gain_q, cosine[:, None, :], sine[:, None, :]).astype(BF16)
    k = rotate(kp * inverse_k * gain_k, cosine, sine).astype(BF16)
    q = jnp.transpose(q, (1, 0, 2))
    empty = jnp.zeros_like(q)
    q_pad = jnp.concatenate([q, empty], axis=2)
    dy_block, kv = gather(
        "gather_keys",
        2,
        [(cotangent, 0, (0, 64))],
        [(jnp.concatenate([k, value], axis=1), 0, (0, 512))],
    )

    sums, totals = forward_attention(ranges, shift, q_pad, first[:, None], kv)
    totals = totals[:, :, :1]
    o = sums[:, :, HD:] / totals
    ob = jnp.transpose(o.astype(BF16), (1, 0, 2)).reshape(block, per_head)
    ob_block, gate_up, down_w = gather(
        "gather_attended",
        3,
        [(ob, 1, (0, 512))],
        [(gate_up, 1, (1, 32)), (down_piece, 0, (0, 32))],
    )
    gate_w, up_w = gate_up[0], gate_up[1]
    down_w = down_w.reshape(fsdp_count, PIECE, width)[:, :pieces].reshape(part, width)

    h1 = x + dot_nn(ob_block, wo)
    inverse_two = rms_scale(h1)
    n2 = (h1 * inverse_two * gain_two).astype(BF16)
    gate = dot_nn(n2, gate_w)
    up = dot_nn(n2, up_w)
    sig = jax.nn.sigmoid(gate)
    act = (gate * sig * up).astype(BF16)
    gact = dot_nt(dy_block, down_w)
    ggate = (gact * up * sig * (1.0 + gate * (1.0 - sig))).astype(BF16)
    gup = (gact * gate * sig).astype(BF16)
    gn2_part = (dot_nt(ggate, gate_w) + dot_nt(gup, up_w)).astype(BF16)
    branch = dot_nn(act, down_w).astype(BF16)
    own = lambda array: take(array, seq * rows, rows)
    h1_own = own(h1)
    by_core = lambda array: array.reshape(8, 2, -1, array.shape[-1])
    g_down = dot_tn(act, dy_block).astype(BF16).reshape(fsdp_count, pieces, width)
    g_down = jnp.pad(g_down, ((0, 0), (0, PIECE - pieces), (0, 0)))
    gh1, gb, gain_two_term, go, g_gate, g_up, g_down = scatter_hidden(
        gn2_part.reshape(seq_count, rows, width),
        h1_own,
        cotangent,
        gain_two[None, :],
        wo,
        by_core(dot_tn(n2, ggate).astype(BF16)),
        by_core(dot_tn(n2, gup).astype(BF16)),
        by_core(g_down.reshape(-1, width)),
    )
    g_down = lax.ppermute(g_down, both, back_pairs)
    g_out = dot_tn(own(ob_block), gb).astype(BF16)
    go = jnp.transpose(go.reshape(block, H // KVH, HD), (1, 0, 2)).astype(F32)
    ga = (go / totals).astype(BF16)
    ga_pad = jnp.concatenate([empty, ga], axis=2)
    delta = jnp.sum(go * o, axis=2) / totals[:, :, 0]

    tiled = lambda a: jnp.transpose(a.reshape(2, tiles, TILE), (1, 0, 2)).reshape(tiles, 1, 2 * TILE)
    gq, gkv = backward_attention(
        ranges,
        shift,
        q_pad,
        ga_pad,
        tiled(delta),
        tiled(jnp.stack([first, first])),
        kv,
    )
    layer_out, gkv, g_out, g_gate, g_up, g_down = scatter_keys(
        branch.reshape(seq_count, rows, width),
        h1_own,
        by_core(gkv),
        by_core(g_out),
        g_gate,
        g_up,
        g_down,
    )
    gq = jnp.transpose((gq[:, :, :HD] * HD**-0.5).astype(BF16), (1, 0, 2)).astype(F32)
    gk = gkv[:, :HD].astype(F32)
    gv = gkv[:, HD:]
    gain_q_term, gqp = norm_back(
        qp, inverse_q, gain_q, rotate(gq, cosine[:, None, :], -sine[:, None, :])
    )
    gain_k_term, gkp = norm_back(kp, inverse_k, gain_k, rotate(gk, cosine, -sine))
    gpre = jnp.concatenate(
        [gqp.reshape(block, per_head).astype(BF16), gkp.astype(BF16), gv], axis=1
    )
    gn1_partial = dot_nt(gpre, heads_weight)
    gain_one_term = jnp.sum(gn1_partial * (x * inverse_one), axis=0)
    g_heads = dot_tn(n1, gpre).astype(BF16).reshape(fsdp_count, shard, -1)
    terms = jnp.concatenate(
        [
            gain_one_term.reshape(fsdp_count, shard),
            gain_two_term.reshape(fsdp_count, shard),
            gain_q_term.reshape(fsdp_count, qshard),
            gain_k_term.reshape(fsdp_count, qshard),
        ],
        axis=1,
    ).astype(BF16)
    terms = jnp.pad(terms[:, None, :], ((0, 0), (0, 15), (0, g_heads.shape[2] - terms.shape[1])))
    pack = jnp.concatenate([g_heads, terms], axis=1)
    input_grad, packs, g_out = scatter_input(
        gn1_partial.astype(BF16).reshape(seq_count, rows, width),
        tokens,
        gain_one[None, :],
        gh1,
        pack.reshape((8, 2) + pack.shape[1:]),
        g_out,
    )
    packs = packs.reshape((seq_count,) + pack.shape[1:])
    g_heads = packs[:, :shard]
    terms = jnp.sum(packs[:, shard].astype(F32), axis=0)
    g_out = jnp.sum(g_out.reshape(seq_count, shard, width).astype(F32), axis=0)
    g_down = g_down.reshape(seq_count, PIECE, width)[:, :pieces].reshape(-1, width)
    columns = lambda a: jnp.transpose(a.reshape(seq_count, shard, part), (1, 0, 2)).reshape(shard, hidden)

    g_query = jnp.transpose(g_heads[:, :, :per_head], (1, 0, 2)).reshape(shard, H * HD)
    g_key = jnp.transpose(g_heads[:, :, per_head : per_head + HD], (1, 0, 2)).reshape(shard, KVH * HD)
    g_value = jnp.transpose(g_heads[:, :, per_head + HD :], (1, 0, 2)).reshape(shard, KVH * HD)

    return (
        layer_out,
        input_grad,
        terms[:shard],
        terms[2 * shard : 2 * shard + qshard],
        terms[2 * shard + qshard : 2 * shard + 2 * qshard],
        g_query.astype(F32),
        g_key.astype(F32),
        g_value.astype(F32),
        g_out,
        terms[shard : 2 * shard],
        columns(g_gate).astype(F32),
        columns(g_up).astype(F32),
        g_down.astype(F32),
    )


def solution(mesh):
    rows = P(("fsdp", "seq"), None)
    matrix = P("fsdp", None)
    vector = P("fsdp")
    in_specs = (rows, P(), rows) + (vector,) * 3 + (matrix,) * 4 + (vector,) + (matrix,) * 3
    out_specs = (rows, rows) + (vector,) * 3 + (matrix,) * 4 + (vector,) + (matrix,) * 3
    return jax.shard_map(local, mesh=mesh, in_specs=in_specs, out_specs=out_specs, check_vma=False)
```

```python
import functools
import math

import jax
import jax.numpy as jnp
from jax import lax
from jax.experimental import pallas as pl
from jax.experimental.pallas import tpu as pltpu
from jax.sharding import PartitionSpec as P

H = 16
KVH = 8
HD = 64
DOCS = 4
EPSILON = 1e-06
THETA = 1000000.0
LOG2E = math.log2(math.e)
F32 = jnp.float32
BF16 = jnp.bfloat16
STRIP = 128
FEED = 256
KEYS = 1024
VMEM = 56 * 1024 * 1024
PIECE = 48


def rms_scale(values):
    return lax.rsqrt(jnp.mean(values * values, axis=-1, keepdims=True) + EPSILON)


def norm_back(values, inverse, gain, grad):
    normalized = values * inverse
    gain_term = jnp.sum(grad * normalized, axis=tuple(range(grad.ndim - 1)))
    weighted = grad * gain
    inner = jnp.mean(weighted * normalized, axis=-1, keepdims=True)
    return (gain_term, inverse * (weighted - normalized * inner))


def doc_starts(segments):
    labels = jnp.arange(DOCS, dtype=jnp.int32)
    member = (segments[None, :] == labels[:, None]).astype(jnp.int32)
    lengths = jnp.sum(member, axis=1)
    return jnp.cumsum(lengths) - lengths


def rotate(values, cosine, sine):
    half = values.shape[-1] // 2
    first, second = values[..., :half], values[..., half:]
    return jnp.concatenate(
        [first * cosine - second * sine, second * cosine + first * sine], axis=-1
    )


def dot_nt(a, b):
    return lax.dot_general(a, b, (((1,), (1,)), ((), ())), preferred_element_type=F32)


def dot_tn(a, b):
    return lax.dot_general(a, b, (((0,), (0,)), ((), ())), preferred_element_type=F32)


def dot_nn(a, b):
    return jnp.dot(a, b, preferred_element_type=F32)


def key_loops(ranges_ref, tile, step):
    low, inner_low, inner_high, high = [ranges_ref[i, tile] for i in range(4)]

    def masked(block, _):
        step(block, True)
        return 0

    def plain(block, _):
        step(block, False)
        return 0

    lax.fori_loop(low, inner_low, masked, 0)
    lax.fori_loop(inner_low, inner_high, plain, 0)
    lax.fori_loop(inner_high, high, masked, 0)


def lanes_low(shape):
    return lax.broadcasted_iota(jnp.int32, shape, 1) < HD


def two_heads(packed, low):
    other = pltpu.roll(packed, HD, 1)
    heads = (packed, other) if low else (other, packed)
    keep = lanes_low(packed.shape) if low else ~lanes_low(packed.shape)
    return jnp.concatenate([jnp.where(keep, head, 0.0) for head in heads], axis=0)


def one_row(heads, low):
    rows = heads.shape[0] // 2
    first, second = heads[:rows], heads[rows:]
    if low:
        second = pltpu.roll(second, HD, 1)
    else:
        first = pltpu.roll(first, HD, 1)
    return jnp.where(lanes_low(first.shape), first, second)


def forward_kernel(
    ranges_ref, shift_ref, query_ref, first_ref, kv_ref, ob_ref, o_ref, totals_ref, total
):
    tile = pl.program_id(0)
    rows = query_ref.shape[0]
    query = two_heads(query_ref[...].astype(F32) * HD**-0.5, True).astype(BF16)
    first = jnp.concatenate([first_ref[...]] * 2, axis=0)
    index = ranges_ref[4, tile] + lax.broadcasted_iota(jnp.int32, (rows, 1), 0)
    index = jnp.concatenate([index, index], axis=0)
    shift = shift_ref[0]
    ones = jnp.ones((KEYS, 2 * HD), BF16)
    total[...] = jnp.zeros_like(total)

    def step(block, masked):
        start = pl.multiple_of(block * KEYS, KEYS)
        kv = kv_ref[pl.ds(start, KEYS), :]
        exps = jnp.exp2(dot_nt(query, kv) * LOG2E - shift)
        if masked:
            keys = start + lax.broadcasted_iota(jnp.int32, (2 * rows, KEYS), 1)
            exps = jnp.where((keys >= first) & (keys <= index), exps, 0.0)
        total[...] += dot_nn(exps.astype(BF16), jnp.concatenate([kv, ones], axis=1))

    key_loops(ranges_ref, tile, step)
    totals = total[:, 2 * HD :]
    o = total[:, : 2 * HD] / totals
    o_ref[0] = o
    totals_ref[0] = totals
    ob_ref[...] = one_row(o, False).astype(BF16)


def forward_attention(ranges, shift, query, first, kv):
    tiles = query.shape[0] // STRIP
    whole = lambda t, *_: (0, 0)
    part = lambda t, *_: (t, 0)
    wide = lambda t, *_: (t, 0, 0)
    return pl.pallas_call(
        forward_kernel,
        grid_spec=pltpu.PrefetchScalarGridSpec(
            num_scalar_prefetch=2,
            grid=(tiles,),
            in_specs=[
                pl.BlockSpec((STRIP, 2 * HD), part),
                pl.BlockSpec((STRIP, 1), part),
                pl.BlockSpec(kv.shape, whole),
            ],
            out_specs=[
                pl.BlockSpec((STRIP, 2 * HD), part),
                pl.BlockSpec((1, 2 * STRIP, 2 * HD), wide),
                pl.BlockSpec((1, 2 * STRIP, 2 * HD), wide),
            ],
            scratch_shapes=[pltpu.VMEM((2 * STRIP, 4 * HD), F32)],
        ),
        out_shape=[
            jax.ShapeDtypeStruct(query.shape, BF16),
            jax.ShapeDtypeStruct((tiles, 2 * STRIP, 2 * HD), F32),
            jax.ShapeDtypeStruct((tiles, 2 * STRIP, 2 * HD), F32),
        ],
        compiler_params=pltpu.CompilerParams(vmem_limit_bytes=VMEM),
        cost_estimate=pl.CostEstimate(
            flops=8 * 10**9, bytes_accessed=8 * 10**6, transcendentals=16 * 10**6
        ),
        name="attention_forward",
    )(ranges, shift, query, first, kv)


def backward_kernel(
    ranges_ref, shift_ref, query_ref, grad_ref, o_ref, totals_ref, first_ref, kv_ref,
    gq_ref, gkv_ref, total, gq,
):
    tile = pl.program_id(0)
    rows = query_ref.shape[0]
    query = two_heads(query_ref[...].astype(F32) * HD**-0.5, True).astype(BF16)
    go = two_heads(grad_ref[...].astype(F32), False)
    totals = totals_ref[0]
    grad = (go / totals).astype(BF16)
    delta = jnp.sum(go * o_ref[0], axis=1, keepdims=True) / totals
    delta = jnp.transpose(delta)[:1]
    both = jnp.concatenate([query, grad], axis=0)
    first = jnp.concatenate([first_ref[0]] * 2, axis=1)
    index = ranges_ref[4, tile] + lax.broadcasted_iota(jnp.int32, (1, rows), 1)
    index = jnp.concatenate([index, index], axis=1)
    shift = shift_ref[0]

    @pl.when(tile == 0)
    def _():
        total[...] = jnp.zeros_like(total)

    gq[...] = jnp.zeros_like(gq)

    def step(block, masked):
        start = pl.multiple_of(block * KEYS, KEYS)
        kv = kv_ref[pl.ds(start, KEYS), :]
        exps = jnp.exp2(dot_nt(kv, query) * LOG2E - shift)
        if masked:
            keys = start + lax.broadcasted_iota(jnp.int32, (KEYS, 2 * rows), 0)
            exps = jnp.where((keys >= first) & (keys <= index), exps, 0.0)
        scores = (exps * (dot_nt(kv, grad) - delta)).astype(BF16)
        gq[...] += dot_tn(scores, kv)
        total[pl.ds(start, KEYS), :] += dot_nn(
            jnp.concatenate([scores, exps.astype(BF16)], axis=1), both
        )

    key_loops(ranges_ref, tile, step)
    gq_ref[...] = (one_row(gq[...], True) * HD**-0.5).astype(BF16)

    @pl.when(tile == pl.num_programs(0) - 1)
    def _():
        gkv_ref[...] = total[...].astype(BF16)


def backward_attention(ranges, shift, query, grad, o, totals, first, kv):
    tiles = query.shape[0] // STRIP
    whole = lambda t, *_: (0, 0)
    part = lambda t, *_: (t, 0)
    wide = lambda t, *_: (t, 0, 0)
    return pl.pallas_call(
        backward_kernel,
        grid_spec=pltpu.PrefetchScalarGridSpec(
            num_scalar_prefetch=2,
            grid=(tiles,),
            in_specs=[
                pl.BlockSpec((STRIP, 2 * HD), part),
                pl.BlockSpec((STRIP, 2 * HD), part),
                pl.BlockSpec((1, 2 * STRIP, 2 * HD), wide),
                pl.BlockSpec((1, 2 * STRIP, 2 * HD), wide),
                pl.BlockSpec((1, 1, STRIP), wide),
                pl.BlockSpec(kv.shape, whole),
            ],
            out_specs=[
                pl.BlockSpec((STRIP, 2 * HD), part),
                pl.BlockSpec(kv.shape, whole),
            ],
            scratch_shapes=[pltpu.VMEM(kv.shape, F32), pltpu.VMEM((2 * STRIP, 2 * HD), F32)],
        ),
        out_shape=[
            jax.ShapeDtypeStruct(query.shape, BF16),
            jax.ShapeDtypeStruct(kv.shape, BF16),
        ],
        compiler_params=pltpu.CompilerParams(vmem_limit_bytes=VMEM),
        cost_estimate=pl.CostEstimate(
            flops=20 * 10**9, bytes_accessed=16 * 10**6, transcendentals=16 * 10**6
        ),
        name="attention_backward",
    )(ranges, shift, query, grad, o, totals, first, kv)


def feed_kernel(
    n2_ref, dy_ref, weights_ref, down_ref,
    gn2_ref, branch_ref, gate_out, up_out, down_out,
    act_ref, ggate_ref, gup_ref,
):
    count, width = n2_ref.shape

    def tokens(t, _):
        at = pl.ds(pl.multiple_of(t * FEED, FEED), FEED)
        n2 = n2_ref[at, :]
        gate = dot_nn(n2, weights_ref[0])
        up = dot_nn(n2, weights_ref[1])
        gact = dot_nt(dy_ref[at, :], down_ref[...])
        sig = jax.nn.sigmoid(gate)
        silu = gate * sig
        act = (silu * up).astype(BF16)
        ggate = (gact * up * sig * (1.0 + gate * (1.0 - sig))).astype(BF16)
        gup = (gact * silu).astype(BF16)
        act_ref[at, :] = act
        ggate_ref[at, :] = ggate
        gup_ref[at, :] = gup
        gn2_ref[at, :] = (dot_nt(ggate, weights_ref[0]) + dot_nt(gup, weights_ref[1])).astype(BF16)
        branch_ref[at, :] = dot_nn(act, down_ref[...]).astype(BF16)
        return 0

    lax.fori_loop(0, count // FEED, tokens, 0)

    def columns(c, _):
        at = pl.ds(pl.multiple_of(c * FEED, FEED), FEED)
        n2 = n2_ref[:, at]
        gate_out[at, :] = dot_tn(n2, ggate_ref[...]).astype(BF16)
        up_out[at, :] = dot_tn(n2, gup_ref[...]).astype(BF16)
        down_out[:, at] = dot_tn(act_ref[...], dy_ref[:, at]).astype(BF16)
        return 0

    lax.fori_loop(0, width // FEED, columns, 0)


def feed_forward(n2, dy, weights, down):
    part = down.shape[0]
    count, width = n2.shape
    return pl.pallas_call(
        feed_kernel,
        out_shape=[
            jax.ShapeDtypeStruct(shape, BF16)
            for shape in [(count, width)] * 2 + [(width, part)] * 2 + [(part, width)]
        ],
        in_specs=[IN_VMEM] * 4,
        out_specs=[IN_VMEM] * 5,
        scratch_shapes=[pltpu.VMEM((count, part), BF16)] * 3,
        compiler_params=pltpu.CompilerParams(vmem_limit_bytes=VMEM),
        cost_estimate=pl.CostEstimate(
            flops=11 * 10**9, bytes_accessed=16 * 10**6, transcendentals=10**6
        ),
        name="feed_forward",
    )(n2, dy, weights, down)


MESH = pl.DeviceIdType.MESH
HBM = pl.BlockSpec(memory_space=pl.ANY)
IN_VMEM = pl.BlockSpec(memory_space=pltpu.VMEM)
RING = 8


def pair_of(value):
    return value + 1 - 2 * lax.rem(value, 2)


def ring_step(index, steps):
    return lax.div(index, RING) * RING + lax.rem(lax.rem(index, RING) + 2 * steps, RING)


class Copies:
    def __init__(self, send, recv, local):
        self.send, self.recv, self.local = send, recv, local
        self.started, self.locals = [], []

    def remote(self, src, dst, peer, recv=None):
        i = len(self.started)
        copy = pltpu.make_async_remote_copy(
            src_ref=src,
            dst_ref=dst,
            send_sem=self.send.at[i],
            recv_sem=self.recv.at[i] if recv is None else recv,
            device_id=peer,
            device_id_type=MESH,
        )
        copy.start()
        self.started.append(copy)
        return copy

    def here(self, src, dst):
        copy = pltpu.make_async_copy(src, dst, self.local.at[len(self.locals)])
        copy.start()
        self.locals.append(copy)
        return copy

    def finish(self):
        for copy in self.started:
            copy.wait_send()


def greet(peers):
    barrier = pltpu.get_barrier_semaphore()
    for peer in peers:
        pl.semaphore_signal(barrier, inc=1, device_id=peer, device_id_type=MESH)
    pl.semaphore_wait(barrier, len(peers))


def slot(ref, axis, size, index, split=None, half=0):
    start = index * size
    where = [pl.ds(0, n) for n in ref.shape]
    where[axis] = pl.ds(pl.multiple_of(start, 16), size)
    if split is not None:
        along, cut = split
        whole = size if along == axis else ref.shape[along]
        base = start if along == axis else 0
        begin, count = (0, cut) if half == 0 else (cut, whole - cut)
        offset = base + begin
        where[along] = pl.ds(pl.multiple_of(offset, 16) if along == axis else offset, count)
    return ref.at[tuple(where)]


def gather_stages(copies, src, out, axis, size, split, me, pair, device, sibling):
    plus, minus = ring_step(me, 1), ring_step(me, 3)
    at = functools.partial(slot, out, axis, size)
    halves = lambda index, half: at(index, split, half)
    to_sibling = []

    def pass_on(index):
        if sibling is not None:
            to_sibling.append(copies.remote(at(index), at(index), device(sibling)))

    kept = copies.here(src, at(me))
    first = copies.remote(src, at(me), device(pair))
    up = copies.remote(src, at(me), device(plus))
    down = copies.remote(src, at(me), device(minus))
    if sibling is not None:
        to_sibling.append(copies.remote(src, at(me), device(sibling)))
    yield
    up.wait_recv()
    far = [copies.remote(halves(minus, 0), halves(minus, 0), device(plus))]
    pass_on(minus)
    down.wait_recv()
    far.append(copies.remote(halves(plus, 1), halves(plus, 1), device(minus)))
    pass_on(plus)
    yield
    first.wait_recv()
    up = copies.remote(at(pair), at(pair), device(plus))
    down = copies.remote(at(pair), at(pair), device(minus))
    pass_on(pair)
    yield
    shift = pair - me
    up.wait_recv()
    last = [copies.remote(halves(minus + shift, 0), halves(minus + shift, 0), device(plus))]
    pass_on(minus + shift)
    down.wait_recv()
    last.append(copies.remote(halves(plus + shift, 1), halves(plus + shift, 1), device(minus)))
    pass_on(plus + shift)
    yield
    opposite = ring_step(me, 2)
    for copy in far:
        copy.wait_recv()
    pass_on(opposite)
    yield
    for copy in last:
        copy.wait_recv()
    pass_on(opposite + shift)
    yield
    for copy in to_sibling:
        copy.wait_recv()
    kept.wait()


def run_stages(stages):
    live = list(stages)
    while live:
        live = [stage for stage in live if next(stage, stage) is not stage]


class Swap:
    def __init__(self, copies, recv, sem, tag, stays, sends):
        self.copies, self.recv, self.tag, self.stays = copies, recv, tag, stays
        (src, dst, peer), rest = sends[0], sends[1:]
        self.own = pltpu.make_async_remote_copy(
            src_ref=src,
            dst_ref=dst,
            send_sem=sem.at[0],
            recv_sem=recv.at[tag],
            device_id=peer,
            device_id_type=MESH,
        )
        self.kept = pltpu.make_async_copy(src, dst, sem.at[1])

        @pl.when(stays)
        def _():
            self.kept.start()

        @pl.when(jnp.logical_not(stays))
        def _():
            self.own.start()

        self.sample = (src, dst, peer, sem)
        for src, dst, peer in rest:
            copies.remote(src, dst, peer, recv.at[tag])

    def wait(self, landing):
        src, _, peer, sem = self.sample
        for step in range(1, 8):
            sender = lax.rem(self.tag + step, 8)
            pltpu.make_async_remote_copy(
                src_ref=src,
                dst_ref=landing(sender),
                send_sem=sem.at[0],
                recv_sem=self.recv.at[sender],
                device_id=peer,
                device_id_type=MESH,
            ).wait_recv()

        @pl.when(self.stays)
        def _():
            self.kept.wait()

        @pl.when(jnp.logical_not(self.stays))
        def _():
            self.own.wait()


def greet_for_swap(places, peers, senders):
    barrier = pltpu.get_barrier_semaphore()
    peers = peers + senders[1:]
    for peer in peers:
        pl.semaphore_signal(barrier, inc=1, device_id=peer, device_id_type=MESH)

    @pl.when(places.stays)
    def _():
        pl.semaphore_wait(barrier, len(peers))

    @pl.when(jnp.logical_not(places.stays))
    def _():
        pl.semaphore_signal(barrier, inc=1, device_id=senders[0], device_id_type=MESH)
        pl.semaphore_wait(barrier, len(peers) + 1)


def strips_at(ref, index):
    return ref.at[pl.ds(pl.multiple_of(index * STRIP, STRIP), STRIP), :]


def heads_at(ref, index):
    return ref.at[:, pl.ds(pl.multiple_of(index * 2 * HD, 2 * HD), 2 * HD)]


class Places:
    def __init__(self):
        self.seq, self.fsdp = lax.axis_index("seq"), lax.axis_index("fsdp")
        self.core = lax.rem(self.fsdp, 2)
        self.chip = lax.div(self.fsdp, 2)
        self.row = lax.div(self.chip, 4)
        self.col = lax.rem(self.chip, 4)
        self.sibling = pair_of(self.fsdp)
        self.across = lax.rem(self.fsdp + 8, 16)
        self.stays = self.chip == self.seq

    def on_seq(self, index):
        return (index, self.fsdp)

    def on_fsdp(self, index):
        return (self.seq, index)

    def other_seq(self, step):
        return lax.rem(self.seq + step, 8)

    def other_chip(self, step):
        return lax.rem(self.row + step // 4, 2) * 4 + lax.rem(self.col + step % 4, 4)

    def gather_peers(self):
        seq = [pair_of(self.seq), ring_step(self.seq, 1), ring_step(self.seq, 3)]
        fsdp = [self.across, ring_step(self.fsdp, 1), ring_step(self.fsdp, 3), self.sibling]
        return [self.on_seq(i) for i in seq] + [self.on_fsdp(i) for i in fsdp]

    def strip_peers(self):
        return [self.on_fsdp(self.other_chip(d) * 2 + self.core) for d in range(1, 8)]

    def owners(self):
        strips = [lax.rem(self.chip + d, 8) for d in range(8)]
        return strips, [(self.chip, strip * 2 + self.core) for strip in strips]

    def heads(self):
        heads = [lax.rem(self.seq + d, 8) for d in range(8)]
        return heads, [(head, self.seq * 2 + self.core) for head in heads]


def params(name_id):
    return pltpu.CompilerParams(
        collective_id=name_id, has_side_effects=True, vmem_limit_bytes=VMEM
    )


def semaphores(remote, local):
    return [
        pltpu.SemaphoreType.DMA((remote,)),
        pltpu.SemaphoreType.DMA((remote,)),
        pltpu.SemaphoreType.DMA((local,)),
    ]


def seq_gather(copies, places, src, out, axis, split):
    size = src.shape[axis]
    return gather_stages(
        copies, src, out, axis, size, split, places.seq, pair_of(places.seq), places.on_seq, None
    )


def fsdp_gather(copies, places, src, out, axis, split):
    size = src.shape[axis]
    return gather_stages(
        copies, src, out, axis, size, split, places.fsdp, places.across, places.on_fsdp, places.sibling
    )


class Strips:
    def __init__(self, copies, places, src, out):
        self.kept = copies.here(strips_at(src, places.chip), strips_at(out, places.chip))
        self.copies = []
        for d in range(1, 8):
            chip = places.other_chip(d)
            peer = places.on_fsdp(chip * 2 + places.core)
            self.copies.append(copies.remote(strips_at(src, chip), strips_at(out, places.chip), peer))

    def wait(self):
        for copy in self.copies:
            copy.wait_recv()
        self.kept.wait()


def gather(name, name_id, seq_items, fsdp_items, strips=()):
    items = seq_items + fsdp_items
    count = len(items)
    every = count + len(strips)

    def kernel(*refs):
        srcs, outs = refs[:every], refs[every : 2 * every]
        copies, places = Copies(*refs[2 * every :]), Places()
        greet(places.gather_peers() + (places.strip_peers() if strips else []))
        moved = [Strips(copies, places, srcs[i], outs[i]) for i in range(count, every)]
        stages = []
        for i, (_, axis, split) in enumerate(items):
            make = seq_gather if i < len(seq_items) else fsdp_gather
            stages.append(make(copies, places, srcs[i], outs[i], axis, split))
        run_stages(stages)
        for item in moved:
            item.wait()
        copies.finish()

    shapes = []
    for i, (array, axis, _) in enumerate(items):
        shape = list(array.shape)
        shape[axis] *= 8 if i < len(seq_items) else 16
        shapes.append(jax.ShapeDtypeStruct(tuple(shape), array.dtype))
    shapes += [jax.ShapeDtypeStruct(array.shape, array.dtype) for array in strips]
    remote = 9 * len(seq_items) + 17 * len(fsdp_items) + 7 * len(strips)
    return pl.pallas_call(
        kernel,
        out_shape=shapes,
        in_specs=[HBM] * every,
        out_specs=[HBM] * every,
        scratch_shapes=semaphores(remote, every),
        compiler_params=params(name_id),
        name=name,
    )(*[item[0] for item in items], *strips)


def attended_kernel(
    ob, wo, tokens, gain, gate_up, down,
    own_ref, h1_ref, n2_all, gate_up_all, down_all,
    own, n2, tags, ends, send, recv, local_sem,
):
    copies, places = Copies(send, recv, local_sem), Places()
    strips, owners = places.owners()
    _, senders = places.heads()
    greet_for_swap(places, places.gather_peers(), senders)
    landing = heads_at(own, places.seq)
    sends = [(strips_at(ob, strip), landing, peer) for strip, peer in zip(strips, owners)]
    swap = Swap(copies, tags, ends, places.seq, places.stays, sends)
    stages = [
        fsdp_gather(copies, places, gate_up, gate_up_all, 1, (1, 32)),
        fsdp_gather(copies, places, down, down_all, 0, (0, 32)),
    ]
    for stage in stages:
        next(stage)
    swap.wait(lambda sender: heads_at(own, sender))
    own_ref[...] = own[...]

    def columns(j, _):
        at = pl.ds(pl.multiple_of(j * 256, 256), 256)
        h1_ref[:, at] = tokens[:, at].astype(F32) + dot_nn(own[...], wo[:, at])
        return 0

    lax.fori_loop(0, 4, columns, 0)
    value = h1_ref[...]
    n2[...] = (value * unit_rows(value) * gain[...]).astype(BF16)
    stages.insert(0, seq_gather(copies, places, n2, n2_all, 0, (0, 64)))
    run_stages(stages)
    copies.finish()


def gather_attended(ob, wo, tokens, gain, gate_up, down):
    rows, width = tokens.shape
    return pl.pallas_call(
        attended_kernel,
        out_shape=[
            jax.ShapeDtypeStruct((rows, width), BF16),
            jax.ShapeDtypeStruct((rows, width), F32),
            jax.ShapeDtypeStruct((8 * rows, width), BF16),
            jax.ShapeDtypeStruct((2, 16 * gate_up.shape[1], gate_up.shape[2]), BF16),
            jax.ShapeDtypeStruct((16 * down.shape[0], width), BF16),
        ],
        in_specs=[HBM] + [IN_VMEM] * 3 + [HBM] * 2,
        out_specs=[IN_VMEM] * 2 + [HBM] * 3,
        scratch_shapes=[
            pltpu.VMEM((rows, width), BF16),
            pltpu.VMEM((rows, width), BF16),
            pltpu.SemaphoreType.DMA((8,)),
            pltpu.SemaphoreType.DMA((2,)),
        ]
        + semaphores(7 + 9 + 2 * 17, 3),
        compiler_params=params(3),
        name="gather_attended",
    )(ob, wo, tokens, gain, gate_up, down)


class RingSum:
    def __init__(self, copies, near, mine, held, cut, index, device):
        self.remote, self.mine, self.device = copies.remote, mine, device
        self.half, self.ring, self.other = held
        self.cut, self.index = cut, index
        self.plus, self.minus, self.pair = near

    def parts(self):
        rows = self.mine.shape[1]
        return pl.ds(0, self.cut), pl.ds(self.cut, rows - self.cut)

    def send(self):
        low, high = self.parts()
        self.first, self.second = [], []
        for flip in (1, 0):
            far, up, down = [self.mine.at[self.index(flip, step)] for step in (2, 1, 3)]
            self.first.append(
                (
                    self.remote(far.at[low], self.half.at[flip, low], self.plus),
                    self.remote(far.at[high], self.half.at[flip, high], self.minus),
                )
            )
            self.second.append(
                [
                    self.remote(up.at[high], self.ring.at[flip, 0, high], self.plus),
                    self.remote(down.at[low], self.ring.at[flip, 1, low], self.minus),
                ]
            )

    def relay(self):
        low, high = self.parts()
        for i, flip in enumerate((1, 0)):
            for copy, step, part, way, peer in (
                (self.first[i][0], 1, low, 0, self.plus),
                (self.first[i][1], 3, high, 1, self.minus),
            ):
                copy.wait_recv()
                at = self.index(flip, step)
                self.mine[at, part] = (
                    self.mine[at, part].astype(F32) + self.half[flip, part].astype(F32)
                ).astype(BF16)
                self.second[i].append(
                    self.remote(self.mine.at[at, part], self.ring.at[flip, way, part], peer)
                )

    def gathered(self, i, flip):
        for copy in self.second[i]:
            copy.wait_recv()
        return (
            self.mine[self.index(flip, 0)].astype(F32)
            + self.ring[flip, 0].astype(F32)
            + self.ring[flip, 1].astype(F32)
        )

    def cross(self):
        self.other[0] = self.gathered(0, 1).astype(BF16)
        self.last = self.remote(self.other.at[0], self.other.at[1], self.pair)

    def total(self):
        total = self.gathered(1, 0)
        self.last.wait_recv()
        return total + self.other[1].astype(F32)


def ring_buffers(shape):
    return [
        pltpu.VMEM((2,) + shape, BF16),
        pltpu.VMEM((2, 2) + shape, BF16),
        pltpu.VMEM((2,) + shape, BF16),
    ]


RING_COPIES = 13


class SeqSum(RingSum):
    def __init__(self, copies, places, part, buffers, cut):
        mine, held = buffers[0], buffers[1:]
        seq = places.seq

        def index(flip, step):
            base = ring_step(seq, step)
            return pair_of(base) if flip else base

        near = [places.on_seq(i) for i in (ring_step(seq, 1), ring_step(seq, 3), pair_of(seq))]
        super().__init__(copies, near, mine, held, cut, index, places.on_seq)
        self.kept = copies.here(part, mine)

    def ready(self):
        self.kept.wait()


class FsdpSum(RingSum):
    def __init__(self, copies, places, part, buffers, cut):
        mine, self.theirs, held = buffers[0], buffers[1], buffers[2:]
        fsdp = places.fsdp

        def index(flip, step):
            return lax.rem(places.row + flip, 2) * 4 + lax.rem(places.col + step, 4)

        near = [places.on_fsdp(i) for i in (ring_step(fsdp, 1), ring_step(fsdp, 3), places.across)]
        super().__init__(copies, near, mine, held, cut, index, places.on_fsdp)
        self.order = [index(flip, step) for flip in (1, 0) for step in (2, 1, 3, 0)]
        self.others = [
            copies.remote(
                part.at[at, 1 - places.core], self.theirs.at[at], places.on_fsdp(places.sibling)
            )
            for at in self.order
        ]
        self.kept = copies.here(part.at[:, places.core], mine)

    def ready(self):
        self.kept.wait()
        for at, copy in zip(self.order, self.others):
            copy.wait_recv()
            self.mine[at] = (self.mine[at].astype(F32) + self.theirs[at].astype(F32)).astype(BF16)


def seq_buffers(shape):
    return [pltpu.VMEM((8,) + shape, BF16)] + ring_buffers(shape)


def fsdp_buffers(shape):
    return [pltpu.VMEM((8,) + shape, BF16)] * 2 + ring_buffers(shape)


SEQ_COPIES = RING_COPIES
FSDP_COPIES = RING_COPIES + 8


def unit_rows(values):
    return lax.rsqrt(jnp.mean(values * values, axis=-1, keepdims=True) + EPSILON)


def hidden_kernel(
    part, h1, dy, gain, wo, gate, up, down,
    gh1_ref, gb_ref, term_ref, go_ref, gate_out, up_out, down_out,
    go_own, tags, ends, *scratch,
):
    copies, places = Copies(*scratch[19:]), Places()
    heads, workers = places.heads()
    _, senders = places.owners()
    greet_for_swap(places, places.gather_peers(), senders)
    hidden = SeqSum(copies, places, part, scratch[:4], 64)
    sums = [
        FsdpSum(copies, places, gate, scratch[4:9], 32),
        FsdpSum(copies, places, up, scratch[9:14], 32),
        FsdpSum(copies, places, down, scratch[14:19], 32),
    ]
    for item in [hidden] + sums:
        item.ready()
        item.send()
    for item in [hidden] + sums:
        item.relay()
    for item in [hidden] + sums:
        item.cross()
    gn2 = hidden.total()
    value = h1[...]
    inverse = unit_rows(value)
    normed = value * inverse
    term_ref[...] = jnp.sum(gn2 * normed, axis=0, keepdims=True)
    weighted = gn2 * gain[...]
    inner = jnp.mean(weighted * normed, axis=-1, keepdims=True)
    gh1 = dy[...].astype(F32) + inverse * (weighted - normed * inner)
    gh1_ref[...] = gh1
    gb_ref[...] = gh1.astype(BF16)

    def columns(j, _):
        begin = pl.multiple_of(j * 256, 256)
        go_own[:, pl.ds(begin, 256)] = dot_nt(gb_ref[...], wo[pl.ds(begin, 256), :]).astype(BF16)
        return 0

    lax.fori_loop(0, 4, columns, 0)
    landing = strips_at(go_ref, places.chip)
    sends = [(heads_at(go_own, head), landing, peer) for head, peer in zip(heads, workers)]
    swap = Swap(copies, tags, ends, places.chip, places.stays, sends)
    for item, out in zip(sums, (gate_out, up_out, down_out)):
        out[...] = item.total().astype(BF16)
    swap.wait(lambda sender: strips_at(go_ref, sender))
    copies.finish()


def scatter_hidden(part, h1, dy, gain, wo, gate, up, down):
    rows, width = h1.shape
    shapes = [a.shape[2:] for a in (gate, up, down)]
    scratch = [
        pltpu.VMEM((rows, width), BF16),
        pltpu.SemaphoreType.DMA((8,)),
        pltpu.SemaphoreType.DMA((2,)),
    ] + seq_buffers((rows, width))
    for shape in shapes:
        scratch += fsdp_buffers(shape)
    return pl.pallas_call(
        hidden_kernel,
        out_shape=[
            jax.ShapeDtypeStruct((rows, width), F32),
            jax.ShapeDtypeStruct((rows, width), BF16),
            jax.ShapeDtypeStruct((1, width), F32),
            jax.ShapeDtypeStruct((8 * rows, 128), BF16),
        ]
        + [jax.ShapeDtypeStruct(shape, BF16) for shape in shapes],
        in_specs=[HBM] + [IN_VMEM] * 4 + [HBM] * 3,
        out_specs=[IN_VMEM] * 3 + [HBM] + [IN_VMEM] * 3,
        scratch_shapes=scratch + semaphores(SEQ_COPIES + 7 + 3 * FSDP_COPIES, 4),
        compiler_params=params(4),
        name="scatter_hidden",
    )(part, h1, dy, gain, wo, gate, up, down)


def keys_kernel(
    branch, h1, gkv, gout, gate, up, down, gq,
    layer_ref, gkv_out, gout_out, gate_all, up_all, down_all, gq_out,
    *scratch,
):
    copies, places = Copies(*scratch[14:]), Places()
    greet(places.gather_peers() + places.strip_peers())
    moved = Strips(copies, places, gq, gq_out)
    sums = [
        FsdpSum(copies, places, gkv, scratch[4:9], 512),
        FsdpSum(copies, places, gout, scratch[9:14], 32),
    ]
    hidden = SeqSum(copies, places, branch, scratch[:4], 64)
    stages = [
        seq_gather(copies, places, gate, gate_all, 0, (0, 32)),
        seq_gather(copies, places, up, up_all, 0, (0, 32)),
        seq_gather(copies, places, down, down_all, 0, (0, 16)),
    ]
    items = [hidden] + sums
    hidden.ready()
    hidden.send()
    for stage in stages:
        next(stage)
    for item in sums:
        item.ready()
        item.send()
    for item in items:
        item.relay()
    for stage in stages:
        next(stage)
    for item in items:
        item.cross()
    run_stages(stages)
    for item, out in zip(sums, (gkv_out, gout_out)):
        out[...] = item.total().astype(BF16)
    layer_ref[...] = (h1[...] + hidden.total()).astype(BF16)
    moved.wait()
    copies.finish()


def scatter_keys(branch, h1, gkv, gout, gate, up, down, gq):
    rows, width = h1.shape
    shapes = [a.shape[2:] for a in (gkv, gout)]
    scratch = seq_buffers((rows, width))
    for shape in shapes:
        scratch += fsdp_buffers(shape)
    wide = [jax.ShapeDtypeStruct((8 * a.shape[0],) + a.shape[1:], BF16) for a in (gate, up, down)]
    return pl.pallas_call(
        keys_kernel,
        out_shape=[jax.ShapeDtypeStruct((rows, width), BF16)]
        + [jax.ShapeDtypeStruct(shape, BF16) for shape in shapes]
        + wide
        + [jax.ShapeDtypeStruct(gq.shape, BF16)],
        in_specs=[HBM, IN_VMEM] + [HBM] * 6,
        out_specs=[IN_VMEM] * 3 + [HBM] * 4,
        scratch_shapes=scratch + semaphores(SEQ_COPIES + 2 * FSDP_COPIES + 27 + 7, 7),
        compiler_params=params(5),
        name="scatter_keys",
    )(branch, h1, gkv, gout, gate, up, down, gq)


def input_kernel(
    part, tokens, gain, gh1, pack, gout,
    grad_ref, pack_all, gout_all,
    small, *scratch,
):
    copies, places = Copies(*scratch[9:]), Places()
    greet(places.gather_peers())
    packs = FsdpSum(copies, places, pack, scratch[4:9], 48)
    hidden = SeqSum(copies, places, part, scratch[:4], 64)
    for item in (hidden, packs):
        item.ready()
        item.send()
    stages = [seq_gather(copies, places, gout, gout_all, 0, (0, 32))]
    next(stages[0])
    for item in (packs, hidden):
        item.relay()
    for item in (packs, hidden):
        item.cross()
    small[...] = packs.total().astype(BF16)
    stages.append(seq_gather(copies, places, small, pack_all, 0, (0, 48)))
    run_stages(stages)
    gn1 = hidden.total()
    value = tokens[...].astype(F32)
    inverse = unit_rows(value)
    normed = value * inverse
    weighted = gn1 * gain[...]
    inner = jnp.mean(weighted * normed, axis=-1, keepdims=True)
    grad_ref[...] = gh1[...] + inverse * (weighted - normed * inner)
    copies.finish()


def scatter_input(part, tokens, gain, gh1, pack, gout):
    rows, width = gh1.shape
    shape = pack.shape[2:]
    return pl.pallas_call(
        input_kernel,
        out_shape=[
            jax.ShapeDtypeStruct((rows, width), F32),
            jax.ShapeDtypeStruct((8 * shape[0], shape[1]), BF16),
            jax.ShapeDtypeStruct((8 * gout.shape[0], width), BF16),
        ],
        in_specs=[HBM] + [IN_VMEM] * 3 + [HBM] * 2,
        out_specs=[IN_VMEM] + [HBM] * 2,
        scratch_shapes=[pltpu.VMEM(shape, BF16)]
        + seq_buffers((rows, width))
        + fsdp_buffers(shape)
        + semaphores(SEQ_COPIES + FSDP_COPIES + 18, 4),
        compiler_params=params(6),
        name="scatter_input",
    )(part, tokens, gain, gh1, pack, gout)


def local(
    tokens,
    segments,
    cotangent,
    attention_gain,
    query_gain,
    key_gain,
    query_weight,
    key_weight,
    value_weight,
    out_weight,
    feedforward_gain,
    gate_weight,
    up_weight,
    down_weight,
):
    seq_count = lax.axis_size("seq")
    fsdp_count = lax.axis_size("fsdp")
    fsdp = lax.axis_index("fsdp")
    seq = lax.axis_index("seq")
    rows, width = tokens.shape
    block = rows * seq_count
    hidden = gate_weight.shape[1]
    part = hidden // seq_count
    per_head = (H // KVH) * HD
    block_start = fsdp * block
    take = lax.dynamic_slice_in_dim

    ratio = fsdp_count // seq_count
    pairs = [
        (
            f % seq_count * fsdp_count + ratio * s + f // (fsdp_count // ratio),
            s * fsdp_count + f,
        )
        for f in range(fsdp_count)
        for s in range(seq_count)
    ]
    back_pairs = [(b, a) for a, b in pairs]
    both = ("seq", "fsdp")

    gains = jnp.concatenate([attention_gain, feedforward_gain, query_gain, key_gain])
    heads_weight = jnp.concatenate(
        [
            take(query_weight, seq * per_head, per_head, 1),
            take(key_weight, seq * HD, HD, 1),
            take(value_weight, seq * HD, HD, 1),
        ],
        axis=1,
    )
    gains = jnp.pad(gains[None, :], ((0, 15), (0, heads_weight.shape[1] - gains.shape[0])))
    pieces = down_weight.shape[0] // seq_count
    down_piece = lax.ppermute(take(down_weight, seq * pieces, pieces, 0), both, pairs)
    down_piece = jnp.pad(down_piece, ((0, PIECE - pieces), (0, 0)))
    gate_up = jnp.stack(
        [take(gate_weight, seq * part, part, 1), take(up_weight, seq * part, part, 1)]
    )
    x_block, packs, wo = gather(
        "gather_inputs",
        1,
        [(tokens, 0, (0, 64))],
        [(jnp.concatenate([heads_weight, gains]), 0, (0, 48)), (out_weight, 0, (0, 32))],
    )
    packs = packs.reshape(fsdp_count, -1, packs.shape[1])
    heads_weight = packs[:, : width // fsdp_count].reshape(width, -1)
    gains = packs[:, width // fsdp_count].astype(F32)

    shard = width // fsdp_count
    gain_one = gains[:, :shard].reshape(width)
    gain_two = gains[:, shard : 2 * shard].reshape(width)
    qshard = HD // fsdp_count
    gain_q = gains[:, 2 * shard : 2 * shard + qshard].reshape(HD)
    gain_k = gains[:, 2 * shard + qshard : 2 * shard + 2 * qshard].reshape(HD)

    starts = doc_starts(segments)
    labels = jnp.arange(DOCS, dtype=jnp.int32)

    def firsts(ids):
        picked = (ids[:, None] == labels[None, :]).astype(jnp.int32)
        return jnp.sum(picked * starts[None, :], axis=1)

    index = block_start + jnp.arange(block, dtype=jnp.int32)
    positions = index - firsts(take(segments, block_start, block))
    freqs = THETA ** (-2.0 * jnp.arange(HD // 2, dtype=F32) / HD)
    angles = positions.astype(F32)[:, None] * freqs[None, :]
    cosine, sine = jnp.cos(angles), jnp.sin(angles)
    shift = (HD**0.5 * LOG2E) * jnp.max(jnp.abs(gain_q)) * jnp.max(jnp.abs(gain_k))
    shift = shift.reshape(1)

    core, chip = fsdp % 2, fsdp // 2
    strip_ids = segments.reshape(fsdp_count // 2, 2, block // STRIP, STRIP)
    strip_ids = lax.dynamic_index_in_dim(strip_ids, core, 1, keepdims=False)
    strip_ids = lax.dynamic_index_in_dim(strip_ids, chip, 1, keepdims=False)
    first = firsts(strip_ids.reshape(-1))
    strip_first = first.reshape(-1, STRIP)
    q_first = (2 * jnp.arange(fsdp_count // 2, dtype=jnp.int32) + core) * block + chip * STRIP
    low = strip_first[:, 0] // KEYS
    high = (q_first + STRIP - 1) // KEYS + 1
    inner_low = jnp.minimum((strip_first[:, STRIP - 1] + KEYS - 1) // KEYS, high)
    inner_high = jnp.maximum((q_first + 1) // KEYS, inner_low)
    ranges = jnp.stack([low, inner_low, inner_high, high, q_first])

    x = x_block.astype(F32)
    inverse_one = rms_scale(x)
    n1 = (x * inverse_one * gain_one).astype(BF16)
    pre = dot_nn(n1, heads_weight)
    qp = pre[:, :per_head].reshape(block, H // KVH, HD)
    kp = pre[:, per_head : per_head + HD]
    value = pre[:, per_head + HD :].astype(BF16)
    inverse_q = rms_scale(qp)
    inverse_k = rms_scale(kp)
    q = rotate(qp * inverse_q * gain_q, cosine[:, None, :], sine[:, None, :]).astype(BF16)
    k = rotate(kp * inverse_k * gain_k, cosine, sine).astype(BF16)
    dy_block, kv, q = gather(
        "gather_keys",
        2,
        [(cotangent, 0, (0, 64))],
        [(jnp.concatenate([k, value], axis=1), 0, (0, 512))],
        [q.reshape(block, per_head)],
    )

    ob, o, totals = forward_attention(ranges, shift, q, first[:, None], kv)
    ob_own, h1_own, n2, gate_up, down_w = gather_attended(
        ob, wo, tokens, gain_two[None, :], gate_up, down_piece
    )
    down_w = down_w.reshape(fsdp_count, PIECE, width)[:, :pieces].reshape(part, width)

    gn2_part, branch, g_gate, g_up, g_down = feed_forward(n2, dy_block, gate_up, down_w)
    by_core = lambda array: array.reshape(8, 2, -1, array.shape[-1])
    g_down = g_down.reshape(fsdp_count, pieces, width)
    g_down = jnp.pad(g_down, ((0, 0), (0, PIECE - pieces), (0, 0)))
    gh1, gb, gain_two_term, go, g_gate, g_up, g_down = scatter_hidden(
        gn2_part.reshape(seq_count, rows, width),
        h1_own,
        cotangent,
        gain_two[None, :],
        wo,
        by_core(g_gate),
        by_core(g_up),
        by_core(g_down.reshape(-1, width)),
    )
    g_down = lax.ppermute(g_down, both, back_pairs)
    g_out = dot_tn(ob_own, gb).astype(BF16)
    gq, gkv = backward_attention(
        ranges, shift, q, go, o, totals, strip_first[:, None, :], kv
    )
    layer_out, gkv, g_out, g_gate, g_up, g_down, gq = scatter_keys(
        branch.reshape(seq_count, rows, width),
        h1_own,
        by_core(gkv),
        by_core(g_out),
        g_gate,
        g_up,
        g_down,
        gq,
    )
    gq = gq.astype(F32).reshape(block, H // KVH, HD)
    gk = gkv[:, :HD].astype(F32)
    gv = gkv[:, HD:]
    gain_q_term, gqp = norm_back(
        qp, inverse_q, gain_q, rotate(gq, cosine[:, None, :], -sine[:, None, :])
    )
    gain_k_term, gkp = norm_back(kp, inverse_k, gain_k, rotate(gk, cosine, -sine))
    gpre = jnp.concatenate(
        [gqp.reshape(block, per_head).astype(BF16), gkp.astype(BF16), gv], axis=1
    )
    gn1_partial = dot_nt(gpre, heads_weight)
    gain_one_term = jnp.sum(gn1_partial * (x * inverse_one), axis=0)
    g_heads = dot_tn(n1, gpre).astype(BF16).reshape(fsdp_count, shard, -1)
    terms = jnp.concatenate(
        [
            gain_one_term.reshape(fsdp_count, shard),
            gain_two_term.reshape(fsdp_count, shard),
            gain_q_term.reshape(fsdp_count, qshard),
            gain_k_term.reshape(fsdp_count, qshard),
        ],
        axis=1,
    ).astype(BF16)
    terms = jnp.pad(terms[:, None, :], ((0, 0), (0, 15), (0, g_heads.shape[2] - terms.shape[1])))
    pack = jnp.concatenate([g_heads, terms], axis=1)
    input_grad, packs, g_out = scatter_input(
        gn1_partial.astype(BF16).reshape(seq_count, rows, width),
        tokens,
        gain_one[None, :],
        gh1,
        pack.reshape((8, 2) + pack.shape[1:]),
        g_out,
    )
    packs = packs.reshape((seq_count,) + pack.shape[1:])
    g_heads = packs[:, :shard]
    terms = jnp.sum(packs[:, shard].astype(F32), axis=0)
    g_out = jnp.sum(g_out.reshape(seq_count, shard, width).astype(F32), axis=0)
    g_down = g_down.reshape(seq_count, PIECE, width)[:, :pieces].reshape(-1, width)
    columns = lambda a: jnp.transpose(a.reshape(seq_count, shard, part), (1, 0, 2)).reshape(shard, hidden)

    g_query = jnp.transpose(g_heads[:, :, :per_head], (1, 0, 2)).reshape(shard, H * HD)
    g_key = jnp.transpose(g_heads[:, :, per_head : per_head + HD], (1, 0, 2)).reshape(shard, KVH * HD)
    g_value = jnp.transpose(g_heads[:, :, per_head + HD :], (1, 0, 2)).reshape(shard, KVH * HD)

    return (
        layer_out,
        input_grad,
        terms[:shard],
        terms[2 * shard : 2 * shard + qshard],
        terms[2 * shard + qshard : 2 * shard + 2 * qshard],
        g_query.astype(F32),
        g_key.astype(F32),
        g_value.astype(F32),
        g_out,
        terms[shard : 2 * shard],
        columns(g_gate).astype(F32),
        columns(g_up).astype(F32),
        g_down.astype(F32),
    )


def solution(mesh):
    rows = P(("fsdp", "seq"), None)
    matrix = P("fsdp", None)
    vector = P("fsdp")
    in_specs = (rows, P(), rows) + (vector,) * 3 + (matrix,) * 4 + (vector,) + (matrix,) * 3
    out_specs = (rows, rows) + (vector,) * 3 + (matrix,) * 4 + (vector,) + (matrix,) * 3
    return jax.shard_map(local, mesh=mesh, in_specs=in_specs, out_specs=out_specs, check_vma=False)
```

```python
import functools
import math

import jax
import jax.numpy as jnp
from jax import lax
from jax.experimental import pallas as pl
from jax.experimental.pallas import tpu as pltpu
from jax.sharding import PartitionSpec as P

H = 16
KVH = 8
HD = 64
DOCS = 4
EPSILON = 1e-06
THETA = 1000000.0
LOG2E = math.log2(math.e)
F32 = jnp.float32
BF16 = jnp.bfloat16
STRIP = 128
FEED = 256
KEYS = 1024
VMEM = 56 * 1024 * 1024
PIECE = 48


def doc_starts(segments):
    labels = jnp.arange(DOCS, dtype=jnp.int32)
    member = (segments[None, :] == labels[:, None]).astype(jnp.int32)
    lengths = jnp.sum(member, axis=1)
    return jnp.cumsum(lengths) - lengths


def dot_nt(a, b):
    return lax.dot_general(a, b, (((1,), (1,)), ((), ())), preferred_element_type=F32)


def dot_tn(a, b):
    return lax.dot_general(a, b, (((0,), (0,)), ((), ())), preferred_element_type=F32)


def dot_nn(a, b):
    return jnp.dot(a, b, preferred_element_type=F32)


def key_loops(ranges_ref, tile, step):
    low, inner_low, inner_high, high = [ranges_ref[i, tile] for i in range(4)]

    def masked(block, _):
        step(block, True)
        return 0

    def plain(block, _):
        step(block, False)
        return 0

    lax.fori_loop(low, inner_low, masked, 0)
    lax.fori_loop(inner_low, inner_high, plain, 0)
    lax.fori_loop(inner_high, high, masked, 0)


def lanes_low(shape):
    return lax.broadcasted_iota(jnp.int32, shape, 1) < HD


def two_heads(packed, low):
    other = pltpu.roll(packed, HD, 1)
    heads = (packed, other) if low else (other, packed)
    keep = lanes_low(packed.shape) if low else ~lanes_low(packed.shape)
    return jnp.concatenate([jnp.where(keep, head, 0.0) for head in heads], axis=0)


def one_row(heads, low):
    rows = heads.shape[0] // 2
    first, second = heads[:rows], heads[rows:]
    if low:
        second = pltpu.roll(second, HD, 1)
    else:
        first = pltpu.roll(first, HD, 1)
    return jnp.where(lanes_low(first.shape), first, second)


def forward_kernel(
    ranges_ref, shift_ref, query_ref, first_ref, kv_ref, ob_ref, o_ref, totals_ref, total
):
    tile = pl.program_id(0)
    rows = query_ref.shape[0]
    query = two_heads(query_ref[...].astype(F32) * HD**-0.5, True).astype(BF16)
    first = jnp.concatenate([first_ref[...]] * 2, axis=0)
    index = ranges_ref[4, tile] + lax.broadcasted_iota(jnp.int32, (rows, 1), 0)
    index = jnp.concatenate([index, index], axis=0)
    shift = shift_ref[0]
    ones = jnp.ones((KEYS, 2 * HD), BF16)
    total[...] = jnp.zeros_like(total)

    def step(block, masked):
        start = pl.multiple_of(block * KEYS, KEYS)
        kv = kv_ref[pl.ds(start, KEYS), :]
        exps = jnp.exp2(dot_nt(query, kv) * LOG2E - shift)
        if masked:
            keys = start + lax.broadcasted_iota(jnp.int32, (2 * rows, KEYS), 1)
            exps = jnp.where((keys >= first) & (keys <= index), exps, 0.0)
        total[...] += dot_nn(exps.astype(BF16), jnp.concatenate([kv, ones], axis=1))

    key_loops(ranges_ref, tile, step)
    totals = total[:, 2 * HD :]
    o = total[:, : 2 * HD] / totals
    o_ref[0] = o
    totals_ref[0] = totals
    ob_ref[...] = one_row(o, False).astype(BF16)


def forward_attention(ranges, shift, query, first, kv):
    tiles = query.shape[0] // STRIP
    whole = lambda t, *_: (0, 0)
    part = lambda t, *_: (t, 0)
    wide = lambda t, *_: (t, 0, 0)
    return pl.pallas_call(
        forward_kernel,
        grid_spec=pltpu.PrefetchScalarGridSpec(
            num_scalar_prefetch=2,
            grid=(tiles,),
            in_specs=[
                pl.BlockSpec((STRIP, 2 * HD), part),
                pl.BlockSpec((STRIP, 1), part),
                pl.BlockSpec(kv.shape, whole),
            ],
            out_specs=[
                pl.BlockSpec((STRIP, 2 * HD), part),
                pl.BlockSpec((1, 2 * STRIP, 2 * HD), wide),
                pl.BlockSpec((1, 2 * STRIP, 2 * HD), wide),
            ],
            scratch_shapes=[pltpu.VMEM((2 * STRIP, 4 * HD), F32)],
        ),
        out_shape=[
            jax.ShapeDtypeStruct(query.shape, BF16),
            jax.ShapeDtypeStruct((tiles, 2 * STRIP, 2 * HD), F32),
            jax.ShapeDtypeStruct((tiles, 2 * STRIP, 2 * HD), F32),
        ],
        compiler_params=pltpu.CompilerParams(vmem_limit_bytes=VMEM),
        cost_estimate=pl.CostEstimate(
            flops=8 * 10**9, bytes_accessed=8 * 10**6, transcendentals=16 * 10**6
        ),
        name="attention_forward",
    )(ranges, shift, query, first, kv)


def backward_kernel(
    ranges_ref, shift_ref, query_ref, grad_ref, o_ref, totals_ref, first_ref, kv_ref,
    gq_ref, gkv_ref, total, gq,
):
    tile = pl.program_id(0)
    rows = query_ref.shape[0]
    query = two_heads(query_ref[...].astype(F32) * HD**-0.5, True).astype(BF16)
    go = two_heads(grad_ref[...].astype(F32), False)
    totals = totals_ref[0]
    grad = (go / totals).astype(BF16)
    delta = jnp.sum(go * o_ref[0], axis=1, keepdims=True) / totals
    delta = jnp.transpose(delta)[:1]
    both = jnp.concatenate([query, grad], axis=0)
    first = jnp.concatenate([first_ref[0]] * 2, axis=1)
    index = ranges_ref[4, tile] + lax.broadcasted_iota(jnp.int32, (1, rows), 1)
    index = jnp.concatenate([index, index], axis=1)
    shift = shift_ref[0]

    @pl.when(tile == 0)
    def _():
        total[...] = jnp.zeros_like(total)

    gq[...] = jnp.zeros_like(gq)

    def step(block, masked):
        start = pl.multiple_of(block * KEYS, KEYS)
        kv = kv_ref[pl.ds(start, KEYS), :]
        exps = jnp.exp2(dot_nt(kv, query) * LOG2E - shift)
        if masked:
            keys = start + lax.broadcasted_iota(jnp.int32, (KEYS, 2 * rows), 0)
            exps = jnp.where((keys >= first) & (keys <= index), exps, 0.0)
        scores = (exps * (dot_nt(kv, grad) - delta)).astype(BF16)
        gq[...] += dot_tn(scores, kv)
        total[pl.ds(start, KEYS), :] += dot_nn(
            jnp.concatenate([scores, exps.astype(BF16)], axis=1), both
        )

    key_loops(ranges_ref, tile, step)
    gq_ref[...] = (one_row(gq[...], True) * HD**-0.5).astype(BF16)

    @pl.when(tile == pl.num_programs(0) - 1)
    def _():
        gkv_ref[...] = total[...].astype(BF16)


def backward_attention(ranges, shift, query, grad, o, totals, first, kv):
    tiles = query.shape[0] // STRIP
    whole = lambda t, *_: (0, 0)
    part = lambda t, *_: (t, 0)
    wide = lambda t, *_: (t, 0, 0)
    return pl.pallas_call(
        backward_kernel,
        grid_spec=pltpu.PrefetchScalarGridSpec(
            num_scalar_prefetch=2,
            grid=(tiles,),
            in_specs=[
                pl.BlockSpec((STRIP, 2 * HD), part),
                pl.BlockSpec((STRIP, 2 * HD), part),
                pl.BlockSpec((1, 2 * STRIP, 2 * HD), wide),
                pl.BlockSpec((1, 2 * STRIP, 2 * HD), wide),
                pl.BlockSpec((1, 1, STRIP), wide),
                pl.BlockSpec(kv.shape, whole),
            ],
            out_specs=[
                pl.BlockSpec((STRIP, 2 * HD), part),
                pl.BlockSpec(kv.shape, whole),
            ],
            scratch_shapes=[pltpu.VMEM(kv.shape, F32), pltpu.VMEM((2 * STRIP, 2 * HD), F32)],
        ),
        out_shape=[
            jax.ShapeDtypeStruct(query.shape, BF16),
            jax.ShapeDtypeStruct(kv.shape, BF16),
        ],
        compiler_params=pltpu.CompilerParams(vmem_limit_bytes=VMEM),
        cost_estimate=pl.CostEstimate(
            flops=20 * 10**9, bytes_accessed=16 * 10**6, transcendentals=16 * 10**6
        ),
        name="attention_backward",
    )(ranges, shift, query, grad, o, totals, first, kv)


MESH = pl.DeviceIdType.MESH
HBM = pl.BlockSpec(memory_space=pl.ANY)
IN_VMEM = pl.BlockSpec(memory_space=pltpu.VMEM)
RING = 8


def pair_of(value):
    return value + 1 - 2 * lax.rem(value, 2)


def ring_step(index, steps):
    return lax.div(index, RING) * RING + lax.rem(lax.rem(index, RING) + 2 * steps, RING)


class Copies:
    def __init__(self, send, recv, local):
        self.send, self.recv, self.local = send, recv, local
        self.started, self.locals = [], []

    def remote(self, src, dst, peer, recv=None):
        i = len(self.started)
        copy = pltpu.make_async_remote_copy(
            src_ref=src,
            dst_ref=dst,
            send_sem=self.send.at[i],
            recv_sem=self.recv.at[i] if recv is None else recv,
            device_id=peer,
            device_id_type=MESH,
        )
        copy.start()
        self.started.append(copy)
        return copy

    def here(self, src, dst):
        copy = pltpu.make_async_copy(src, dst, self.local.at[len(self.locals)])
        copy.start()
        self.locals.append(copy)
        return copy

    def finish(self):
        for copy in self.started:
            copy.wait_send()


def greet(peers):
    barrier = pltpu.get_barrier_semaphore()
    for peer in peers:
        pl.semaphore_signal(barrier, inc=1, device_id=peer, device_id_type=MESH)
    pl.semaphore_wait(barrier, len(peers))


def slot(ref, axis, size, index, split=None, half=0):
    start = index * size
    where = [pl.ds(0, n) for n in ref.shape]
    where[axis] = pl.ds(pl.multiple_of(start, 16), size)
    if split is not None:
        along, cut = split
        whole = size if along == axis else ref.shape[along]
        base = start if along == axis else 0
        begin, count = (0, cut) if half == 0 else (cut, whole - cut)
        offset = base + begin
        where[along] = pl.ds(pl.multiple_of(offset, 16) if along == axis else offset, count)
    return ref.at[tuple(where)]


def gather_stages(copies, src, out, axis, size, split, me, pair, device, sibling):
    plus, minus = ring_step(me, 1), ring_step(me, 3)
    at = functools.partial(slot, out, axis, size)
    halves = lambda index, half: at(index, split, half)
    to_sibling = []

    def pass_on(index):
        if sibling is not None:
            to_sibling.append(copies.remote(at(index), at(index), device(sibling)))

    kept = copies.here(src, at(me))
    first = copies.remote(src, at(me), device(pair))
    up = copies.remote(src, at(me), device(plus))
    down = copies.remote(src, at(me), device(minus))
    if sibling is not None:
        to_sibling.append(copies.remote(src, at(me), device(sibling)))
    yield
    up.wait_recv()
    far = [copies.remote(halves(minus, 0), halves(minus, 0), device(plus))]
    pass_on(minus)
    down.wait_recv()
    far.append(copies.remote(halves(plus, 1), halves(plus, 1), device(minus)))
    pass_on(plus)
    yield
    first.wait_recv()
    up = copies.remote(at(pair), at(pair), device(plus))
    down = copies.remote(at(pair), at(pair), device(minus))
    pass_on(pair)
    yield
    shift = pair - me
    up.wait_recv()
    last = [copies.remote(halves(minus + shift, 0), halves(minus + shift, 0), device(plus))]
    pass_on(minus + shift)
    down.wait_recv()
    last.append(copies.remote(halves(plus + shift, 1), halves(plus + shift, 1), device(minus)))
    pass_on(plus + shift)
    yield
    opposite = ring_step(me, 2)
    for copy in far:
        copy.wait_recv()
    pass_on(opposite)
    yield
    for copy in last:
        copy.wait_recv()
    pass_on(opposite + shift)
    yield
    for copy in to_sibling:
        copy.wait_recv()
    kept.wait()


def run_stages(stages):
    live = list(stages)
    while live:
        live = [stage for stage in live if next(stage, stage) is not stage]


class Swap:
    def __init__(self, copies, recv, sem, tag, stays, sends):
        self.copies, self.recv, self.tag, self.stays = copies, recv, tag, stays
        (src, dst, peer), rest = sends[0], sends[1:]
        self.own = pltpu.make_async_remote_copy(
            src_ref=src,
            dst_ref=dst,
            send_sem=sem.at[0],
            recv_sem=recv.at[tag],
            device_id=peer,
            device_id_type=MESH,
        )
        self.kept = pltpu.make_async_copy(src, dst, sem.at[1])

        @pl.when(stays)
        def _():
            self.kept.start()

        @pl.when(jnp.logical_not(stays))
        def _():
            self.own.start()

        self.sample = (src, dst, peer, sem)
        for src, dst, peer in rest:
            copies.remote(src, dst, peer, recv.at[tag])

    def wait(self, landing):
        src, _, peer, sem = self.sample
        for step in range(1, 8):
            sender = lax.rem(self.tag + step, 8)
            pltpu.make_async_remote_copy(
                src_ref=src,
                dst_ref=landing(sender),
                send_sem=sem.at[0],
                recv_sem=self.recv.at[sender],
                device_id=peer,
                device_id_type=MESH,
            ).wait_recv()

        @pl.when(self.stays)
        def _():
            self.kept.wait()

        @pl.when(jnp.logical_not(self.stays))
        def _():
            self.own.wait()


def greet_for_swaps(places, peers):
    barrier = pltpu.get_barrier_semaphore()
    senders, others = places.heads()[1], places.owners()[1]
    peers = peers + senders[1:] + others[1:]
    for peer in peers:
        pl.semaphore_signal(barrier, inc=1, device_id=peer, device_id_type=MESH)

    @pl.when(places.stays)
    def _():
        pl.semaphore_wait(barrier, len(peers))

    @pl.when(jnp.logical_not(places.stays))
    def _():
        for peer in (senders[0], others[0]):
            pl.semaphore_signal(barrier, inc=1, device_id=peer, device_id_type=MESH)
        pl.semaphore_wait(barrier, len(peers) + 2)


def strips_at(ref, index):
    return ref.at[pl.ds(pl.multiple_of(index * STRIP, STRIP), STRIP), :]


def heads_at(ref, index):
    return ref.at[:, pl.ds(pl.multiple_of(index * 2 * HD, 2 * HD), 2 * HD)]


class Places:
    def __init__(self):
        self.seq, self.fsdp = lax.axis_index("seq"), lax.axis_index("fsdp")
        self.core = lax.rem(self.fsdp, 2)
        self.chip = lax.div(self.fsdp, 2)
        self.row = lax.div(self.chip, 4)
        self.col = lax.rem(self.chip, 4)
        self.sibling = pair_of(self.fsdp)
        self.across = lax.rem(self.fsdp + 8, 16)
        self.stays = self.chip == self.seq

    def on_seq(self, index):
        return (index, self.fsdp)

    def on_fsdp(self, index):
        return (self.seq, index)

    def other_seq(self, step):
        return lax.rem(self.seq + step, 8)

    def other_chip(self, step):
        return lax.rem(self.row + step // 4, 2) * 4 + lax.rem(self.col + step % 4, 4)

    def gather_peers(self):
        seq = [pair_of(self.seq), ring_step(self.seq, 1), ring_step(self.seq, 3)]
        fsdp = [self.across, ring_step(self.fsdp, 1), ring_step(self.fsdp, 3), self.sibling]
        return [self.on_seq(i) for i in seq] + [self.on_fsdp(i) for i in fsdp]

    def strip_peers(self):
        return [self.on_fsdp(self.other_chip(d) * 2 + self.core) for d in range(1, 8)]

    def owners(self):
        strips = [lax.rem(self.chip + d, 8) for d in range(8)]
        return strips, [(self.chip, strip * 2 + self.core) for strip in strips]

    def heads(self):
        heads = [lax.rem(self.seq + d, 8) for d in range(8)]
        return heads, [(head, self.seq * 2 + self.core) for head in heads]


def params(name_id):
    return pltpu.CompilerParams(
        collective_id=name_id, has_side_effects=True, vmem_limit_bytes=VMEM
    )


def semaphores(remote, local):
    return [
        pltpu.SemaphoreType.DMA((remote,)),
        pltpu.SemaphoreType.DMA((remote,)),
        pltpu.SemaphoreType.DMA((local,)),
    ]


def seq_gather(copies, places, src, out, axis, split):
    size = src.shape[axis]
    return gather_stages(
        copies, src, out, axis, size, split, places.seq, pair_of(places.seq), places.on_seq, None
    )


def fsdp_gather(copies, places, src, out, axis, split):
    size = src.shape[axis]
    return gather_stages(
        copies, src, out, axis, size, split, places.fsdp, places.across, places.on_fsdp, places.sibling
    )


class Strips:
    def __init__(self, copies, places, src, out):
        self.kept = copies.here(strips_at(src, places.chip), strips_at(out, places.chip))
        self.copies = []
        for d in range(1, 8):
            chip = places.other_chip(d)
            peer = places.on_fsdp(chip * 2 + places.core)
            self.copies.append(copies.remote(strips_at(src, chip), strips_at(out, places.chip), peer))

    def wait(self):
        for copy in self.copies:
            copy.wait_recv()
        self.kept.wait()


def gather(name, name_id, seq_items, fsdp_items, strips=()):
    items = seq_items + fsdp_items
    count = len(items)
    every = count + len(strips)

    def kernel(*refs):
        srcs, outs = refs[:every], refs[every : 2 * every]
        copies, places = Copies(*refs[2 * every :]), Places()
        greet(places.gather_peers() + (places.strip_peers() if strips else []))
        stages = []
        order = list(range(count))
        for i in order[::-1] if strips else order:
            _, axis, split = items[i]
            make = seq_gather if i < len(seq_items) else fsdp_gather
            stages.append(make(copies, places, srcs[i], outs[i], axis, split))
            next(stages[-1])
        moved = [Strips(copies, places, srcs[i], outs[i]) for i in range(count, every)]
        run_stages(stages)
        for item in moved:
            item.wait()
        copies.finish()

    shapes = []
    for i, (array, axis, _) in enumerate(items):
        shape = list(array.shape)
        shape[axis] *= 8 if i < len(seq_items) else 16
        shapes.append(jax.ShapeDtypeStruct(tuple(shape), array.dtype))
    shapes += [jax.ShapeDtypeStruct(array.shape, array.dtype) for array in strips]
    remote = 9 * len(seq_items) + 17 * len(fsdp_items) + 7 * len(strips)
    return pl.pallas_call(
        kernel,
        out_shape=shapes,
        in_specs=[HBM] * every,
        out_specs=[HBM] * every,
        scratch_shapes=semaphores(remote, every),
        compiler_params=params(name_id),
        name=name,
    )(*[item[0] for item in items], *strips)


class RingSum:
    def __init__(self, copies, near, mine, held, cut, index, device):
        self.remote, self.mine, self.device = copies.remote, mine, device
        self.half, self.ring, self.other = held
        self.cut, self.index = cut, index
        self.plus, self.minus, self.pair = near

    def parts(self):
        rows = self.mine.shape[1]
        return pl.ds(0, self.cut), pl.ds(self.cut, rows - self.cut)

    def send(self):
        low, high = self.parts()
        self.first, self.second = [], []
        for flip in (1, 0):
            far, up, down = [self.mine.at[self.index(flip, step)] for step in (2, 1, 3)]
            self.first.append(
                (
                    self.remote(far.at[low], self.half.at[flip, low], self.plus),
                    self.remote(far.at[high], self.half.at[flip, high], self.minus),
                )
            )
            self.second.append(
                [
                    self.remote(up.at[high], self.ring.at[flip, 0, high], self.plus),
                    self.remote(down.at[low], self.ring.at[flip, 1, low], self.minus),
                ]
            )

    def relay(self):
        low, high = self.parts()
        for i, flip in enumerate((1, 0)):
            for copy, step, part, way, peer in (
                (self.first[i][0], 1, low, 0, self.plus),
                (self.first[i][1], 3, high, 1, self.minus),
            ):
                copy.wait_recv()
                at = self.index(flip, step)
                self.mine[at, part] = (
                    self.mine[at, part].astype(F32) + self.half[flip, part].astype(F32)
                ).astype(BF16)
                self.second[i].append(
                    self.remote(self.mine.at[at, part], self.ring.at[flip, way, part], peer)
                )

    def gathered(self, i, flip):
        for copy in self.second[i]:
            copy.wait_recv()
        return (
            self.mine[self.index(flip, 0)].astype(F32)
            + self.ring[flip, 0].astype(F32)
            + self.ring[flip, 1].astype(F32)
        )

    def cross(self):
        self.other[0] = self.gathered(0, 1).astype(BF16)
        self.last = self.remote(self.other.at[0], self.other.at[1], self.pair)

    def total(self):
        total = self.gathered(1, 0)
        self.last.wait_recv()
        return total + self.other[1].astype(F32)


def ring_buffers(shape):
    return [
        pltpu.VMEM((2,) + shape, BF16),
        pltpu.VMEM((2, 2) + shape, BF16),
        pltpu.VMEM((2,) + shape, BF16),
    ]


RING_COPIES = 13


class SeqSum(RingSum):
    def __init__(self, copies, places, part, buffers, cut):
        mine, held = buffers[0], buffers[1:]
        seq = places.seq

        def index(flip, step):
            base = ring_step(seq, step)
            return pair_of(base) if flip else base

        near = [places.on_seq(i) for i in (ring_step(seq, 1), ring_step(seq, 3), pair_of(seq))]
        super().__init__(copies, near, mine, held, cut, index, places.on_seq)
        self.kept = copies.here(part, mine)

    def ready(self):
        self.kept.wait()


class FsdpSum(RingSum):
    def __init__(self, copies, places, part, buffers, cut):
        mine, self.theirs, held = buffers[0], buffers[1], buffers[2:]
        fsdp = places.fsdp

        def index(flip, step):
            return lax.rem(places.row + flip, 2) * 4 + lax.rem(places.col + step, 4)

        near = [places.on_fsdp(i) for i in (ring_step(fsdp, 1), ring_step(fsdp, 3), places.across)]
        super().__init__(copies, near, mine, held, cut, index, places.on_fsdp)
        self.order = [index(flip, step) for flip in (1, 0) for step in (2, 1, 3, 0)]
        self.others = [
            copies.remote(
                part.at[at, 1 - places.core], self.theirs.at[at], places.on_fsdp(places.sibling)
            )
            for at in self.order
        ]
        self.kept = copies.here(part.at[:, places.core], mine)

    def ready(self):
        self.kept.wait()
        for at, copy in zip(self.order, self.others):
            copy.wait_recv()
            self.mine[at] = (self.mine[at].astype(F32) + self.theirs[at].astype(F32)).astype(BF16)


def seq_buffers(shape):
    return [pltpu.VMEM((8,) + shape, BF16)] + ring_buffers(shape)


def fsdp_buffers(shape):
    return [pltpu.VMEM((8,) + shape, BF16)] * 2 + ring_buffers(shape)


SEQ_COPIES = RING_COPIES
FSDP_COPIES = RING_COPIES + 8


def unit_rows(values):
    return lax.rsqrt(jnp.mean(values * values, axis=-1, keepdims=True) + EPSILON)


def spread(pieces, part):
    shape = (pieces * PIECE, part)
    row = lax.broadcasted_iota(jnp.int32, shape, 0)
    column = lax.broadcasted_iota(jnp.int32, shape, 1)
    size = part // pieces
    inside = lax.rem(row, PIECE)
    hit = (lax.div(row, PIECE) * size + inside == column) & (inside < size)
    return jnp.where(hit, 1.0, 0.0).astype(BF16)


def hidden_kernel(
    ob, wo, tokens, dy_own, gain, gate_up, down, dy,
    own_ref, h1_ref, branch_ref, gh1_ref, gb_ref, term_ref, go_ref, gate_out, up_out, down_out,
    own, n2, go_own, n2_all, weights, down_pad, down_all, act, ggate, gup, gn2_all, held,
    gate_part, up_part, down_part, *scratch,
):
    sums_at = scratch[:15]
    tags, ends, tags_back, ends_back = scratch[15:19]
    copies, places = Copies(*scratch[19:]), Places()
    others = [places.on_seq(places.other_seq(d)) for d in range(1, 8)]
    greet_for_swaps(places, places.gather_peers() + others)
    rows, width = own.shape
    part = down_all.shape[0]
    pieces = down_pad.shape[0] // PIECE

    strips, owners = places.owners()
    heads, workers = places.heads()
    landing = heads_at(own, places.seq)
    sends = [(strips_at(ob, strip), landing, peer) for strip, peer in zip(strips, owners)]
    swap = Swap(copies, tags, ends, places.seq, places.stays, sends)
    gathers = [
        fsdp_gather(copies, places, gate_up, weights, 1, (1, 32)),
        fsdp_gather(copies, places, down, down_pad, 0, (0, 32)),
    ]
    for stage in gathers:
        next(stage)
    swap.wait(lambda sender: heads_at(own, sender))
    own_ref[...] = own[...]

    def project(j, _):
        at = pl.ds(pl.multiple_of(j * 256, 256), 256)
        h1_ref[:, at] = tokens[:, at].astype(F32) + dot_nn(own[...], wo[:, at])
        return 0

    lax.fori_loop(0, width // 256, project, 0)
    value = h1_ref[...]
    inverse = unit_rows(value)
    n2[...] = (value * inverse * gain[...]).astype(BF16)
    tokens_in = seq_gather(copies, places, n2, n2_all, 0, (0, 64))
    next(tokens_in)
    for _ in range(3):
        for stage in gathers:
            next(stage)
        if _ < 2:
            next(tokens_in)
    run_stages(gathers)
    matrix = spread(pieces, part)

    def pack_down(j, _):
        at = pl.ds(pl.multiple_of(j * 256, 256), 256)
        down_all[:, at] = dot_tn(matrix, down_pad[:, at]).astype(BF16)
        return 0

    lax.fori_loop(0, width // 256, pack_down, 0)

    arrivals = []

    def feed(step):
        base = lax.div(ring_step(places.seq, step), 2) * 2 * rows
        at = pl.ds(pl.multiple_of(base, 2 * rows), 2 * rows)
        values = n2_all[at, :]
        gate = dot_nn(values, weights[0])
        up = dot_nn(values, weights[1])
        gact = dot_nt(dy[at, :], down_all[...])
        sig = jax.nn.sigmoid(gate)
        silu = gate * sig
        act_here = (silu * up).astype(BF16)
        gg = (gact * up * sig * (1.0 + gate * (1.0 - sig))).astype(BF16)
        gu = (gact * silu).astype(BF16)
        act[at, :] = act_here
        ggate[at, :] = gg
        gup[at, :] = gu
        gn2_all[at, :] = (dot_nt(gg, weights[0]) + dot_nt(gu, weights[1])).astype(BF16)
        for flip in (1, 0):
            if step == 0 and flip == 0:
                continue
            peer = ring_step(places.seq, step)
            peer = pair_of(peer) if flip else peer
            arrivals.append(
                copies.remote(
                    gn2_all.at[pl.ds(pl.multiple_of(peer * rows, rows), rows), :],
                    held.at[2 * step + flip],
                    places.on_seq(peer),
                )
            )
        branch_ref[at, :] = dot_nn(act_here, down_all[...]).astype(BF16)

    tokens_in.send(None)
    kept_first = copies.locals[-1]
    kept_first.wait()
    feed(0)
    feed(1)
    feed(3)
    next(tokens_in)
    next(tokens_in)
    feed(2)

    def columns(c, _):
        at = pl.ds(pl.multiple_of(c * 256, 256), 256)
        values = n2_all[:, at]
        two = pl.ds(c * 2, 2)
        shape = (2, 2) + gate_part.shape[2:]
        gate_part[two] = dot_tn(values, ggate[...]).astype(BF16).reshape(shape)
        up_part[two] = dot_tn(values, gup[...]).astype(BF16).reshape(shape)
        g_down = dot_nn(matrix, dot_tn(act[...], dy[:, at]).astype(BF16)).astype(BF16)
        down_part[:, :, :, at] = g_down.reshape((8, 2, PIECE, 256))
        return 0

    lax.fori_loop(0, width // 256, columns, 0)
    sums = [
        FsdpSum(copies, places, gate_part, sums_at[:5], 32),
        FsdpSum(copies, places, up_part, sums_at[5:10], 32),
        FsdpSum(copies, places, down_part, sums_at[10:15], 32),
    ]
    for item in sums:
        item.ready()
        item.send()
    gn2 = gn2_all[pl.ds(pl.multiple_of(places.seq * rows, rows), rows), :].astype(F32)
    for copy in arrivals:
        copy.wait_recv()
    for slot_index in range(1, 8):
        gn2 += held[slot_index].astype(F32)
    value = h1_ref[...]
    inverse = unit_rows(value)
    normed = value * inverse
    term_ref[...] = jnp.sum(gn2 * normed, axis=0, keepdims=True)
    weighted = gn2 * gain[...]
    inner = jnp.mean(weighted * normed, axis=-1, keepdims=True)
    gh1 = dy_own[...].astype(F32) + inverse * (weighted - normed * inner)
    gh1_ref[...] = gh1
    gb_ref[...] = gh1.astype(BF16)

    def project_back(j, _):
        begin = pl.multiple_of(j * 256, 256)
        go_own[:, pl.ds(begin, 256)] = dot_nt(gb_ref[...], wo[pl.ds(begin, 256), :]).astype(BF16)
        return 0

    lax.fori_loop(0, width // 256, project_back, 0)
    landing = strips_at(go_ref, places.chip)
    sends = [(heads_at(go_own, head), landing, peer) for head, peer in zip(heads, workers)]
    swap_back = Swap(copies, tags_back, ends_back, places.chip, places.stays, sends)
    for item in sums:
        item.relay()
    for item in sums:
        item.cross()
    for item, out in zip(sums, (gate_out, up_out, down_out)):
        out[...] = item.total().astype(BF16)
    swap_back.wait(lambda sender: strips_at(go_ref, sender))
    copies.finish()


def hidden_block(ob, wo, tokens, dy_own, gain, gate_up, down, dy):
    rows, width = tokens.shape
    shard, part = gate_up.shape[1:]
    slices = [(shard, part), (shard, part), (PIECE, width)]
    block = (8 * rows, width)
    vmem = [(rows, width)] * 3 + [block, (2, width, part), (16 * PIECE, width), (part, width)]
    vmem += [(8 * rows, part)] * 3 + [block, (8, rows, width)]
    vmem += [(8, 2) + shape for shape in slices]
    scratch = [pltpu.VMEM(shape, BF16) for shape in vmem]
    for shape in slices:
        scratch += fsdp_buffers(shape)
    scratch += [pltpu.SemaphoreType.DMA((n,)) for n in (8, 2, 8, 2)]
    return pl.pallas_call(
        hidden_kernel,
        out_shape=[
            jax.ShapeDtypeStruct((rows, width), BF16),
            jax.ShapeDtypeStruct((rows, width), F32),
            jax.ShapeDtypeStruct(block, BF16),
            jax.ShapeDtypeStruct((rows, width), F32),
            jax.ShapeDtypeStruct((rows, width), BF16),
            jax.ShapeDtypeStruct((1, width), F32),
            jax.ShapeDtypeStruct((8 * rows, 128), BF16),
        ]
        + [jax.ShapeDtypeStruct(shape, BF16) for shape in slices],
        in_specs=[HBM] + [IN_VMEM] * 4 + [HBM] * 2 + [IN_VMEM],
        out_specs=[IN_VMEM] * 6 + [HBM] + [IN_VMEM] * 3,
        scratch_shapes=scratch + semaphores(2 * 7 + 9 + 2 * 17 + 7 + 3 * FSDP_COPIES, 6),
        compiler_params=params(4),
        name="scatter_hidden_block",
    )(ob, wo, tokens, dy_own, gain, gate_up, down, dy)


def keys_kernel(
    branch, h1, gkv, gout, gate, up, gq,
    layer_ref, gkv_out, gout_out, gate_all, up_all, gq_out,
    *scratch,
):
    copies, places = Copies(*scratch[14:]), Places()
    greet(places.gather_peers() + places.strip_peers())
    moved = Strips(copies, places, gq, gq_out)
    sums = [
        FsdpSum(copies, places, gkv, scratch[4:9], 512),
        FsdpSum(copies, places, gout, scratch[9:14], 32),
    ]
    hidden = SeqSum(copies, places, branch, scratch[:4], 64)
    stages = [
        seq_gather(copies, places, gate, gate_all, 0, (0, 32)),
        seq_gather(copies, places, up, up_all, 0, (0, 32)),
    ]
    items = [hidden] + sums
    hidden.ready()
    hidden.send()
    for stage in stages:
        next(stage)
    for item in sums:
        item.ready()
        item.send()
    for item in items:
        item.relay()
    for stage in stages:
        next(stage)
    for item in items:
        item.cross()
    run_stages(stages)
    for item, out in zip(sums, (gkv_out, gout_out)):
        out[...] = item.total().astype(BF16)
    layer_ref[...] = (h1[...] + hidden.total()).astype(BF16)
    moved.wait()
    copies.finish()


def scatter_keys(branch, h1, gkv, gout, gate, up, gq):
    rows, width = h1.shape
    shapes = [a.shape[2:] for a in (gkv, gout)]
    scratch = seq_buffers((rows, width))
    for shape in shapes:
        scratch += fsdp_buffers(shape)
    wide = [jax.ShapeDtypeStruct((8 * a.shape[0],) + a.shape[1:], BF16) for a in (gate, up)]
    return pl.pallas_call(
        keys_kernel,
        out_shape=[jax.ShapeDtypeStruct((rows, width), BF16)]
        + [jax.ShapeDtypeStruct(shape, BF16) for shape in shapes]
        + wide
        + [jax.ShapeDtypeStruct(gq.shape, BF16)],
        in_specs=[HBM, IN_VMEM] + [HBM] * 5,
        out_specs=[IN_VMEM] * 3 + [HBM] * 3,
        scratch_shapes=scratch + semaphores(SEQ_COPIES + 2 * FSDP_COPIES + 18 + 7, 6),
        compiler_params=params(5),
        name="scatter_keys",
    )(branch, h1, gkv, gout, gate, up, gq)


def input_kernel(
    part, tokens, gain, gh1, pack, gout, down,
    grad_ref, pack_all, down_all,
    small, gathered, *scratch,
):
    copies, places = Copies(*scratch[9:]), Places()
    steps = range(1, 8)
    greet(places.gather_peers() + [places.on_seq(places.other_seq(d)) for d in steps])
    hidden = SeqSum(copies, places, part, scratch[:4], 64)
    hidden.ready()
    hidden.send()
    outs = [
        copies.remote(
            gout.at[places.other_seq(d)], gathered.at[d], places.on_seq(places.other_seq(d))
        )
        for d in steps
    ]
    own = copies.here(gout.at[places.seq], gathered.at[0])
    packs = FsdpSum(copies, places, pack, scratch[4:9], 48)
    packs.ready()
    packs.send()
    stages = [seq_gather(copies, places, down, down_all, 0, (0, 16))]
    next(stages[0])
    packs.relay()
    hidden.relay()
    packs.cross()
    next(stages[0])
    hidden.cross()
    own.wait()
    for copy in outs:
        copy.wait_recv()
    rows = pack.shape[2]
    total = gathered[0].astype(F32)
    for d in steps:
        total += gathered[d].astype(F32)
    small[rows:] = total.astype(BF16)
    small[:rows] = packs.total().astype(BF16)
    stages.append(seq_gather(copies, places, small, pack_all, 0, (0, 64)))
    next(stages[1])
    run_stages(stages)
    gn1 = hidden.total()
    value = tokens[...].astype(F32)
    inverse = unit_rows(value)
    normed = value * inverse
    weighted = gn1 * gain[...]
    inner = jnp.mean(weighted * normed, axis=-1, keepdims=True)
    grad_ref[...] = gh1[...] + inverse * (weighted - normed * inner)
    copies.finish()


def scatter_input(part, tokens, gain, gh1, pack, gout, down):
    rows, width = gh1.shape
    shape = pack.shape[2:]
    small = (shape[0] + gout.shape[1], shape[1])
    return pl.pallas_call(
        input_kernel,
        out_shape=[
            jax.ShapeDtypeStruct((rows, width), F32),
            jax.ShapeDtypeStruct((8 * small[0], small[1]), BF16),
            jax.ShapeDtypeStruct((8 * down.shape[0], width), BF16),
        ],
        in_specs=[HBM] + [IN_VMEM] * 3 + [HBM] * 3,
        out_specs=[IN_VMEM] + [HBM] * 2,
        scratch_shapes=[pltpu.VMEM(small, BF16), pltpu.VMEM(gout.shape, BF16)]
        + seq_buffers((rows, width))
        + fsdp_buffers(shape)
        + semaphores(SEQ_COPIES + FSDP_COPIES + 18 + 7, 5),
        compiler_params=params(6),
        name="scatter_input",
    )(part, tokens, gain, gh1, pack, gout, down)


def swap_halves(values):
    lane = lax.broadcasted_iota(jnp.int32, values.shape, 1)
    ahead, behind = pltpu.roll(values, 2 * HD - HD // 2, 1), pltpu.roll(values, HD // 2, 1)
    return jnp.where(lax.rem(lane, HD) < HD // 2, ahead, behind)


def head_means(values):
    low = lanes_low(values.shape)
    first = jnp.sum(jnp.where(low, values, 0.0), axis=1, keepdims=True)
    second = jnp.sum(jnp.where(low, 0.0, values), axis=1, keepdims=True)
    return jnp.where(low, first, second) * (1.0 / HD)


def heads_kernel(x_ref, weight_ref, gain_ref, gains_ref, cos_ref, sin_ref, n1_ref, pre_ref, q_ref, kv_ref):
    def tokens(t, _):
        at = pl.ds(pl.multiple_of(t * 256, 256), 256)
        x = x_ref[at, :].astype(F32)
        n1 = (x * unit_rows(x) * gain_ref[...]).astype(BF16)
        n1_ref[at, :] = n1
        pre = dot_nn(n1, weight_ref[...])
        pre_ref[at, :] = pre
        cosine, sine = cos_ref[at, :], sin_ref[at, :]
        outs = []
        for part in (0, 1):
            values = pre[:, part * 2 * HD : (part + 1) * 2 * HD]
            inverse = lax.rsqrt(head_means(values * values) + EPSILON)
            normed = values * inverse * gains_ref[part : part + 1, :]
            outs.append(normed * cosine + swap_halves(normed) * sine)
        q_ref[at, :] = outs[0].astype(BF16)
        kv_ref[at, :] = jnp.where(lanes_low(outs[1].shape), outs[1], pre[:, 2 * HD :]).astype(BF16)
        return 0

    lax.fori_loop(0, x_ref.shape[0] // 256, tokens, 0)


def project_heads(x, weight, gain, gains, cosine, sine):
    count, width = x.shape
    return pl.pallas_call(
        heads_kernel,
        out_shape=[
            jax.ShapeDtypeStruct((count, width), BF16),
            jax.ShapeDtypeStruct((count, 4 * HD), F32),
            jax.ShapeDtypeStruct((count, 2 * HD), BF16),
            jax.ShapeDtypeStruct((count, 2 * HD), BF16),
        ],
        in_specs=[IN_VMEM] * 6,
        out_specs=[IN_VMEM] * 4,
        compiler_params=pltpu.CompilerParams(vmem_limit_bytes=VMEM),
        name="project_heads",
    )(x, weight, gain, gains, cosine, sine)


def heads_back_kernel(
    x_ref, n1_ref, pre_ref, weight_ref, gains_ref, cos_ref, sin_ref, gq_ref, gkv_ref,
    gn1_ref, gheads_ref, gain_ref, terms_ref, gpre_ref,
):
    count, width = x_ref.shape
    gain_ref[...] = jnp.zeros_like(gain_ref)
    terms_ref[...] = jnp.zeros_like(terms_ref)

    def tokens(t, _):
        at = pl.ds(pl.multiple_of(t * 256, 256), 256)
        cosine, sine = cos_ref[at, :], sin_ref[at, :]
        for part, ref in ((0, gq_ref), (1, gkv_ref)):
            columns = pl.ds(part * 2 * HD, 2 * HD)
            grads = ref[at, :].astype(F32)
            values = pre_ref[at, columns]
            inverse = lax.rsqrt(head_means(values * values) + EPSILON)
            normed = values * inverse
            turned = grads * cosine - swap_halves(grads) * sine
            terms_ref[part : part + 1, :] += jnp.sum(turned * normed, axis=0, keepdims=True)
            weighted = turned * gains_ref[part : part + 1, :]
            back = inverse * (weighted - normed * head_means(weighted * normed))
            if part == 1:
                back = jnp.where(lanes_low(back.shape), back, grads)
            gpre_ref[at, columns] = back.astype(BF16)
        gn1 = dot_nt(gpre_ref[at, :], weight_ref[...])
        gn1_ref[at, :] = gn1.astype(BF16)
        x = x_ref[at, :].astype(F32)
        gain_ref[...] += jnp.sum(gn1 * (x * unit_rows(x)), axis=0, keepdims=True)
        return 0

    lax.fori_loop(0, count // 256, tokens, 0)

    def columns(c, _):
        at = pl.ds(pl.multiple_of(c * 256, 256), 256)
        gheads_ref[at, :] = dot_tn(n1_ref[:, at], gpre_ref[...]).astype(BF16)
        return 0

    lax.fori_loop(0, width // 256, columns, 0)


def heads_back(x, n1, pre, weight, gains, cosine, sine, gq, gkv):
    count, width = x.shape
    return pl.pallas_call(
        heads_back_kernel,
        out_shape=[
            jax.ShapeDtypeStruct((count, width), BF16),
            jax.ShapeDtypeStruct((width, 4 * HD), BF16),
            jax.ShapeDtypeStruct((1, width), F32),
            jax.ShapeDtypeStruct((2, 2 * HD), F32),
        ],
        in_specs=[IN_VMEM] * 9,
        out_specs=[IN_VMEM] * 4,
        scratch_shapes=[pltpu.VMEM((count, 4 * HD), BF16)],
        compiler_params=pltpu.CompilerParams(vmem_limit_bytes=VMEM),
        name="heads_back",
    )(x, n1, pre, weight, gains, cosine, sine, gq, gkv)


def local(
    tokens,
    segments,
    cotangent,
    attention_gain,
    query_gain,
    key_gain,
    query_weight,
    key_weight,
    value_weight,
    out_weight,
    feedforward_gain,
    gate_weight,
    up_weight,
    down_weight,
):
    seq_count = lax.axis_size("seq")
    fsdp_count = lax.axis_size("fsdp")
    fsdp = lax.axis_index("fsdp")
    seq = lax.axis_index("seq")
    rows, width = tokens.shape
    block = rows * seq_count
    hidden = gate_weight.shape[1]
    part = hidden // seq_count
    per_head = (H // KVH) * HD
    block_start = fsdp * block
    take = lax.dynamic_slice_in_dim

    ratio = fsdp_count // seq_count
    pairs = [
        (
            f % seq_count * fsdp_count + ratio * s + f // (fsdp_count // ratio),
            s * fsdp_count + f,
        )
        for f in range(fsdp_count)
        for s in range(seq_count)
    ]
    back_pairs = [(b, a) for a, b in pairs]
    both = ("seq", "fsdp")

    gains = jnp.concatenate([attention_gain, feedforward_gain, query_gain, key_gain])
    heads_weight = jnp.concatenate(
        [
            take(query_weight, seq * per_head, per_head, 1),
            take(key_weight, seq * HD, HD, 1),
            take(value_weight, seq * HD, HD, 1),
        ],
        axis=1,
    )
    gains = jnp.pad(gains[None, :], ((0, 15), (0, heads_weight.shape[1] - gains.shape[0])))
    pieces = down_weight.shape[0] // seq_count
    down_piece = lax.ppermute(take(down_weight, seq * pieces, pieces, 0), both, pairs)
    down_piece = jnp.pad(down_piece, ((0, PIECE - pieces), (0, 0)))
    gate_up = jnp.stack(
        [take(gate_weight, seq * part, part, 1), take(up_weight, seq * part, part, 1)]
    )
    x_block, packs, wo = gather(
        "gather_inputs",
        1,
        [(tokens, 0, (0, 64))],
        [(jnp.concatenate([heads_weight, gains]), 0, (0, 48)), (out_weight, 0, (0, 32))],
    )
    packs = packs.reshape(fsdp_count, -1, packs.shape[1])
    heads_weight = packs[:, : width // fsdp_count].reshape(width, -1)
    gains = packs[:, width // fsdp_count].astype(F32)

    shard = width // fsdp_count
    gain_one = gains[:, :shard].reshape(width)
    gain_two = gains[:, shard : 2 * shard].reshape(width)
    qshard = HD // fsdp_count
    gain_q = gains[:, 2 * shard : 2 * shard + qshard].reshape(HD)
    gain_k = gains[:, 2 * shard + qshard : 2 * shard + 2 * qshard].reshape(HD)

    starts = doc_starts(segments)
    labels = jnp.arange(DOCS, dtype=jnp.int32)

    def firsts(ids):
        picked = (ids[:, None] == labels[None, :]).astype(jnp.int32)
        return jnp.sum(picked * starts[None, :], axis=1)

    index = block_start + jnp.arange(block, dtype=jnp.int32)
    positions = index - firsts(take(segments, block_start, block))
    freqs = THETA ** (-2.0 * jnp.arange(HD // 2, dtype=F32) / HD)
    angles = positions.astype(F32)[:, None] * jnp.tile(freqs, 4)[None, :]
    side = jnp.tile(jnp.repeat(jnp.array([-1.0, 1.0], F32), HD // 2), 2)
    cosine, sine = jnp.cos(angles), jnp.sin(angles) * side[None, :]
    head_gains = jnp.stack([jnp.tile(gain_q, 2), jnp.tile(gain_k, 2)])
    shift = (HD**0.5 * LOG2E) * jnp.max(jnp.abs(gain_q)) * jnp.max(jnp.abs(gain_k))
    shift = shift.reshape(1)

    core, chip = fsdp % 2, fsdp // 2
    strip_ids = segments.reshape(fsdp_count // 2, 2, block // STRIP, STRIP)
    strip_ids = lax.dynamic_index_in_dim(strip_ids, core, 1, keepdims=False)
    strip_ids = lax.dynamic_index_in_dim(strip_ids, chip, 1, keepdims=False)
    first = firsts(strip_ids.reshape(-1))
    strip_first = first.reshape(-1, STRIP)
    q_first = (2 * jnp.arange(fsdp_count // 2, dtype=jnp.int32) + core) * block + chip * STRIP
    low = strip_first[:, 0] // KEYS
    high = (q_first + STRIP - 1) // KEYS + 1
    inner_low = jnp.minimum((strip_first[:, STRIP - 1] + KEYS - 1) // KEYS, high)
    inner_high = jnp.maximum((q_first + 1) // KEYS, inner_low)
    ranges = jnp.stack([low, inner_low, inner_high, high, q_first])

    n1, pre, q, kv = project_heads(
        x_block, heads_weight, gain_one[None, :], head_gains, cosine, sine
    )
    dy_block, kv, q = gather(
        "gather_keys",
        2,
        [(cotangent, 0, (0, 64))],
        [(kv, 0, (0, 512))],
        [q],
    )

    ob, o, totals = forward_attention(ranges, shift, q, first[:, None], kv)
    ob_own, h1_own, branch, gh1, gb, gain_two_term, go, g_gate, g_up, g_down = hidden_block(
        ob, wo, tokens, cotangent, gain_two[None, :], gate_up, down_piece, dy_block
    )
    by_core = lambda array: array.reshape(8, 2, -1, array.shape[-1])
    g_down = lax.ppermute(g_down, both, back_pairs)
    g_out = dot_tn(ob_own, gb).astype(BF16)
    gq, gkv = backward_attention(
        ranges, shift, q, go, o, totals, strip_first[:, None, :], kv
    )
    layer_out, gkv, g_out, g_gate, g_up, gq = scatter_keys(
        branch.reshape(seq_count, rows, width),
        h1_own,
        by_core(gkv),
        by_core(g_out),
        g_gate,
        g_up,
        gq,
    )
    gn1_partial, g_heads, gain_one_term, head_terms = heads_back(
        x_block, n1, pre, heads_weight, head_gains, cosine, sine, gq, gkv
    )
    gain_q_term = head_terms[0, :HD] + head_terms[0, HD:]
    gain_k_term = head_terms[1, :HD]
    g_heads = g_heads.reshape(fsdp_count, shard, -1)
    terms = jnp.concatenate(
        [
            gain_one_term.reshape(fsdp_count, shard),
            gain_two_term.reshape(fsdp_count, shard),
            gain_q_term.reshape(fsdp_count, qshard),
            gain_k_term.reshape(fsdp_count, qshard),
        ],
        axis=1,
    ).astype(BF16)
    terms = jnp.pad(terms[:, None, :], ((0, 0), (0, 15), (0, g_heads.shape[2] - terms.shape[1])))
    pack = jnp.concatenate([g_heads, terms], axis=1)
    input_grad, packs, g_down = scatter_input(
        gn1_partial.reshape(seq_count, rows, width),
        tokens,
        gain_one[None, :],
        gh1,
        pack.reshape((8, 2) + pack.shape[1:]),
        g_out.reshape(seq_count, -1, pack.shape[2]),
        g_down,
    )
    packs = packs.reshape(seq_count, -1, pack.shape[2])
    g_heads = packs[:, :shard]
    terms = jnp.sum(packs[:, shard].astype(F32), axis=0)
    g_out = packs[:, pack.shape[1] :].astype(F32).reshape(shard, width)
    g_down = g_down.reshape(seq_count, PIECE, width)[:, :pieces].reshape(-1, width)
    columns = lambda a: jnp.transpose(a.reshape(seq_count, shard, part), (1, 0, 2)).reshape(shard, hidden)

    g_query = jnp.transpose(g_heads[:, :, :per_head], (1, 0, 2)).reshape(shard, H * HD)
    g_key = jnp.transpose(g_heads[:, :, per_head : per_head + HD], (1, 0, 2)).reshape(shard, KVH * HD)
    g_value = jnp.transpose(g_heads[:, :, per_head + HD :], (1, 0, 2)).reshape(shard, KVH * HD)

    return (
        layer_out,
        input_grad,
        terms[:shard],
        terms[2 * shard : 2 * shard + qshard],
        terms[2 * shard + qshard : 2 * shard + 2 * qshard],
        g_query.astype(F32),
        g_key.astype(F32),
        g_value.astype(F32),
        g_out,
        terms[shard : 2 * shard],
        columns(g_gate).astype(F32),
        columns(g_up).astype(F32),
        g_down.astype(F32),
    )


def solution(mesh):
    rows = P(("fsdp", "seq"), None)
    matrix = P("fsdp", None)
    vector = P("fsdp")
    in_specs = (rows, P(), rows) + (vector,) * 3 + (matrix,) * 4 + (vector,) + (matrix,) * 3
    out_specs = (rows, rows) + (vector,) * 3 + (matrix,) * 4 + (vector,) + (matrix,) * 3
    return jax.shard_map(local, mesh=mesh, in_specs=in_specs, out_specs=out_specs, check_vma=False)
```

```python
import functools
import math

import jax
import jax.numpy as jnp
from jax import lax
from jax.experimental import pallas as pl
from jax.experimental.pallas import tpu as pltpu
from jax.sharding import PartitionSpec as P

H = 16
KVH = 8
HD = 64
DOCS = 4
EPSILON = 1e-06
THETA = 1000000.0
LOG2E = math.log2(math.e)
F32 = jnp.float32
BF16 = jnp.bfloat16
STRIP = 128
FEED = 256
KEYS = 1024
VMEM = 56 * 1024 * 1024
PIECE = 48


def doc_starts(segments):
    labels = jnp.arange(DOCS, dtype=jnp.int32)
    member = (segments[None, :] == labels[:, None]).astype(jnp.int32)
    lengths = jnp.sum(member, axis=1)
    return jnp.cumsum(lengths) - lengths


def dot_nt(a, b):
    return lax.dot_general(a, b, (((1,), (1,)), ((), ())), preferred_element_type=F32)


def dot_tn(a, b):
    return lax.dot_general(a, b, (((0,), (0,)), ((), ())), preferred_element_type=F32)


def dot_nn(a, b):
    return jnp.dot(a, b, preferred_element_type=F32)


def key_loops(ranges_ref, tile, step):
    low, inner_low, inner_high, high = [ranges_ref[i, tile] for i in range(4)]

    def masked(block, _):
        step(block, True)
        return 0

    def plain(block, _):
        step(block, False)
        return 0

    lax.fori_loop(low, inner_low, masked, 0)
    lax.fori_loop(inner_low, inner_high, plain, 0)
    lax.fori_loop(inner_high, high, masked, 0)


def lanes_low(shape):
    return lax.broadcasted_iota(jnp.int32, shape, 1) < HD


def two_heads(packed, low):
    other = pltpu.roll(packed, HD, 1)
    heads = (packed, other) if low else (other, packed)
    keep = lanes_low(packed.shape) if low else ~lanes_low(packed.shape)
    return jnp.concatenate([jnp.where(keep, head, 0.0) for head in heads], axis=0)


def one_row(heads, low):
    rows = heads.shape[0] // 2
    first, second = heads[:rows], heads[rows:]
    if low:
        second = pltpu.roll(second, HD, 1)
    else:
        first = pltpu.roll(first, HD, 1)
    return jnp.where(lanes_low(first.shape), first, second)


def forward_kernel(
    ranges_ref, shift_ref, query_ref, first_ref, kv_ref, ob_ref, o_ref, totals_ref, total
):
    tile = pl.program_id(0)
    rows = query_ref.shape[0]
    query = two_heads(query_ref[...].astype(F32) * HD**-0.5, True).astype(BF16)
    first = jnp.concatenate([first_ref[...]] * 2, axis=0)
    index = ranges_ref[4, tile] + lax.broadcasted_iota(jnp.int32, (rows, 1), 0)
    index = jnp.concatenate([index, index], axis=0)
    shift = shift_ref[0]
    ones = jnp.ones((KEYS, 2 * HD), BF16)
    total[...] = jnp.zeros_like(total)

    def step(block, masked):
        start = pl.multiple_of(block * KEYS, KEYS)
        kv = kv_ref[pl.ds(start, KEYS), :]
        exps = jnp.exp2(dot_nt(query, kv) * LOG2E - shift)
        if masked:
            keys = start + lax.broadcasted_iota(jnp.int32, (2 * rows, KEYS), 1)
            exps = jnp.where((keys >= first) & (keys <= index), exps, 0.0)
        total[...] += dot_nn(exps.astype(BF16), jnp.concatenate([kv, ones], axis=1))

    key_loops(ranges_ref, tile, step)
    totals = total[:, 2 * HD :]
    o = total[:, : 2 * HD] / totals
    o_ref[0] = o
    totals_ref[0] = totals
    ob_ref[...] = one_row(o, False).astype(BF16)


def forward_attention(ranges, shift, query, first, kv):
    tiles = query.shape[0] // STRIP
    whole = lambda t, *_: (0, 0)
    part = lambda t, *_: (t, 0)
    wide = lambda t, *_: (t, 0, 0)
    return pl.pallas_call(
        forward_kernel,
        grid_spec=pltpu.PrefetchScalarGridSpec(
            num_scalar_prefetch=2,
            grid=(tiles,),
            in_specs=[
                pl.BlockSpec((STRIP, 2 * HD), part),
                pl.BlockSpec((STRIP, 1), part),
                pl.BlockSpec(kv.shape, whole),
            ],
            out_specs=[
                pl.BlockSpec((STRIP, 2 * HD), part),
                pl.BlockSpec((1, 2 * STRIP, 2 * HD), wide),
                pl.BlockSpec((1, 2 * STRIP, 2 * HD), wide),
            ],
            scratch_shapes=[pltpu.VMEM((2 * STRIP, 4 * HD), F32)],
        ),
        out_shape=[
            jax.ShapeDtypeStruct(query.shape, BF16),
            jax.ShapeDtypeStruct((tiles, 2 * STRIP, 2 * HD), F32),
            jax.ShapeDtypeStruct((tiles, 2 * STRIP, 2 * HD), F32),
        ],
        compiler_params=pltpu.CompilerParams(vmem_limit_bytes=VMEM),
        cost_estimate=pl.CostEstimate(
            flops=8 * 10**9, bytes_accessed=8 * 10**6, transcendentals=16 * 10**6
        ),
        name="attention_forward",
    )(ranges, shift, query, first, kv)


def backward_kernel(
    ranges_ref, shift_ref, query_ref, grad_ref, o_ref, totals_ref, first_ref, kv_ref,
    gq_ref, gkv_ref, total, gq,
):
    tile = pl.program_id(0)
    rows = query_ref.shape[0]
    query = two_heads(query_ref[...].astype(F32) * HD**-0.5, True).astype(BF16)
    go = two_heads(grad_ref[...].astype(F32), False)
    totals = totals_ref[0]
    grad = (go / totals).astype(BF16)
    delta = jnp.sum(go * o_ref[0], axis=1, keepdims=True) / totals
    delta = jnp.transpose(delta)[:1]
    both = jnp.concatenate([query, grad], axis=0)
    first = jnp.concatenate([first_ref[0]] * 2, axis=1)
    index = ranges_ref[4, tile] + lax.broadcasted_iota(jnp.int32, (1, rows), 1)
    index = jnp.concatenate([index, index], axis=1)
    shift = shift_ref[0]

    @pl.when(tile == 0)
    def _():
        total[...] = jnp.zeros_like(total)

    gq[...] = jnp.zeros_like(gq)

    def step(block, masked):
        start = pl.multiple_of(block * KEYS, KEYS)
        kv = kv_ref[pl.ds(start, KEYS), :]
        exps = jnp.exp2(dot_nt(kv, query) * LOG2E - shift)
        if masked:
            keys = start + lax.broadcasted_iota(jnp.int32, (KEYS, 2 * rows), 0)
            exps = jnp.where((keys >= first) & (keys <= index), exps, 0.0)
        scores = (exps * (dot_nt(kv, grad) - delta)).astype(BF16)
        gq[...] += dot_tn(scores, kv)
        total[pl.ds(start, KEYS), :] += dot_nn(
            jnp.concatenate([scores, exps.astype(BF16)], axis=1), both
        )

    key_loops(ranges_ref, tile, step)
    gq_ref[...] = (one_row(gq[...], True) * HD**-0.5).astype(BF16)

    @pl.when(tile == pl.num_programs(0) - 1)
    def _():
        gkv_ref[...] = total[...].astype(BF16)


def backward_attention(ranges, shift, query, grad, o, totals, first, kv):
    tiles = query.shape[0] // STRIP
    whole = lambda t, *_: (0, 0)
    part = lambda t, *_: (t, 0)
    wide = lambda t, *_: (t, 0, 0)
    return pl.pallas_call(
        backward_kernel,
        grid_spec=pltpu.PrefetchScalarGridSpec(
            num_scalar_prefetch=2,
            grid=(tiles,),
            in_specs=[
                pl.BlockSpec((STRIP, 2 * HD), part),
                pl.BlockSpec((STRIP, 2 * HD), part),
                pl.BlockSpec((1, 2 * STRIP, 2 * HD), wide),
                pl.BlockSpec((1, 2 * STRIP, 2 * HD), wide),
                pl.BlockSpec((1, 1, STRIP), wide),
                pl.BlockSpec(kv.shape, whole),
            ],
            out_specs=[
                pl.BlockSpec((STRIP, 2 * HD), part),
                pl.BlockSpec(kv.shape, whole),
            ],
            scratch_shapes=[pltpu.VMEM(kv.shape, F32), pltpu.VMEM((2 * STRIP, 2 * HD), F32)],
        ),
        out_shape=[
            jax.ShapeDtypeStruct(query.shape, BF16),
            jax.ShapeDtypeStruct(kv.shape, BF16),
        ],
        compiler_params=pltpu.CompilerParams(vmem_limit_bytes=VMEM),
        cost_estimate=pl.CostEstimate(
            flops=20 * 10**9, bytes_accessed=16 * 10**6, transcendentals=16 * 10**6
        ),
        name="attention_backward",
    )(ranges, shift, query, grad, o, totals, first, kv)


MESH = pl.DeviceIdType.MESH
HBM = pl.BlockSpec(memory_space=pl.ANY)
IN_VMEM = pl.BlockSpec(memory_space=pltpu.VMEM)
RING = 8


def pair_of(value):
    return value + 1 - 2 * lax.rem(value, 2)


def ring_step(index, steps):
    return lax.div(index, RING) * RING + lax.rem(lax.rem(index, RING) + 2 * steps, RING)


class Copies:
    def __init__(self, send, recv, local):
        self.send, self.recv, self.local = send, recv, local
        self.started, self.locals = [], []

    def remote(self, src, dst, peer, recv=None):
        i = len(self.started)
        copy = pltpu.make_async_remote_copy(
            src_ref=src,
            dst_ref=dst,
            send_sem=self.send.at[i],
            recv_sem=self.recv.at[i] if recv is None else recv,
            device_id=peer,
            device_id_type=MESH,
        )
        copy.start()
        self.started.append(copy)
        return copy

    def here(self, src, dst):
        copy = pltpu.make_async_copy(src, dst, self.local.at[len(self.locals)])
        copy.start()
        self.locals.append(copy)
        return copy

    def finish(self):
        for copy in self.started:
            copy.wait_send()


def greet(peers):
    barrier = pltpu.get_barrier_semaphore()
    for peer in peers:
        pl.semaphore_signal(barrier, inc=1, device_id=peer, device_id_type=MESH)
    pl.semaphore_wait(barrier, len(peers))


def slot(ref, axis, size, index, split=None, half=0):
    start = index * size
    where = [pl.ds(0, n) for n in ref.shape]
    where[axis] = pl.ds(pl.multiple_of(start, 16), size)
    if split is not None:
        along, cut = split
        whole = size if along == axis else ref.shape[along]
        base = start if along == axis else 0
        begin, count = (0, cut) if half == 0 else (cut, whole - cut)
        offset = base + begin
        where[along] = pl.ds(pl.multiple_of(offset, 16) if along == axis else offset, count)
    return ref.at[tuple(where)]


def gather_stages(copies, src, out, axis, size, split, me, pair, device, sibling):
    plus, minus = ring_step(me, 1), ring_step(me, 3)
    at = functools.partial(slot, out, axis, size)
    halves = lambda index, half: at(index, split, half)
    to_sibling = []

    def pass_on(index):
        if sibling is not None:
            to_sibling.append(copies.remote(at(index), at(index), device(sibling)))

    kept = copies.here(src, at(me))
    first = copies.remote(src, at(me), device(pair))
    up = copies.remote(src, at(me), device(plus))
    down = copies.remote(src, at(me), device(minus))
    if sibling is not None:
        to_sibling.append(copies.remote(src, at(me), device(sibling)))
    yield
    up.wait_recv()
    far = [copies.remote(halves(minus, 0), halves(minus, 0), device(plus))]
    pass_on(minus)
    down.wait_recv()
    far.append(copies.remote(halves(plus, 1), halves(plus, 1), device(minus)))
    pass_on(plus)
    yield
    first.wait_recv()
    up = copies.remote(at(pair), at(pair), device(plus))
    down = copies.remote(at(pair), at(pair), device(minus))
    pass_on(pair)
    yield
    shift = pair - me
    up.wait_recv()
    last = [copies.remote(halves(minus + shift, 0), halves(minus + shift, 0), device(plus))]
    pass_on(minus + shift)
    down.wait_recv()
    last.append(copies.remote(halves(plus + shift, 1), halves(plus + shift, 1), device(minus)))
    pass_on(plus + shift)
    yield
    opposite = ring_step(me, 2)
    for copy in far:
        copy.wait_recv()
    pass_on(opposite)
    yield
    for copy in last:
        copy.wait_recv()
    pass_on(opposite + shift)
    yield
    for copy in to_sibling:
        copy.wait_recv()
    kept.wait()


def run_stages(stages):
    live = list(stages)
    while live:
        live = [stage for stage in live if next(stage, stage) is not stage]


class Swap:
    def __init__(self, copies, recv, sem, tag, stays, sends):
        self.copies, self.recv, self.tag, self.stays = copies, recv, tag, stays
        (src, dst, peer), rest = sends[0], sends[1:]
        self.own = pltpu.make_async_remote_copy(
            src_ref=src,
            dst_ref=dst,
            send_sem=sem.at[0],
            recv_sem=recv.at[tag],
            device_id=peer,
            device_id_type=MESH,
        )
        self.kept = pltpu.make_async_copy(src, dst, sem.at[1])

        @pl.when(stays)
        def _():
            self.kept.start()

        @pl.when(jnp.logical_not(stays))
        def _():
            self.own.start()

        self.sample = (src, dst, peer, sem)
        for src, dst, peer in rest:
            copies.remote(src, dst, peer, recv.at[tag])

    def wait(self, landing):
        src, _, peer, sem = self.sample
        for step in range(1, 8):
            sender = lax.rem(self.tag + step, 8)
            pltpu.make_async_remote_copy(
                src_ref=src,
                dst_ref=landing(sender),
                send_sem=sem.at[0],
                recv_sem=self.recv.at[sender],
                device_id=peer,
                device_id_type=MESH,
            ).wait_recv()

        @pl.when(self.stays)
        def _():
            self.kept.wait()

        @pl.when(jnp.logical_not(self.stays))
        def _():
            self.own.wait()


def greet_for_swaps(places, peers):
    barrier = pltpu.get_barrier_semaphore()
    senders, others = places.heads()[1], places.owners()[1]
    peers = peers + senders[1:] + others[1:]
    for peer in peers:
        pl.semaphore_signal(barrier, inc=1, device_id=peer, device_id_type=MESH)

    @pl.when(places.stays)
    def _():
        pl.semaphore_wait(barrier, len(peers))

    @pl.when(jnp.logical_not(places.stays))
    def _():
        for peer in (senders[0], others[0]):
            pl.semaphore_signal(barrier, inc=1, device_id=peer, device_id_type=MESH)
        pl.semaphore_wait(barrier, len(peers) + 2)


class Move:
    def __init__(self, src, dst, peer, stays, sem):
        self.stays = stays
        self.own = pltpu.make_async_remote_copy(
            src_ref=src,
            dst_ref=dst,
            send_sem=sem.at[0],
            recv_sem=sem.at[1],
            device_id=peer,
            device_id_type=MESH,
        )
        self.kept = pltpu.make_async_copy(src, dst, sem.at[2])

        @pl.when(stays)
        def _():
            self.kept.start()

        @pl.when(jnp.logical_not(stays))
        def _():
            self.own.start()

    def wait(self):
        @pl.when(self.stays)
        def _():
            self.kept.wait()

        @pl.when(jnp.logical_not(self.stays))
        def _():
            self.own.wait()


def greet_for_move(places, peers, sender):
    barrier = pltpu.get_barrier_semaphore()
    for peer in peers:
        pl.semaphore_signal(barrier, inc=1, device_id=peer, device_id_type=MESH)

    @pl.when(places.fixed)
    def _():
        pl.semaphore_wait(barrier, len(peers))

    @pl.when(jnp.logical_not(places.fixed))
    def _():
        pl.semaphore_signal(barrier, inc=1, device_id=sender, device_id_type=MESH)
        pl.semaphore_wait(barrier, len(peers) + 1)


def strips_at(ref, index):
    return ref.at[pl.ds(pl.multiple_of(index * STRIP, STRIP), STRIP), :]


def heads_at(ref, index):
    return ref.at[:, pl.ds(pl.multiple_of(index * 2 * HD, 2 * HD), 2 * HD)]


class Places:
    def __init__(self):
        self.seq, self.fsdp = lax.axis_index("seq"), lax.axis_index("fsdp")
        self.core = lax.rem(self.fsdp, 2)
        self.chip = lax.div(self.fsdp, 2)
        self.row = lax.div(self.chip, 4)
        self.col = lax.rem(self.chip, 4)
        self.sibling = pair_of(self.fsdp)
        self.across = lax.rem(self.fsdp + 8, 16)
        self.stays = self.chip == self.seq
        self.piece_to = (self.chip, self.core * 8 + self.seq)
        self.piece_from = (lax.rem(self.fsdp, 8), 2 * self.seq + lax.div(self.fsdp, 8))
        self.fixed = (self.chip == self.seq) & (self.core * 8 + self.seq == self.fsdp)

    def on_seq(self, index):
        return (index, self.fsdp)

    def on_fsdp(self, index):
        return (self.seq, index)

    def other_seq(self, step):
        return lax.rem(self.seq + step, 8)

    def other_chip(self, step):
        return lax.rem(self.row + step // 4, 2) * 4 + lax.rem(self.col + step % 4, 4)

    def gather_peers(self):
        seq = [pair_of(self.seq), ring_step(self.seq, 1), ring_step(self.seq, 3)]
        fsdp = [self.across, ring_step(self.fsdp, 1), ring_step(self.fsdp, 3), self.sibling]
        return [self.on_seq(i) for i in seq] + [self.on_fsdp(i) for i in fsdp]

    def strip_peers(self):
        return [self.on_fsdp(self.other_chip(d) * 2 + self.core) for d in range(1, 8)]

    def owners(self):
        strips = [lax.rem(self.chip + d, 8) for d in range(8)]
        return strips, [(self.chip, strip * 2 + self.core) for strip in strips]

    def heads(self):
        heads = [lax.rem(self.seq + d, 8) for d in range(8)]
        return heads, [(head, self.seq * 2 + self.core) for head in heads]


def params(name_id):
    return pltpu.CompilerParams(
        collective_id=name_id, has_side_effects=True, vmem_limit_bytes=VMEM
    )


def semaphores(remote, local):
    return [
        pltpu.SemaphoreType.DMA((remote,)),
        pltpu.SemaphoreType.DMA((remote,)),
        pltpu.SemaphoreType.DMA((local,)),
    ]


def seq_gather(copies, places, src, out, axis, split):
    size = src.shape[axis]
    return gather_stages(
        copies, src, out, axis, size, split, places.seq, pair_of(places.seq), places.on_seq, None
    )


def fsdp_gather(copies, places, src, out, axis, split):
    size = src.shape[axis]
    return gather_stages(
        copies, src, out, axis, size, split, places.fsdp, places.across, places.on_fsdp, places.sibling
    )


class Strips:
    def __init__(self, copies, places, src, out):
        self.kept = copies.here(strips_at(src, places.chip), strips_at(out, places.chip))
        self.copies = []
        for d in range(1, 8):
            chip = places.other_chip(d)
            peer = places.on_fsdp(chip * 2 + places.core)
            self.copies.append(copies.remote(strips_at(src, chip), strips_at(out, places.chip), peer))

    def wait(self):
        for copy in self.copies:
            copy.wait_recv()
        self.kept.wait()


def gather(name, name_id, seq_items, fsdp_items, strips=(), pieces=None):
    items = seq_items + fsdp_items
    count = len(items)
    every = count + len(strips)
    sources = [item[0] for item in items] + list(strips) + ([] if pieces is None else [pieces])

    def kernel(*refs):
        total = len(sources)
        srcs, outs, rest = refs[:total], refs[total : 2 * total], refs[2 * total :]
        copies, places = Copies(*rest[:3]), Places()
        peers = places.gather_peers() + (places.strip_peers() if strips else [])
        if pieces is None:
            greet(peers)
        else:
            greet_for_move(places, peers, places.piece_from)
        stages = []
        order = list(range(count))
        for i in order[::-1] if strips else order:
            _, axis, split = items[i]
            make = seq_gather if i < len(seq_items) else fsdp_gather
            stages.append(make(copies, places, srcs[i], outs[i], axis, split))
            next(stages[-1])
        moved = [Strips(copies, places, srcs[i], outs[i]) for i in range(count, every)]
        if pieces is not None:
            at = pl.ds(pl.multiple_of(places.seq * PIECE, 16), PIECE)
            moved.append(Move(srcs[-1].at[at], outs[-1], places.piece_to, places.fixed, rest[3]))
        run_stages(stages)
        for item in moved:
            item.wait()
        copies.finish()

    shapes = []
    for i, (array, axis, _) in enumerate(items):
        shape = list(array.shape)
        shape[axis] *= 8 if i < len(seq_items) else 16
        shapes.append(jax.ShapeDtypeStruct(tuple(shape), array.dtype))
    shapes += [jax.ShapeDtypeStruct(array.shape, array.dtype) for array in strips]
    extra = []
    if pieces is not None:
        shapes.append(jax.ShapeDtypeStruct((PIECE,) + pieces.shape[1:], pieces.dtype))
        extra = [pltpu.SemaphoreType.DMA((3,))]
    remote = 9 * len(seq_items) + 17 * len(fsdp_items) + 7 * len(strips)
    return pl.pallas_call(
        kernel,
        out_shape=shapes,
        in_specs=[HBM] * len(sources),
        out_specs=[HBM] * len(sources),
        scratch_shapes=semaphores(remote, every) + extra,
        compiler_params=params(name_id),
        name=name,
    )(*sources)


class RingSum:
    def __init__(self, copies, near, mine, held, cut, index, device):
        self.remote, self.mine, self.device = copies.remote, mine, device
        self.half, self.ring, self.other = held
        self.cut, self.index = cut, index
        self.plus, self.minus, self.pair = near

    def parts(self):
        rows = self.mine.shape[1]
        return pl.ds(0, self.cut), pl.ds(self.cut, rows - self.cut)

    def send(self):
        low, high = self.parts()
        self.first, self.second = [], []
        for flip in (1, 0):
            far, up, down = [self.mine.at[self.index(flip, step)] for step in (2, 1, 3)]
            self.first.append(
                (
                    self.remote(far.at[low], self.half.at[flip, low], self.plus),
                    self.remote(far.at[high], self.half.at[flip, high], self.minus),
                )
            )
            self.second.append(
                [
                    self.remote(up.at[high], self.ring.at[flip, 0, high], self.plus),
                    self.remote(down.at[low], self.ring.at[flip, 1, low], self.minus),
                ]
            )

    def relay(self):
        low, high = self.parts()
        for i, flip in enumerate((1, 0)):
            for copy, step, part, way, peer in (
                (self.first[i][0], 1, low, 0, self.plus),
                (self.first[i][1], 3, high, 1, self.minus),
            ):
                copy.wait_recv()
                at = self.index(flip, step)
                self.mine[at, part] = (
                    self.mine[at, part].astype(F32) + self.half[flip, part].astype(F32)
                ).astype(BF16)
                self.second[i].append(
                    self.remote(self.mine.at[at, part], self.ring.at[flip, way, part], peer)
                )

    def gathered(self, i, flip):
        for copy in self.second[i]:
            copy.wait_recv()
        return (
            self.mine[self.index(flip, 0)].astype(F32)
            + self.ring[flip, 0].astype(F32)
            + self.ring[flip, 1].astype(F32)
        )

    def cross(self):
        self.other[0] = self.gathered(0, 1).astype(BF16)
        self.last = self.remote(self.other.at[0], self.other.at[1], self.pair)

    def total(self):
        total = self.gathered(1, 0)
        self.last.wait_recv()
        return total + self.other[1].astype(F32)


def ring_buffers(shape):
    return [
        pltpu.VMEM((2,) + shape, BF16),
        pltpu.VMEM((2, 2) + shape, BF16),
        pltpu.VMEM((2,) + shape, BF16),
    ]


RING_COPIES = 13


class SeqSum(RingSum):
    def __init__(self, copies, places, part, buffers, cut):
        mine, held = buffers[0], buffers[1:]
        seq = places.seq

        def index(flip, step):
            base = ring_step(seq, step)
            return pair_of(base) if flip else base

        near = [places.on_seq(i) for i in (ring_step(seq, 1), ring_step(seq, 3), pair_of(seq))]
        super().__init__(copies, near, mine, held, cut, index, places.on_seq)
        self.kept = copies.here(part, mine)

    def ready(self):
        self.kept.wait()


class FsdpSum(RingSum):
    def __init__(self, copies, places, part, buffers, cut):
        mine, self.theirs, held = buffers[0], buffers[1], buffers[2:]
        fsdp = places.fsdp

        def index(flip, step):
            return lax.rem(places.row + flip, 2) * 4 + lax.rem(places.col + step, 4)

        near = [places.on_fsdp(i) for i in (ring_step(fsdp, 1), ring_step(fsdp, 3), places.across)]
        super().__init__(copies, near, mine, held, cut, index, places.on_fsdp)
        self.order = [index(flip, step) for flip in (1, 0) for step in (2, 1, 3, 0)]
        self.others = [
            copies.remote(
                part.at[at, 1 - places.core], self.theirs.at[at], places.on_fsdp(places.sibling)
            )
            for at in self.order
        ]
        self.kept = copies.here(part.at[:, places.core], mine)

    def ready(self):
        self.kept.wait()
        for at, copy in zip(self.order, self.others):
            copy.wait_recv()
            self.mine[at] = (self.mine[at].astype(F32) + self.theirs[at].astype(F32)).astype(BF16)


def seq_buffers(shape):
    return [pltpu.VMEM((8,) + shape, BF16)] + ring_buffers(shape)


def fsdp_buffers(shape):
    return [pltpu.VMEM((8,) + shape, BF16)] * 2 + ring_buffers(shape)


SEQ_COPIES = RING_COPIES
FSDP_COPIES = RING_COPIES + 8


def unit_rows(values):
    return lax.rsqrt(jnp.mean(values * values, axis=-1, keepdims=True) + EPSILON)


def spread(pieces, part):
    shape = (pieces * PIECE, part)
    row = lax.broadcasted_iota(jnp.int32, shape, 0)
    column = lax.broadcasted_iota(jnp.int32, shape, 1)
    size = part // pieces
    inside = lax.rem(row, PIECE)
    hit = (lax.div(row, PIECE) * size + inside == column) & (inside < size)
    return jnp.where(hit, 1.0, 0.0).astype(BF16)


def hidden_kernel(
    ob, wo, tokens, dy_own, gain, gate_up, down, dy,
    own_ref, h1_ref, branch_ref, gh1_ref, gb_ref, term_ref, go_ref, gate_out, up_out, down_out,
    own, n2, go_own, n2_all, weights, down_pad, down_all, act, ggate, gup, gn2_all, held,
    gate_part, up_part, down_part, *scratch,
):
    sums_at = scratch[:15]
    tags, ends, tags_back, ends_back = scratch[15:19]
    copies, places = Copies(*scratch[19:]), Places()
    others = [places.on_seq(places.other_seq(d)) for d in range(1, 8)]
    greet_for_swaps(places, places.gather_peers() + others)
    rows, width = own.shape
    part = down_all.shape[0]
    pieces = down_pad.shape[0] // PIECE

    strips, owners = places.owners()
    heads, workers = places.heads()
    landing = heads_at(own, places.seq)
    sends = [(strips_at(ob, strip), landing, peer) for strip, peer in zip(strips, owners)]
    swap = Swap(copies, tags, ends, places.seq, places.stays, sends)
    gathers = [
        fsdp_gather(copies, places, gate_up, weights, 1, (1, 32)),
        fsdp_gather(copies, places, down, down_pad, 0, (0, 32)),
    ]
    for stage in gathers:
        next(stage)
    swap.wait(lambda sender: heads_at(own, sender))
    own_ref[...] = own[...]

    def project(j, _):
        at = pl.ds(pl.multiple_of(j * 256, 256), 256)
        h1_ref[:, at] = tokens[:, at].astype(F32) + dot_nn(own[...], wo[:, at])
        return 0

    lax.fori_loop(0, width // 256, project, 0)
    value = h1_ref[...]
    inverse = unit_rows(value)
    n2[...] = (value * inverse * gain[...]).astype(BF16)
    tokens_in = seq_gather(copies, places, n2, n2_all, 0, (0, 64))
    next(tokens_in)
    for _ in range(3):
        for stage in gathers:
            next(stage)
        if _ < 2:
            next(tokens_in)
    run_stages(gathers)
    matrix = spread(pieces, part)

    def pack_down(j, _):
        at = pl.ds(pl.multiple_of(j * 256, 256), 256)
        down_all[:, at] = dot_tn(matrix, down_pad[:, at]).astype(BF16)
        return 0

    lax.fori_loop(0, width // 256, pack_down, 0)

    arrivals = []

    def feed(step):
        base = lax.div(ring_step(places.seq, step), 2) * 2 * rows
        at = pl.ds(pl.multiple_of(base, 2 * rows), 2 * rows)
        values = n2_all[at, :]
        gate = dot_nn(values, weights[0])
        up = dot_nn(values, weights[1])
        gact = dot_nt(dy[at, :], down_all[...])
        sig = jax.nn.sigmoid(gate)
        silu = gate * sig
        act_here = (silu * up).astype(BF16)
        gg = (gact * up * sig * (1.0 + gate * (1.0 - sig))).astype(BF16)
        gu = (gact * silu).astype(BF16)
        act[at, :] = act_here
        ggate[at, :] = gg
        gup[at, :] = gu
        gn2_all[at, :] = (dot_nt(gg, weights[0]) + dot_nt(gu, weights[1])).astype(BF16)
        for flip in (1, 0):
            if step == 0 and flip == 0:
                continue
            peer = ring_step(places.seq, step)
            peer = pair_of(peer) if flip else peer
            arrivals.append(
                copies.remote(
                    gn2_all.at[pl.ds(pl.multiple_of(peer * rows, rows), rows), :],
                    held.at[2 * step + flip],
                    places.on_seq(peer),
                )
            )
        branch_ref[at, :] = dot_nn(act_here, down_all[...]).astype(BF16)

    tokens_in.send(None)
    kept_first = copies.locals[-1]
    kept_first.wait()
    feed(0)
    feed(1)
    feed(3)
    next(tokens_in)
    next(tokens_in)
    feed(2)

    sums = []

    def weight_sum(c, part_ref, grads):
        at = pl.ds(pl.multiple_of(c * 256, 256), 256)
        shape = (2, 2) + part_ref.shape[2:]
        part_ref[pl.ds(c * 2, 2)] = dot_tn(n2_all[:, at], grads[...]).astype(BF16).reshape(shape)
        return 0

    def down_sum(c, _):
        at = pl.ds(pl.multiple_of(c * 256, 256), 256)
        g_down = dot_nn(matrix, dot_tn(act[...], dy[:, at]).astype(BF16)).astype(BF16)
        down_part[:, :, :, at] = g_down.reshape((8, 2, PIECE, 256))
        return 0

    lax.fori_loop(0, width // 256, lambda c, _: weight_sum(c, gate_part, ggate), 0)
    sums.append(FsdpSum(copies, places, gate_part, sums_at[:5], 32))
    lax.fori_loop(0, width // 256, lambda c, _: weight_sum(c, up_part, gup), 0)
    sums.append(FsdpSum(copies, places, up_part, sums_at[5:10], 32))
    sums[0].ready()
    sums[0].send()
    lax.fori_loop(0, width // 256, down_sum, 0)
    sums.append(FsdpSum(copies, places, down_part, sums_at[10:15], 32))
    for item in sums[1:]:
        item.ready()
        item.send()
    for item in sums[:2]:
        item.relay()
    gn2 = gn2_all[pl.ds(pl.multiple_of(places.seq * rows, rows), rows), :].astype(F32)
    for copy in arrivals:
        copy.wait_recv()
    for slot_index in range(1, 8):
        gn2 += held[slot_index].astype(F32)
    value = h1_ref[...]
    inverse = unit_rows(value)
    normed = value * inverse
    term_ref[...] = jnp.sum(gn2 * normed, axis=0, keepdims=True)
    weighted = gn2 * gain[...]
    inner = jnp.mean(weighted * normed, axis=-1, keepdims=True)
    gh1 = dy_own[...].astype(F32) + inverse * (weighted - normed * inner)
    gh1_ref[...] = gh1
    gb_ref[...] = gh1.astype(BF16)

    def project_back(j, _):
        begin = pl.multiple_of(j * 256, 256)
        go_own[:, pl.ds(begin, 256)] = dot_nt(gb_ref[...], wo[pl.ds(begin, 256), :]).astype(BF16)
        return 0

    lax.fori_loop(0, width // 256, project_back, 0)
    landing = strips_at(go_ref, places.chip)
    sends = [(heads_at(go_own, head), landing, peer) for head, peer in zip(heads, workers)]
    swap_back = Swap(copies, tags_back, ends_back, places.chip, places.stays, sends)
    sums[2].relay()
    for item in sums:
        item.cross()
    for item, out in zip(sums, (gate_out, up_out, down_out)):
        out[...] = item.total().astype(BF16)
    swap_back.wait(lambda sender: strips_at(go_ref, sender))
    copies.finish()


def hidden_block(ob, wo, tokens, dy_own, gain, gate_up, down, dy):
    rows, width = tokens.shape
    shard, part = gate_up.shape[1:]
    slices = [(shard, part), (shard, part), (PIECE, width)]
    block = (8 * rows, width)
    vmem = [(rows, width)] * 3 + [block, (2, width, part), (16 * PIECE, width), (part, width)]
    vmem += [(8 * rows, part)] * 3 + [block, (8, rows, width)]
    vmem += [(8, 2) + shape for shape in slices]
    scratch = [pltpu.VMEM(shape, BF16) for shape in vmem]
    for shape in slices:
        scratch += fsdp_buffers(shape)
    scratch += [pltpu.SemaphoreType.DMA((n,)) for n in (8, 2, 8, 2)]
    return pl.pallas_call(
        hidden_kernel,
        out_shape=[
            jax.ShapeDtypeStruct((rows, width), BF16),
            jax.ShapeDtypeStruct((rows, width), F32),
            jax.ShapeDtypeStruct(block, BF16),
            jax.ShapeDtypeStruct((rows, width), F32),
            jax.ShapeDtypeStruct((rows, width), BF16),
            jax.ShapeDtypeStruct((1, width), F32),
            jax.ShapeDtypeStruct((8 * rows, 128), BF16),
        ]
        + [jax.ShapeDtypeStruct(shape, BF16) for shape in slices],
        in_specs=[HBM] + [IN_VMEM] * 4 + [HBM] * 2 + [IN_VMEM],
        out_specs=[IN_VMEM] * 6 + [HBM] + [IN_VMEM] * 3,
        scratch_shapes=scratch + semaphores(2 * 7 + 9 + 2 * 17 + 7 + 3 * FSDP_COPIES, 6),
        compiler_params=params(4),
        name="scatter_hidden_block",
    )(ob, wo, tokens, dy_own, gain, gate_up, down, dy)


def keys_kernel(
    branch, h1, gkv, gout, gate, up, gq, down,
    layer_ref, gkv_out, gout_out, gate_all, up_all, gq_out, down_out, ends,
    *scratch,
):
    copies, places = Copies(*scratch[14:]), Places()
    greet_for_move(places, places.gather_peers() + places.strip_peers(), places.piece_to)
    moved = Move(down, down_out, places.piece_from, places.fixed, ends)
    stages = [
        seq_gather(copies, places, gate, gate_all, 0, (0, 32)),
        seq_gather(copies, places, up, up_all, 0, (0, 32)),
    ]
    for stage in stages:
        next(stage)
    sums = [
        FsdpSum(copies, places, gkv, scratch[4:9], 512),
        FsdpSum(copies, places, gout, scratch[9:14], 32),
    ]
    hidden = SeqSum(copies, places, branch, scratch[:4], 64)
    items = [hidden] + sums
    for item in items:
        item.ready()
        item.send()
    strips = Strips(copies, places, gq, gq_out)
    for _ in range(2):
        for stage in stages:
            next(stage)
    hidden.relay()
    for item in sums:
        item.relay()
    for stage in stages:
        next(stage)
    for item in items:
        item.cross()
    run_stages(stages)
    for item, out in zip(sums, (gkv_out, gout_out)):
        out[...] = item.total().astype(BF16)
    layer_ref[...] = (h1[...] + hidden.total()).astype(BF16)
    strips.wait()
    moved.wait()
    copies.finish()


def scatter_keys(branch, h1, gkv, gout, gate, up, gq, down):
    rows, width = h1.shape
    shapes = [a.shape[2:] for a in (gkv, gout)]
    scratch = [pltpu.SemaphoreType.DMA((3,))] + seq_buffers((rows, width))
    for shape in shapes:
        scratch += fsdp_buffers(shape)
    wide = [jax.ShapeDtypeStruct((8 * a.shape[0],) + a.shape[1:], BF16) for a in (gate, up)]
    return pl.pallas_call(
        keys_kernel,
        out_shape=[jax.ShapeDtypeStruct((rows, width), BF16)]
        + [jax.ShapeDtypeStruct(shape, BF16) for shape in shapes]
        + wide
        + [jax.ShapeDtypeStruct(gq.shape, BF16), jax.ShapeDtypeStruct(down.shape, BF16)],
        in_specs=[HBM, IN_VMEM] + [HBM] * 6,
        out_specs=[IN_VMEM] * 3 + [HBM] * 4,
        scratch_shapes=scratch + semaphores(SEQ_COPIES + 2 * FSDP_COPIES + 18 + 7, 6),
        compiler_params=params(5),
        name="scatter_keys",
    )(branch, h1, gkv, gout, gate, up, gq, down)


def input_kernel(
    part, tokens, gain, gh1, pack, gout, down,
    grad_ref, pack_all, down_all,
    small, gathered, *scratch,
):
    copies, places = Copies(*scratch[9:]), Places()
    steps = range(1, 8)
    greet(places.gather_peers() + [places.on_seq(places.other_seq(d)) for d in steps])
    packs = FsdpSum(copies, places, pack, scratch[4:9], 48)
    stages = [seq_gather(copies, places, down, down_all, 0, (0, 16))]
    next(stages[0])
    outs = [
        copies.remote(
            gout.at[places.other_seq(d)], gathered.at[d], places.on_seq(places.other_seq(d))
        )
        for d in steps
    ]
    own = copies.here(gout.at[places.seq], gathered.at[0])
    hidden = SeqSum(copies, places, part, scratch[:4], 64)
    packs.ready()
    packs.send()
    hidden.ready()
    hidden.send()
    next(stages[0])
    packs.relay()
    next(stages[0])
    packs.cross()
    own.wait()
    for copy in outs:
        copy.wait_recv()
    rows = pack.shape[2]
    total = gathered[0].astype(F32)
    for d in steps:
        total += gathered[d].astype(F32)
    small[rows:] = total.astype(BF16)
    small[:rows] = packs.total().astype(BF16)
    stages.append(seq_gather(copies, places, small, pack_all, 0, (0, 64)))
    next(stages[1])
    hidden.relay()
    next(stages[0])
    next(stages[1])
    next(stages[1])
    hidden.cross()
    run_stages(stages)
    gn1 = hidden.total()
    value = tokens[...].astype(F32)
    inverse = unit_rows(value)
    normed = value * inverse
    weighted = gn1 * gain[...]
    inner = jnp.mean(weighted * normed, axis=-1, keepdims=True)
    grad_ref[...] = gh1[...] + inverse * (weighted - normed * inner)
    copies.finish()


def scatter_input(part, tokens, gain, gh1, pack, gout, down):
    rows, width = gh1.shape
    shape = pack.shape[2:]
    small = (shape[0] + gout.shape[1], shape[1])
    return pl.pallas_call(
        input_kernel,
        out_shape=[
            jax.ShapeDtypeStruct((rows, width), F32),
            jax.ShapeDtypeStruct((8 * small[0], small[1]), BF16),
            jax.ShapeDtypeStruct((8 * down.shape[0], width), BF16),
        ],
        in_specs=[HBM] + [IN_VMEM] * 3 + [HBM] * 3,
        out_specs=[IN_VMEM] + [HBM] * 2,
        scratch_shapes=[pltpu.VMEM(small, BF16), pltpu.VMEM(gout.shape, BF16)]
        + seq_buffers((rows, width))
        + fsdp_buffers(shape)
        + semaphores(SEQ_COPIES + FSDP_COPIES + 18 + 7, 5),
        compiler_params=params(6),
        name="scatter_input",
    )(part, tokens, gain, gh1, pack, gout, down)


def swap_halves(values):
    lane = lax.broadcasted_iota(jnp.int32, values.shape, 1)
    ahead, behind = pltpu.roll(values, 2 * HD - HD // 2, 1), pltpu.roll(values, HD // 2, 1)
    return jnp.where(lax.rem(lane, HD) < HD // 2, ahead, behind)


def head_means(values):
    low = lanes_low(values.shape)
    first = jnp.sum(jnp.where(low, values, 0.0), axis=1, keepdims=True)
    second = jnp.sum(jnp.where(low, 0.0, values), axis=1, keepdims=True)
    return jnp.where(low, first, second) * (1.0 / HD)


def heads_kernel(x_ref, weight_ref, gain_ref, gains_ref, cos_ref, sin_ref, n1_ref, pre_ref, q_ref, kv_ref):
    def tokens(t, _):
        at = pl.ds(pl.multiple_of(t * 256, 256), 256)
        x = x_ref[at, :].astype(F32)
        n1 = (x * unit_rows(x) * gain_ref[...]).astype(BF16)
        n1_ref[at, :] = n1
        pre = dot_nn(n1, weight_ref[...])
        pre_ref[at, :] = pre
        cosine, sine = cos_ref[at, :], sin_ref[at, :]
        outs = []
        for part in (0, 1):
            values = pre[:, part * 2 * HD : (part + 1) * 2 * HD]
            inverse = lax.rsqrt(head_means(values * values) + EPSILON)
            normed = values * inverse * gains_ref[part : part + 1, :]
            outs.append(normed * cosine + swap_halves(normed) * sine)
        q_ref[at, :] = outs[0].astype(BF16)
        kv_ref[at, :] = jnp.where(lanes_low(outs[1].shape), outs[1], pre[:, 2 * HD :]).astype(BF16)
        return 0

    lax.fori_loop(0, x_ref.shape[0] // 256, tokens, 0)


def project_heads(x, weight, gain, gains, cosine, sine):
    count, width = x.shape
    return pl.pallas_call(
        heads_kernel,
        out_shape=[
            jax.ShapeDtypeStruct((count, width), BF16),
            jax.ShapeDtypeStruct((count, 4 * HD), F32),
            jax.ShapeDtypeStruct((count, 2 * HD), BF16),
            jax.ShapeDtypeStruct((count, 2 * HD), BF16),
        ],
        in_specs=[IN_VMEM] * 6,
        out_specs=[IN_VMEM] * 4,
        compiler_params=pltpu.CompilerParams(vmem_limit_bytes=VMEM),
        name="project_heads",
    )(x, weight, gain, gains, cosine, sine)


def heads_back_kernel(
    x_ref, n1_ref, pre_ref, weight_ref, gains_ref, cos_ref, sin_ref, gq_ref, gkv_ref,
    gn1_ref, gheads_ref, gain_ref, terms_ref, gpre_ref,
):
    count, width = x_ref.shape
    gain_ref[...] = jnp.zeros_like(gain_ref)
    terms_ref[...] = jnp.zeros_like(terms_ref)

    def tokens(t, _):
        at = pl.ds(pl.multiple_of(t * 256, 256), 256)
        cosine, sine = cos_ref[at, :], sin_ref[at, :]
        for part, ref in ((0, gq_ref), (1, gkv_ref)):
            columns = pl.ds(part * 2 * HD, 2 * HD)
            grads = ref[at, :].astype(F32)
            values = pre_ref[at, columns]
            inverse = lax.rsqrt(head_means(values * values) + EPSILON)
            normed = values * inverse
            turned = grads * cosine - swap_halves(grads) * sine
            terms_ref[part : part + 1, :] += jnp.sum(turned * normed, axis=0, keepdims=True)
            weighted = turned * gains_ref[part : part + 1, :]
            back = inverse * (weighted - normed * head_means(weighted * normed))
            if part == 1:
                back = jnp.where(lanes_low(back.shape), back, grads)
            gpre_ref[at, columns] = back.astype(BF16)
        gn1 = dot_nt(gpre_ref[at, :], weight_ref[...])
        gn1_ref[at, :] = gn1.astype(BF16)
        x = x_ref[at, :].astype(F32)
        gain_ref[...] += jnp.sum(gn1 * (x * unit_rows(x)), axis=0, keepdims=True)
        return 0

    lax.fori_loop(0, count // 256, tokens, 0)

    def columns(c, _):
        at = pl.ds(pl.multiple_of(c * 256, 256), 256)
        gheads_ref[at, :] = dot_tn(n1_ref[:, at], gpre_ref[...]).astype(BF16)
        return 0

    lax.fori_loop(0, width // 256, columns, 0)


def heads_back(x, n1, pre, weight, gains, cosine, sine, gq, gkv):
    count, width = x.shape
    return pl.pallas_call(
        heads_back_kernel,
        out_shape=[
            jax.ShapeDtypeStruct((count, width), BF16),
            jax.ShapeDtypeStruct((width, 4 * HD), BF16),
            jax.ShapeDtypeStruct((1, width), F32),
            jax.ShapeDtypeStruct((2, 2 * HD), F32),
        ],
        in_specs=[IN_VMEM] * 9,
        out_specs=[IN_VMEM] * 4,
        scratch_shapes=[pltpu.VMEM((count, 4 * HD), BF16)],
        compiler_params=pltpu.CompilerParams(vmem_limit_bytes=VMEM),
        name="heads_back",
    )(x, n1, pre, weight, gains, cosine, sine, gq, gkv)


def local(
    tokens,
    segments,
    cotangent,
    attention_gain,
    query_gain,
    key_gain,
    query_weight,
    key_weight,
    value_weight,
    out_weight,
    feedforward_gain,
    gate_weight,
    up_weight,
    down_weight,
):
    seq_count = lax.axis_size("seq")
    fsdp_count = lax.axis_size("fsdp")
    fsdp = lax.axis_index("fsdp")
    seq = lax.axis_index("seq")
    rows, width = tokens.shape
    block = rows * seq_count
    hidden = gate_weight.shape[1]
    part = hidden // seq_count
    per_head = (H // KVH) * HD
    block_start = fsdp * block
    take = lax.dynamic_slice_in_dim

    gains = jnp.concatenate([attention_gain, feedforward_gain, query_gain, key_gain])
    heads_weight = jnp.concatenate(
        [
            take(query_weight, seq * per_head, per_head, 1),
            take(key_weight, seq * HD, HD, 1),
            take(value_weight, seq * HD, HD, 1),
        ],
        axis=1,
    )
    gains = jnp.pad(gains[None, :], ((0, 15), (0, heads_weight.shape[1] - gains.shape[0])))
    pieces = down_weight.shape[0] // seq_count
    down_pieces = jnp.pad(
        down_weight.reshape(seq_count, pieces, width), ((0, 0), (0, PIECE - pieces), (0, 0))
    ).reshape(-1, width)
    gate_up = jnp.stack(
        [take(gate_weight, seq * part, part, 1), take(up_weight, seq * part, part, 1)]
    )
    x_block, packs, wo, down_piece = gather(
        "gather_inputs",
        1,
        [(tokens, 0, (0, 64))],
        [(jnp.concatenate([heads_weight, gains]), 0, (0, 48)), (out_weight, 0, (0, 32))],
        pieces=down_pieces,
    )
    packs = packs.reshape(fsdp_count, -1, packs.shape[1])
    heads_weight = packs[:, : width // fsdp_count].reshape(width, -1)
    gains = packs[:, width // fsdp_count].astype(F32)

    shard = width // fsdp_count
    gain_one = gains[:, :shard].reshape(width)
    gain_two = gains[:, shard : 2 * shard].reshape(width)
    qshard = HD // fsdp_count
    gain_q = gains[:, 2 * shard : 2 * shard + qshard].reshape(HD)
    gain_k = gains[:, 2 * shard + qshard : 2 * shard + 2 * qshard].reshape(HD)

    starts = doc_starts(segments)
    labels = jnp.arange(DOCS, dtype=jnp.int32)

    def firsts(ids):
        picked = (ids[:, None] == labels[None, :]).astype(jnp.int32)
        return jnp.sum(picked * starts[None, :], axis=1)

    index = block_start + jnp.arange(block, dtype=jnp.int32)
    positions = index - firsts(take(segments, block_start, block))
    freqs = THETA ** (-2.0 * jnp.arange(HD // 2, dtype=F32) / HD)
    angles = positions.astype(F32)[:, None] * jnp.tile(freqs, 4)[None, :]
    side = jnp.tile(jnp.repeat(jnp.array([-1.0, 1.0], F32), HD // 2), 2)
    cosine, sine = jnp.cos(angles), jnp.sin(angles) * side[None, :]
    head_gains = jnp.stack([jnp.tile(gain_q, 2), jnp.tile(gain_k, 2)])
    shift = (HD**0.5 * LOG2E) * jnp.max(jnp.abs(gain_q)) * jnp.max(jnp.abs(gain_k))
    shift = shift.reshape(1)

    core, chip = fsdp % 2, fsdp // 2
    strip_ids = segments.reshape(fsdp_count // 2, 2, block // STRIP, STRIP)
    strip_ids = lax.dynamic_index_in_dim(strip_ids, core, 1, keepdims=False)
    strip_ids = lax.dynamic_index_in_dim(strip_ids, chip, 1, keepdims=False)
    first = firsts(strip_ids.reshape(-1))
    strip_first = first.reshape(-1, STRIP)
    q_first = (2 * jnp.arange(fsdp_count // 2, dtype=jnp.int32) + core) * block + chip * STRIP
    low = strip_first[:, 0] // KEYS
    high = (q_first + STRIP - 1) // KEYS + 1
    inner_low = jnp.minimum((strip_first[:, STRIP - 1] + KEYS - 1) // KEYS, high)
    inner_high = jnp.maximum((q_first + 1) // KEYS, inner_low)
    ranges = jnp.stack([low, inner_low, inner_high, high, q_first])

    n1, pre, q, kv = project_heads(
        x_block, heads_weight, gain_one[None, :], head_gains, cosine, sine
    )
    dy_block, kv, q = gather(
        "gather_keys",
        2,
        [(cotangent, 0, (0, 64))],
        [(kv, 0, (0, 512))],
        [q],
    )

    ob, o, totals = forward_attention(ranges, shift, q, first[:, None], kv)
    ob_own, h1_own, branch, gh1, gb, gain_two_term, go, g_gate, g_up, g_down = hidden_block(
        ob, wo, tokens, cotangent, gain_two[None, :], gate_up, down_piece, dy_block
    )
    by_core = lambda array: array.reshape(8, 2, -1, array.shape[-1])
    g_out = dot_tn(ob_own, gb).astype(BF16)
    gq, gkv = backward_attention(
        ranges, shift, q, go, o, totals, strip_first[:, None, :], kv
    )
    layer_out, gkv, g_out, g_gate, g_up, gq, g_down = scatter_keys(
        branch.reshape(seq_count, rows, width),
        h1_own,
        by_core(gkv),
        by_core(g_out),
        g_gate,
        g_up,
        gq,
        g_down,
    )
    gn1_partial, g_heads, gain_one_term, head_terms = heads_back(
        x_block, n1, pre, heads_weight, head_gains, cosine, sine, gq, gkv
    )
    gain_q_term = head_terms[0, :HD] + head_terms[0, HD:]
    gain_k_term = head_terms[1, :HD]
    g_heads = g_heads.reshape(fsdp_count, shard, -1)
    terms = jnp.concatenate(
        [
            gain_one_term.reshape(fsdp_count, shard),
            gain_two_term.reshape(fsdp_count, shard),
            gain_q_term.reshape(fsdp_count, qshard),
            gain_k_term.reshape(fsdp_count, qshard),
        ],
        axis=1,
    ).astype(BF16)
    terms = jnp.pad(terms[:, None, :], ((0, 0), (0, 15), (0, g_heads.shape[2] - terms.shape[1])))
    pack = jnp.concatenate([g_heads, terms], axis=1)
    input_grad, packs, g_down = scatter_input(
        gn1_partial.reshape(seq_count, rows, width),
        tokens,
        gain_one[None, :],
        gh1,
        pack.reshape((8, 2) + pack.shape[1:]),
        g_out.reshape(seq_count, -1, pack.shape[2]),
        g_down,
    )
    packs = packs.reshape(seq_count, -1, pack.shape[2])
    g_heads = packs[:, :shard]
    terms = jnp.sum(packs[:, shard].astype(F32), axis=0)
    g_out = packs[:, pack.shape[1] :].astype(F32).reshape(shard, width)
    g_down = g_down.reshape(seq_count, PIECE, width)[:, :pieces].reshape(-1, width)
    columns = lambda a: jnp.transpose(a.reshape(seq_count, shard, part), (1, 0, 2)).reshape(shard, hidden)

    g_query = jnp.transpose(g_heads[:, :, :per_head], (1, 0, 2)).reshape(shard, H * HD)
    g_key = jnp.transpose(g_heads[:, :, per_head : per_head + HD], (1, 0, 2)).reshape(shard, KVH * HD)
    g_value = jnp.transpose(g_heads[:, :, per_head + HD :], (1, 0, 2)).reshape(shard, KVH * HD)

    return (
        layer_out,
        input_grad,
        terms[:shard],
        terms[2 * shard : 2 * shard + qshard],
        terms[2 * shard + qshard : 2 * shard + 2 * qshard],
        g_query.astype(F32),
        g_key.astype(F32),
        g_value.astype(F32),
        g_out,
        terms[shard : 2 * shard],
        columns(g_gate).astype(F32),
        columns(g_up).astype(F32),
        g_down.astype(F32),
    )


def solution(mesh):
    rows = P(("fsdp", "seq"), None)
    matrix = P("fsdp", None)
    vector = P("fsdp")
    in_specs = (rows, P(), rows) + (vector,) * 3 + (matrix,) * 4 + (vector,) + (matrix,) * 3
    out_specs = (rows, rows) + (vector,) * 3 + (matrix,) * 4 + (vector,) + (matrix,) * 3
    return jax.shard_map(local, mesh=mesh, in_specs=in_specs, out_specs=out_specs, check_vma=False)
```

```python
import functools
import math

import jax
import jax.numpy as jnp
from jax import lax
from jax.experimental import pallas as pl
from jax.experimental.pallas import tpu as pltpu
from jax.sharding import PartitionSpec as P

H = 16
KVH = 8
HD = 64
DOCS = 4
EPSILON = 1e-06
THETA = 1000000.0
LOG2E = math.log2(math.e)
F32 = jnp.float32
BF16 = jnp.bfloat16
STRIP = 128
FEED = 256
KEYS = 1024
VMEM = 56 * 1024 * 1024
PIECE = 48


def doc_starts(segments):
    labels = jnp.arange(DOCS, dtype=jnp.int32)
    member = (segments[None, :] == labels[:, None]).astype(jnp.int32)
    lengths = jnp.sum(member, axis=1)
    return jnp.cumsum(lengths) - lengths


def dot_nt(a, b):
    return lax.dot_general(a, b, (((1,), (1,)), ((), ())), preferred_element_type=F32)


def dot_tn(a, b):
    return lax.dot_general(a, b, (((0,), (0,)), ((), ())), preferred_element_type=F32)


def dot_nn(a, b):
    return jnp.dot(a, b, preferred_element_type=F32)


def key_loops(ranges_ref, tile, step):
    low, inner_low, inner_high, high = [ranges_ref[i, tile] for i in range(4)]

    def masked(block, _):
        step(block, True)
        return 0

    def plain(block, _):
        step(block, False)
        return 0

    lax.fori_loop(low, inner_low, masked, 0)
    lax.fori_loop(inner_low, inner_high, plain, 0)
    lax.fori_loop(inner_high, high, masked, 0)


def lanes_low(shape):
    return lax.broadcasted_iota(jnp.int32, shape, 1) < HD


def two_heads(packed, low):
    other = pltpu.roll(packed, HD, 1)
    heads = (packed, other) if low else (other, packed)
    keep = lanes_low(packed.shape) if low else ~lanes_low(packed.shape)
    return jnp.concatenate([jnp.where(keep, head, 0.0) for head in heads], axis=0)


def one_row(heads, low):
    rows = heads.shape[0] // 2
    first, second = heads[:rows], heads[rows:]
    if low:
        second = pltpu.roll(second, HD, 1)
    else:
        first = pltpu.roll(first, HD, 1)
    return jnp.where(lanes_low(first.shape), first, second)


def forward_kernel(
    ranges_ref, shift_ref, query_ref, first_ref, kv_ref, ob_ref, o_ref, totals_ref, total
):
    tile = pl.program_id(0)
    rows = query_ref.shape[0]
    query = two_heads(query_ref[...].astype(F32) * HD**-0.5, True).astype(BF16)
    first = jnp.concatenate([first_ref[...]] * 2, axis=0)
    index = ranges_ref[4, tile] + lax.broadcasted_iota(jnp.int32, (rows, 1), 0)
    index = jnp.concatenate([index, index], axis=0)
    shift = shift_ref[0]
    ones = jnp.ones((KEYS, 2 * HD), BF16)
    total[...] = jnp.zeros_like(total)

    def step(block, masked):
        start = pl.multiple_of(block * KEYS, KEYS)
        kv = kv_ref[pl.ds(start, KEYS), :]
        exps = jnp.exp2(dot_nt(query, kv) * LOG2E - shift)
        if masked:
            keys = start + lax.broadcasted_iota(jnp.int32, (2 * rows, KEYS), 1)
            exps = jnp.where((keys >= first) & (keys <= index), exps, 0.0)
        total[...] += dot_nn(exps.astype(BF16), jnp.concatenate([kv, ones], axis=1))

    key_loops(ranges_ref, tile, step)
    totals = total[:, 2 * HD :]
    o = total[:, : 2 * HD] / totals
    o_ref[0] = o
    totals_ref[0] = totals
    ob_ref[...] = one_row(o, False).astype(BF16)


def forward_attention(ranges, shift, query, first, kv):
    tiles = query.shape[0] // STRIP
    whole = lambda t, *_: (0, 0)
    part = lambda t, *_: (t, 0)
    wide = lambda t, *_: (t, 0, 0)
    return pl.pallas_call(
        forward_kernel,
        grid_spec=pltpu.PrefetchScalarGridSpec(
            num_scalar_prefetch=2,
            grid=(tiles,),
            in_specs=[
                pl.BlockSpec((STRIP, 2 * HD), part),
                pl.BlockSpec((STRIP, 1), part),
                pl.BlockSpec(kv.shape, whole),
            ],
            out_specs=[
                pl.BlockSpec((STRIP, 2 * HD), part),
                pl.BlockSpec((1, 2 * STRIP, 2 * HD), wide),
                pl.BlockSpec((1, 2 * STRIP, 2 * HD), wide),
            ],
            scratch_shapes=[pltpu.VMEM((2 * STRIP, 4 * HD), F32)],
        ),
        out_shape=[
            jax.ShapeDtypeStruct(query.shape, BF16),
            jax.ShapeDtypeStruct((tiles, 2 * STRIP, 2 * HD), F32),
            jax.ShapeDtypeStruct((tiles, 2 * STRIP, 2 * HD), F32),
        ],
        compiler_params=pltpu.CompilerParams(vmem_limit_bytes=VMEM),
        cost_estimate=pl.CostEstimate(
            flops=8 * 10**9, bytes_accessed=8 * 10**6, transcendentals=16 * 10**6
        ),
        name="attention_forward",
    )(ranges, shift, query, first, kv)


def backward_kernel(
    ranges_ref, shift_ref, query_ref, grad_ref, o_ref, totals_ref, first_ref, kv_ref,
    gq_ref, gkv_ref, total, gq,
):
    tile = pl.program_id(0)
    rows = query_ref.shape[0]
    query = two_heads(query_ref[...].astype(F32) * HD**-0.5, True).astype(BF16)
    go = two_heads(grad_ref[...].astype(F32), False)
    totals = totals_ref[0]
    grad = (go / totals).astype(BF16)
    delta = jnp.sum(go * o_ref[0], axis=1, keepdims=True) / totals
    delta = jnp.transpose(delta)[:1]
    both = jnp.concatenate([query, grad], axis=0)
    first = jnp.concatenate([first_ref[0]] * 2, axis=1)
    index = ranges_ref[4, tile] + lax.broadcasted_iota(jnp.int32, (1, rows), 1)
    index = jnp.concatenate([index, index], axis=1)
    shift = shift_ref[0]

    @pl.when(tile == 0)
    def _():
        total[...] = jnp.zeros_like(total)

    gq[...] = jnp.zeros_like(gq)

    def step(block, masked):
        start = pl.multiple_of(block * KEYS, KEYS)
        kv = kv_ref[pl.ds(start, KEYS), :]
        exps = jnp.exp2(dot_nt(kv, query) * LOG2E - shift)
        if masked:
            keys = start + lax.broadcasted_iota(jnp.int32, (KEYS, 2 * rows), 0)
            exps = jnp.where((keys >= first) & (keys <= index), exps, 0.0)
        scores = (exps * (dot_nt(kv, grad) - delta)).astype(BF16)
        gq[...] += dot_tn(scores, kv)
        total[pl.ds(start, KEYS), :] += dot_nn(
            jnp.concatenate([scores, exps.astype(BF16)], axis=1), both
        )

    key_loops(ranges_ref, tile, step)
    gq_ref[...] = (one_row(gq[...], True) * HD**-0.5).astype(BF16)

    @pl.when(tile == pl.num_programs(0) - 1)
    def _():
        gkv_ref[...] = total[...].astype(BF16)


def backward_attention(ranges, shift, query, grad, o, totals, first, kv):
    tiles = query.shape[0] // STRIP
    whole = lambda t, *_: (0, 0)
    part = lambda t, *_: (t, 0)
    wide = lambda t, *_: (t, 0, 0)
    return pl.pallas_call(
        backward_kernel,
        grid_spec=pltpu.PrefetchScalarGridSpec(
            num_scalar_prefetch=2,
            grid=(tiles,),
            in_specs=[
                pl.BlockSpec((STRIP, 2 * HD), part),
                pl.BlockSpec((STRIP, 2 * HD), part),
                pl.BlockSpec((1, 2 * STRIP, 2 * HD), wide),
                pl.BlockSpec((1, 2 * STRIP, 2 * HD), wide),
                pl.BlockSpec((1, 1, STRIP), wide),
                pl.BlockSpec(kv.shape, whole),
            ],
            out_specs=[
                pl.BlockSpec((STRIP, 2 * HD), part),
                pl.BlockSpec(kv.shape, whole),
            ],
            scratch_shapes=[pltpu.VMEM(kv.shape, F32), pltpu.VMEM((2 * STRIP, 2 * HD), F32)],
        ),
        out_shape=[
            jax.ShapeDtypeStruct(query.shape, BF16),
            jax.ShapeDtypeStruct(kv.shape, BF16),
        ],
        compiler_params=pltpu.CompilerParams(vmem_limit_bytes=VMEM),
        cost_estimate=pl.CostEstimate(
            flops=20 * 10**9, bytes_accessed=16 * 10**6, transcendentals=16 * 10**6
        ),
        name="attention_backward",
    )(ranges, shift, query, grad, o, totals, first, kv)


MESH = pl.DeviceIdType.MESH
HBM = pl.BlockSpec(memory_space=pl.ANY)
IN_VMEM = pl.BlockSpec(memory_space=pltpu.VMEM)
RING = 8


def pair_of(value):
    return value + 1 - 2 * lax.rem(value, 2)


def ring_step(index, steps):
    return lax.div(index, RING) * RING + lax.rem(lax.rem(index, RING) + 2 * steps, RING)


class Copies:
    def __init__(self, send, recv, local):
        self.send, self.recv, self.local = send, recv, local
        self.started, self.locals = [], []

    def remote(self, src, dst, peer, recv=None):
        i = len(self.started)
        copy = pltpu.make_async_remote_copy(
            src_ref=src,
            dst_ref=dst,
            send_sem=self.send.at[i],
            recv_sem=self.recv.at[i] if recv is None else recv,
            device_id=peer,
            device_id_type=MESH,
        )
        copy.start()
        self.started.append(copy)
        return copy

    def here(self, src, dst):
        copy = pltpu.make_async_copy(src, dst, self.local.at[len(self.locals)])
        copy.start()
        self.locals.append(copy)
        return copy

    def finish(self):
        for copy in self.started:
            copy.wait_send()


def greet(peers):
    barrier = pltpu.get_barrier_semaphore()
    for peer in peers:
        pl.semaphore_signal(barrier, inc=1, device_id=peer, device_id_type=MESH)
    pl.semaphore_wait(barrier, len(peers))


def slot(ref, axis, size, index, split=None, half=0):
    start = index * size
    where = [pl.ds(0, n) for n in ref.shape]
    where[axis] = pl.ds(pl.multiple_of(start, 16), size)
    if split is not None:
        along, cut = split
        whole = size if along == axis else ref.shape[along]
        base = start if along == axis else 0
        begin, count = (0, cut) if half == 0 else (cut, whole - cut)
        offset = base + begin
        where[along] = pl.ds(pl.multiple_of(offset, 16) if along == axis else offset, count)
    return ref.at[tuple(where)]


def gather_stages(copies, src, out, axis, size, split, me, pair, device, sibling):
    plus, minus = ring_step(me, 1), ring_step(me, 3)
    at = functools.partial(slot, out, axis, size)
    halves = lambda index, half: at(index, split, half)
    to_sibling = []

    def pass_on(index):
        if sibling is not None:
            to_sibling.append(copies.remote(at(index), at(index), device(sibling)))

    def piece(half):
        along, at_row = split
        where = [pl.ds(0, n) for n in src.shape]
        where[along] = pl.ds(0, at_row) if half == 0 else pl.ds(at_row, src.shape[along] - at_row)
        return src.at[tuple(where)]

    def forward(index, half, peer):
        return copies.remote(halves(index, half), halves(index, half), device(peer))

    kept = copies.here(src, at(me))
    first = [copies.remote(piece(half), halves(me, half), device(pair)) for half in (0, 1)]
    ways = ((0, plus), (1, minus), (1, plus), (0, minus))
    near = [copies.remote(piece(half), halves(me, half), device(peer)) for half, peer in ways]
    if sibling is not None:
        to_sibling.append(copies.remote(src, at(me), device(sibling)))
    yield
    near[0].wait_recv()
    far = [forward(minus, 0, plus)]
    near[1].wait_recv()
    far.append(forward(plus, 1, minus))
    near[2].wait_recv()
    pass_on(minus)
    near[3].wait_recv()
    pass_on(plus)
    yield
    first[0].wait_recv()
    up_low, down_low = forward(pair, 0, plus), forward(pair, 0, minus)
    first[1].wait_recv()
    down_high, up_high = forward(pair, 1, minus), forward(pair, 1, plus)
    pass_on(pair)
    yield
    shift = pair - me
    up_low.wait_recv()
    last = [forward(minus + shift, 0, plus)]
    down_high.wait_recv()
    last.append(forward(plus + shift, 1, minus))
    up_high.wait_recv()
    pass_on(minus + shift)
    down_low.wait_recv()
    pass_on(plus + shift)
    yield
    opposite = ring_step(me, 2)
    for copy in far:
        copy.wait_recv()
    pass_on(opposite)
    yield
    for copy in last:
        copy.wait_recv()
    pass_on(opposite + shift)
    yield
    for copy in to_sibling:
        copy.wait_recv()
    kept.wait()


def run_stages(stages):
    live = list(stages)
    while live:
        live = [stage for stage in live if next(stage, stage) is not stage]


class Swap:
    def __init__(self, copies, recv, sem, tag, stays, sends):
        self.copies, self.recv, self.tag, self.stays = copies, recv, tag, stays
        (src, dst, peer), rest = sends[0], sends[1:]
        self.own = pltpu.make_async_remote_copy(
            src_ref=src,
            dst_ref=dst,
            send_sem=sem.at[0],
            recv_sem=recv.at[tag],
            device_id=peer,
            device_id_type=MESH,
        )
        self.kept = pltpu.make_async_copy(src, dst, sem.at[1])

        @pl.when(stays)
        def _():
            self.kept.start()

        @pl.when(jnp.logical_not(stays))
        def _():
            self.own.start()

        self.sample = (src, dst, peer, sem)
        for src, dst, peer in rest:
            copies.remote(src, dst, peer, recv.at[tag])

    def wait(self, landing):
        src, _, peer, sem = self.sample
        for step in range(1, 8):
            sender = lax.rem(self.tag + step, 8)
            pltpu.make_async_remote_copy(
                src_ref=src,
                dst_ref=landing(sender),
                send_sem=sem.at[0],
                recv_sem=self.recv.at[sender],
                device_id=peer,
                device_id_type=MESH,
            ).wait_recv()

        @pl.when(self.stays)
        def _():
            self.kept.wait()

        @pl.when(jnp.logical_not(self.stays))
        def _():
            self.own.wait()


def greet_for_swaps(places, peers):
    barrier = pltpu.get_barrier_semaphore()
    senders, others = places.heads()[1], places.owners()[1]
    peers = peers + senders[1:] + others[1:]
    for peer in peers:
        pl.semaphore_signal(barrier, inc=1, device_id=peer, device_id_type=MESH)

    @pl.when(places.stays)
    def _():
        pl.semaphore_wait(barrier, len(peers))

    @pl.when(jnp.logical_not(places.stays))
    def _():
        for peer in (senders[0], others[0]):
            pl.semaphore_signal(barrier, inc=1, device_id=peer, device_id_type=MESH)
        pl.semaphore_wait(barrier, len(peers) + 2)


class Move:
    def __init__(self, src, dst, peer, stays, sem):
        self.stays = stays
        self.own = pltpu.make_async_remote_copy(
            src_ref=src,
            dst_ref=dst,
            send_sem=sem.at[0],
            recv_sem=sem.at[1],
            device_id=peer,
            device_id_type=MESH,
        )
        self.kept = pltpu.make_async_copy(src, dst, sem.at[2])

        @pl.when(stays)
        def _():
            self.kept.start()

        @pl.when(jnp.logical_not(stays))
        def _():
            self.own.start()

    def wait(self):
        @pl.when(self.stays)
        def _():
            self.kept.wait()

        @pl.when(jnp.logical_not(self.stays))
        def _():
            self.own.wait()


def greet_for_move(places, peers, sender):
    barrier = pltpu.get_barrier_semaphore()
    for peer in peers:
        pl.semaphore_signal(barrier, inc=1, device_id=peer, device_id_type=MESH)

    @pl.when(places.fixed)
    def _():
        pl.semaphore_wait(barrier, len(peers))

    @pl.when(jnp.logical_not(places.fixed))
    def _():
        pl.semaphore_signal(barrier, inc=1, device_id=sender, device_id_type=MESH)
        pl.semaphore_wait(barrier, len(peers) + 1)


def strips_at(ref, index):
    return ref.at[pl.ds(pl.multiple_of(index * STRIP, STRIP), STRIP), :]


def heads_at(ref, index):
    return ref.at[:, pl.ds(pl.multiple_of(index * 2 * HD, 2 * HD), 2 * HD)]


class Places:
    def __init__(self):
        self.seq, self.fsdp = lax.axis_index("seq"), lax.axis_index("fsdp")
        self.core = lax.rem(self.fsdp, 2)
        self.chip = lax.div(self.fsdp, 2)
        self.row = lax.div(self.chip, 4)
        self.col = lax.rem(self.chip, 4)
        self.sibling = pair_of(self.fsdp)
        self.across = lax.rem(self.fsdp + 8, 16)
        self.stays = self.chip == self.seq
        self.piece_to = (self.chip, self.core * 8 + self.seq)
        self.piece_from = (lax.rem(self.fsdp, 8), 2 * self.seq + lax.div(self.fsdp, 8))
        self.fixed = (self.chip == self.seq) & (self.core * 8 + self.seq == self.fsdp)

    def on_seq(self, index):
        return (index, self.fsdp)

    def on_fsdp(self, index):
        return (self.seq, index)

    def other_seq(self, step):
        return lax.rem(self.seq + step, 8)

    def other_chip(self, step):
        return lax.rem(self.row + step // 4, 2) * 4 + lax.rem(self.col + step % 4, 4)

    def gather_peers(self):
        seq = [pair_of(self.seq), ring_step(self.seq, 1), ring_step(self.seq, 3)]
        fsdp = [self.across, ring_step(self.fsdp, 1), ring_step(self.fsdp, 3), self.sibling]
        return [self.on_seq(i) for i in seq] + [self.on_fsdp(i) for i in fsdp]

    def strip_peers(self):
        return [self.on_fsdp(self.other_chip(d) * 2 + self.core) for d in range(1, 8)]

    def owners(self):
        strips = [lax.rem(self.chip + d, 8) for d in range(8)]
        return strips, [(self.chip, strip * 2 + self.core) for strip in strips]

    def heads(self):
        heads = [lax.rem(self.seq + d, 8) for d in range(8)]
        return heads, [(head, self.seq * 2 + self.core) for head in heads]


def params(name_id):
    return pltpu.CompilerParams(
        collective_id=name_id, has_side_effects=True, vmem_limit_bytes=VMEM
    )


def semaphores(remote, local):
    return [
        pltpu.SemaphoreType.DMA((remote,)),
        pltpu.SemaphoreType.DMA((remote,)),
        pltpu.SemaphoreType.DMA((local,)),
    ]


def seq_gather(copies, places, src, out, axis, split):
    size = src.shape[axis]
    return gather_stages(
        copies, src, out, axis, size, split, places.seq, pair_of(places.seq), places.on_seq, None
    )


def fsdp_gather(copies, places, src, out, axis, split):
    size = src.shape[axis]
    return gather_stages(
        copies, src, out, axis, size, split, places.fsdp, places.across, places.on_fsdp, places.sibling
    )


class Strips:
    def __init__(self, copies, places, src, out):
        self.kept = copies.here(strips_at(src, places.chip), strips_at(out, places.chip))
        self.copies = []
        for d in range(1, 8):
            chip = places.other_chip(d)
            peer = places.on_fsdp(chip * 2 + places.core)
            self.copies.append(copies.remote(strips_at(src, chip), strips_at(out, places.chip), peer))

    def wait(self):
        for copy in self.copies:
            copy.wait_recv()
        self.kept.wait()


def gather(name, name_id, seq_items, fsdp_items, strips=(), pieces=None):
    items = seq_items + fsdp_items
    count = len(items)
    every = count + len(strips)
    sources = [item[0] for item in items] + list(strips) + ([] if pieces is None else [pieces])

    def kernel(*refs):
        total = len(sources)
        srcs, outs, rest = refs[:total], refs[total : 2 * total], refs[2 * total :]
        copies, places = Copies(*rest[:3]), Places()
        peers = places.gather_peers() + (places.strip_peers() if strips else [])
        if pieces is None:
            greet(peers)
        else:
            greet_for_move(places, peers, places.piece_from)
        stages = []
        order = list(range(count))
        for i in order[::-1] if strips else order:
            _, axis, split = items[i]
            make = seq_gather if i < len(seq_items) else fsdp_gather
            stages.append(make(copies, places, srcs[i], outs[i], axis, split))
            next(stages[-1])
        moved = [Strips(copies, places, srcs[i], outs[i]) for i in range(count, every)]
        if pieces is not None:
            at = pl.ds(pl.multiple_of(places.seq * PIECE, 16), PIECE)
            moved.append(Move(srcs[-1].at[at], outs[-1], places.piece_to, places.fixed, rest[3]))
        run_stages(stages)
        for item in moved:
            item.wait()
        copies.finish()

    shapes = []
    for i, (array, axis, _) in enumerate(items):
        shape = list(array.shape)
        shape[axis] *= 8 if i < len(seq_items) else 16
        shapes.append(jax.ShapeDtypeStruct(tuple(shape), array.dtype))
    shapes += [jax.ShapeDtypeStruct(array.shape, array.dtype) for array in strips]
    extra = []
    if pieces is not None:
        shapes.append(jax.ShapeDtypeStruct((PIECE,) + pieces.shape[1:], pieces.dtype))
        extra = [pltpu.SemaphoreType.DMA((3,))]
    remote = 14 * len(seq_items) + 22 * len(fsdp_items) + 7 * len(strips)
    return pl.pallas_call(
        kernel,
        out_shape=shapes,
        in_specs=[HBM] * len(sources),
        out_specs=[HBM] * len(sources),
        scratch_shapes=semaphores(remote, every) + extra,
        compiler_params=params(name_id),
        name=name,
    )(*sources)


class RingSum:
    def __init__(self, copies, near, mine, held, cut, index, device):
        self.remote, self.mine, self.device = copies.remote, mine, device
        self.half, self.ring, self.other = held
        self.cut, self.index = cut, index
        self.plus, self.minus, self.pair = near

    def parts(self):
        rows = self.mine.shape[1]
        return pl.ds(0, self.cut), pl.ds(self.cut, rows - self.cut)

    def send(self):
        low, high = self.parts()
        self.first, self.second = [], []
        for flip in (1, 0):
            far, up, down = [self.mine.at[self.index(flip, step)] for step in (2, 1, 3)]
            self.prepare(flip, 2)
            self.first.append(
                (
                    self.remote(far.at[low], self.half.at[flip, low], self.plus),
                    self.remote(far.at[high], self.half.at[flip, high], self.minus),
                )
            )
            self.prepare(flip, 1)
            self.prepare(flip, 3)
            self.second.append(
                [
                    self.remote(up.at[high], self.ring.at[flip, 0, high], self.plus),
                    self.remote(down.at[low], self.ring.at[flip, 1, low], self.minus),
                ]
            )

    def relay(self):
        low, high = self.parts()
        for i, flip in enumerate((1, 0)):
            for copy, step, part, way, peer in (
                (self.first[i][0], 1, low, 0, self.plus),
                (self.first[i][1], 3, high, 1, self.minus),
            ):
                copy.wait_recv()
                at = self.index(flip, step)
                self.mine[at, part] = (
                    self.mine[at, part].astype(F32) + self.half[flip, part].astype(F32)
                ).astype(BF16)
                self.second[i].append(
                    self.remote(self.mine.at[at, part], self.ring.at[flip, way, part], peer)
                )

    def prepare(self, flip, step):
        pass

    def gathered(self, i, flip):
        self.prepare(flip, 0)
        for copy in self.second[i]:
            copy.wait_recv()
        return (
            self.mine[self.index(flip, 0)].astype(F32)
            + self.ring[flip, 0].astype(F32)
            + self.ring[flip, 1].astype(F32)
        )

    def cross(self):
        self.other[0] = self.gathered(0, 1).astype(BF16)
        self.last = self.remote(self.other.at[0], self.other.at[1], self.pair)

    def total(self):
        total = self.gathered(1, 0)
        self.last.wait_recv()
        return total + self.other[1].astype(F32)


def ring_buffers(shape):
    return [
        pltpu.VMEM((2,) + shape, BF16),
        pltpu.VMEM((2, 2) + shape, BF16),
        pltpu.VMEM((2,) + shape, BF16),
    ]


RING_COPIES = 13


class SeqSum(RingSum):
    def __init__(self, copies, places, part, buffers, cut):
        mine, held = buffers[0], buffers[1:]
        seq = places.seq

        def index(flip, step):
            base = ring_step(seq, step)
            return pair_of(base) if flip else base

        near = [places.on_seq(i) for i in (ring_step(seq, 1), ring_step(seq, 3), pair_of(seq))]
        super().__init__(copies, near, mine, held, cut, index, places.on_seq)
        self.kept = copies.here(part, mine)

    def ready(self):
        self.kept.wait()


class FsdpSum(RingSum):
    def __init__(self, copies, places, part, buffers, cut):
        mine, self.theirs, held = buffers[0], buffers[1], buffers[2:]
        fsdp = places.fsdp

        def index(flip, step):
            return lax.rem(places.row + flip, 2) * 4 + lax.rem(places.col + step, 4)

        near = [places.on_fsdp(i) for i in (ring_step(fsdp, 1), ring_step(fsdp, 3), places.across)]
        super().__init__(copies, near, mine, held, cut, index, places.on_fsdp)
        self.others = {
            (flip, step): copies.remote(
                part.at[index(flip, step), 1 - places.core],
                self.theirs.at[index(flip, step)],
                places.on_fsdp(places.sibling),
            )
            for flip in (1, 0)
            for step in (2, 1, 3, 0)
        }
        self.kept = copies.here(part.at[:, places.core], mine)

    def ready(self):
        self.kept.wait()

    def prepare(self, flip, step):
        self.others[flip, step].wait_recv()
        at = self.index(flip, step)
        self.mine[at] = (self.mine[at].astype(F32) + self.theirs[at].astype(F32)).astype(BF16)


def seq_buffers(shape):
    return [pltpu.VMEM((8,) + shape, BF16)] + ring_buffers(shape)


def fsdp_buffers(shape):
    return [pltpu.VMEM((8,) + shape, BF16)] * 2 + ring_buffers(shape)


SEQ_COPIES = RING_COPIES
FSDP_COPIES = RING_COPIES + 8


def unit_rows(values):
    return lax.rsqrt(jnp.mean(values * values, axis=-1, keepdims=True) + EPSILON)


def spread(pieces, part):
    shape = (pieces * PIECE, part)
    row = lax.broadcasted_iota(jnp.int32, shape, 0)
    column = lax.broadcasted_iota(jnp.int32, shape, 1)
    size = part // pieces
    inside = lax.rem(row, PIECE)
    hit = (lax.div(row, PIECE) * size + inside == column) & (inside < size)
    return jnp.where(hit, 1.0, 0.0).astype(BF16)


def hidden_kernel(
    ob, wo, tokens, dy_own, gain, gate_up, down, dy,
    own_ref, h1_ref, branch_ref, gh1_ref, gb_ref, term_ref, go_ref, gate_out, up_out, down_out,
    own, n2, go_own, n2_all, weights, down_pad, down_all, act, ggate, gup, gn2_all, held,
    gate_part, up_part, down_part, *scratch,
):
    sums_at = scratch[:15]
    tags, ends, tags_back, ends_back = scratch[15:19]
    copies, places = Copies(*scratch[19:]), Places()
    others = [places.on_seq(places.other_seq(d)) for d in range(1, 8)]
    greet_for_swaps(places, places.gather_peers() + others)
    rows, width = own.shape
    part = down_all.shape[0]
    pieces = down_pad.shape[0] // PIECE

    strips, owners = places.owners()
    heads, workers = places.heads()
    landing = heads_at(own, places.seq)
    sends = [(strips_at(ob, strip), landing, peer) for strip, peer in zip(strips, owners)]
    swap = Swap(copies, tags, ends, places.seq, places.stays, sends)
    gathers = [
        fsdp_gather(copies, places, gate_up, weights, 1, (1, 32)),
        fsdp_gather(copies, places, down, down_pad, 0, (0, 32)),
    ]
    for stage in gathers:
        next(stage)
    swap.wait(lambda sender: heads_at(own, sender))
    own_ref[...] = own[...]

    def project(j, _):
        at = pl.ds(pl.multiple_of(j * 256, 256), 256)
        h1_ref[:, at] = tokens[:, at].astype(F32) + dot_nn(own[...], wo[:, at])
        return 0

    lax.fori_loop(0, width // 256, project, 0)
    value = h1_ref[...]
    inverse = unit_rows(value)
    n2[...] = (value * inverse * gain[...]).astype(BF16)
    tokens_in = seq_gather(copies, places, n2, n2_all, 0, (0, 64))
    next(tokens_in)
    for _ in range(3):
        for stage in gathers:
            next(stage)
        if _ < 2:
            next(tokens_in)
    run_stages(gathers)
    matrix = spread(pieces, part)

    def pack_down(j, _):
        at = pl.ds(pl.multiple_of(j * 256, 256), 256)
        down_all[:, at] = dot_tn(matrix, down_pad[:, at]).astype(BF16)
        return 0

    lax.fori_loop(0, width // 256, pack_down, 0)

    arrivals = []

    def feed(step):
        base = lax.div(ring_step(places.seq, step), 2) * 2 * rows
        at = pl.ds(pl.multiple_of(base, 2 * rows), 2 * rows)
        values = n2_all[at, :]
        gate = dot_nn(values, weights[0])
        up = dot_nn(values, weights[1])
        gact = dot_nt(dy[at, :], down_all[...])
        sig = jax.nn.sigmoid(gate)
        silu = gate * sig
        act_here = (silu * up).astype(BF16)
        gg = (gact * up * sig * (1.0 + gate * (1.0 - sig))).astype(BF16)
        gu = (gact * silu).astype(BF16)
        act[at, :] = act_here
        ggate[at, :] = gg
        gup[at, :] = gu
        gn2_all[at, :] = (dot_nt(gg, weights[0]) + dot_nt(gu, weights[1])).astype(BF16)
        for flip in (1, 0):
            if step == 0 and flip == 0:
                continue
            peer = ring_step(places.seq, step)
            peer = pair_of(peer) if flip else peer
            arrivals.append(
                copies.remote(
                    gn2_all.at[pl.ds(pl.multiple_of(peer * rows, rows), rows), :],
                    held.at[2 * step + flip],
                    places.on_seq(peer),
                )
            )
        branch_ref[at, :] = dot_nn(act_here, down_all[...]).astype(BF16)

    tokens_in.send(None)
    kept_first = copies.locals[-1]
    kept_first.wait()
    feed(0)
    feed(1)
    feed(3)
    next(tokens_in)
    next(tokens_in)
    feed(2)

    sums = []

    def weight_sum(c, part_ref, grads):
        at = pl.ds(pl.multiple_of(c * 256, 256), 256)
        shape = (2, 2) + part_ref.shape[2:]
        part_ref[pl.ds(c * 2, 2)] = dot_tn(n2_all[:, at], grads[...]).astype(BF16).reshape(shape)
        return 0

    def down_sum(c, _):
        at = pl.ds(pl.multiple_of(c * 256, 256), 256)
        g_down = dot_nn(matrix, dot_tn(act[...], dy[:, at]).astype(BF16)).astype(BF16)
        down_part[:, :, :, at] = g_down.reshape((8, 2, PIECE, 256))
        return 0

    lax.fori_loop(0, width // 256, lambda c, _: weight_sum(c, gate_part, ggate), 0)
    sums.append(FsdpSum(copies, places, gate_part, sums_at[:5], 32))
    lax.fori_loop(0, width // 256, lambda c, _: weight_sum(c, up_part, gup), 0)
    sums.append(FsdpSum(copies, places, up_part, sums_at[5:10], 32))
    sums[0].ready()
    sums[0].send()
    lax.fori_loop(0, width // 256, down_sum, 0)
    sums.append(FsdpSum(copies, places, down_part, sums_at[10:15], 32))
    for item in sums[1:]:
        item.ready()
        item.send()
    for item in sums[:2]:
        item.relay()
    gn2 = gn2_all[pl.ds(pl.multiple_of(places.seq * rows, rows), rows), :].astype(F32)
    for copy in arrivals:
        copy.wait_recv()
    for slot_index in range(1, 8):
        gn2 += held[slot_index].astype(F32)
    value = h1_ref[...]
    inverse = unit_rows(value)
    normed = value * inverse
    term_ref[...] = jnp.sum(gn2 * normed, axis=0, keepdims=True)
    weighted = gn2 * gain[...]
    inner = jnp.mean(weighted * normed, axis=-1, keepdims=True)
    gh1 = dy_own[...].astype(F32) + inverse * (weighted - normed * inner)
    gh1_ref[...] = gh1
    gb_ref[...] = gh1.astype(BF16)

    def project_back(j, _):
        begin = pl.multiple_of(j * 256, 256)
        go_own[:, pl.ds(begin, 256)] = dot_nt(gb_ref[...], wo[pl.ds(begin, 256), :]).astype(BF16)
        return 0

    lax.fori_loop(0, width // 256, project_back, 0)
    landing = strips_at(go_ref, places.chip)
    sends = [(heads_at(go_own, head), landing, peer) for head, peer in zip(heads, workers)]
    swap_back = Swap(copies, tags_back, ends_back, places.chip, places.stays, sends)
    sums[2].relay()
    for item in sums:
        item.cross()
    for item, out in zip(sums, (gate_out, up_out, down_out)):
        out[...] = item.total().astype(BF16)
    swap_back.wait(lambda sender: strips_at(go_ref, sender))
    copies.finish()


def hidden_block(ob, wo, tokens, dy_own, gain, gate_up, down, dy):
    rows, width = tokens.shape
    shard, part = gate_up.shape[1:]
    slices = [(shard, part), (shard, part), (PIECE, width)]
    block = (8 * rows, width)
    vmem = [(rows, width)] * 3 + [block, (2, width, part), (16 * PIECE, width), (part, width)]
    vmem += [(8 * rows, part)] * 3 + [block, (8, rows, width)]
    vmem += [(8, 2) + shape for shape in slices]
    scratch = [pltpu.VMEM(shape, BF16) for shape in vmem]
    for shape in slices:
        scratch += fsdp_buffers(shape)
    scratch += [pltpu.SemaphoreType.DMA((n,)) for n in (8, 2, 8, 2)]
    return pl.pallas_call(
        hidden_kernel,
        out_shape=[
            jax.ShapeDtypeStruct((rows, width), BF16),
            jax.ShapeDtypeStruct((rows, width), F32),
            jax.ShapeDtypeStruct(block, BF16),
            jax.ShapeDtypeStruct((rows, width), F32),
            jax.ShapeDtypeStruct((rows, width), BF16),
            jax.ShapeDtypeStruct((1, width), F32),
            jax.ShapeDtypeStruct((8 * rows, 128), BF16),
        ]
        + [jax.ShapeDtypeStruct(shape, BF16) for shape in slices],
        in_specs=[HBM] + [IN_VMEM] * 4 + [HBM] * 2 + [IN_VMEM],
        out_specs=[IN_VMEM] * 6 + [HBM] + [IN_VMEM] * 3,
        scratch_shapes=scratch + semaphores(2 * 7 + 14 + 2 * 22 + 7 + 3 * FSDP_COPIES, 6),
        compiler_params=params(4),
        name="scatter_hidden_block",
    )(ob, wo, tokens, dy_own, gain, gate_up, down, dy)


def keys_kernel(
    branch, h1, gkv, gout, gate, up, gq, down,
    layer_ref, gkv_out, gout_out, gate_all, up_all, gq_out, down_out, ends,
    *scratch,
):
    copies, places = Copies(*scratch[14:]), Places()
    greet_for_move(places, places.gather_peers() + places.strip_peers(), places.piece_to)
    moved = Move(down, down_out, places.piece_from, places.fixed, ends)
    stages = [
        seq_gather(copies, places, gate, gate_all, 0, (0, 32)),
        seq_gather(copies, places, up, up_all, 0, (0, 32)),
    ]
    for stage in stages:
        next(stage)
    sums = [
        FsdpSum(copies, places, gkv, scratch[4:9], 512),
        FsdpSum(copies, places, gout, scratch[9:14], 32),
    ]
    hidden = SeqSum(copies, places, branch, scratch[:4], 64)
    items = [hidden] + sums
    for item in items:
        item.ready()
        item.send()
    strips = Strips(copies, places, gq, gq_out)
    for _ in range(2):
        for stage in stages:
            next(stage)
    hidden.relay()
    for item in sums:
        item.relay()
    for stage in stages:
        next(stage)
    for item in items:
        item.cross()
    run_stages(stages)
    for item, out in zip(sums, (gkv_out, gout_out)):
        out[...] = item.total().astype(BF16)
    layer_ref[...] = (h1[...] + hidden.total()).astype(BF16)
    strips.wait()
    moved.wait()
    copies.finish()


def scatter_keys(branch, h1, gkv, gout, gate, up, gq, down):
    rows, width = h1.shape
    shapes = [a.shape[2:] for a in (gkv, gout)]
    scratch = [pltpu.SemaphoreType.DMA((3,))] + seq_buffers((rows, width))
    for shape in shapes:
        scratch += fsdp_buffers(shape)
    wide = [jax.ShapeDtypeStruct((8 * a.shape[0],) + a.shape[1:], BF16) for a in (gate, up)]
    return pl.pallas_call(
        keys_kernel,
        out_shape=[jax.ShapeDtypeStruct((rows, width), BF16)]
        + [jax.ShapeDtypeStruct(shape, BF16) for shape in shapes]
        + wide
        + [jax.ShapeDtypeStruct(gq.shape, BF16), jax.ShapeDtypeStruct(down.shape, BF16)],
        in_specs=[HBM, IN_VMEM] + [HBM] * 6,
        out_specs=[IN_VMEM] * 3 + [HBM] * 4,
        scratch_shapes=scratch + semaphores(SEQ_COPIES + 2 * FSDP_COPIES + 28 + 7, 6),
        compiler_params=params(5),
        name="scatter_keys",
    )(branch, h1, gkv, gout, gate, up, gq, down)


def input_kernel(
    part, tokens, gain, gh1, pack, gout, down,
    grad_ref, pack_all, down_all,
    small, gathered, *scratch,
):
    copies, places = Copies(*scratch[9:]), Places()
    steps = range(1, 8)
    greet(places.gather_peers() + [places.on_seq(places.other_seq(d)) for d in steps])
    packs = FsdpSum(copies, places, pack, scratch[4:9], 48)
    stages = [seq_gather(copies, places, down, down_all, 0, (0, 16))]
    next(stages[0])
    outs = [
        copies.remote(
            gout.at[places.other_seq(d)], gathered.at[d], places.on_seq(places.other_seq(d))
        )
        for d in steps
    ]
    own = copies.here(gout.at[places.seq], gathered.at[0])
    hidden = SeqSum(copies, places, part, scratch[:4], 64)
    packs.ready()
    packs.send()
    hidden.ready()
    hidden.send()
    next(stages[0])
    packs.relay()
    next(stages[0])
    packs.cross()
    own.wait()
    for copy in outs:
        copy.wait_recv()
    rows = pack.shape[2]
    total = gathered[0].astype(F32)
    for d in steps:
        total += gathered[d].astype(F32)
    small[rows:] = total.astype(BF16)
    small[:rows] = packs.total().astype(BF16)
    stages.append(seq_gather(copies, places, small, pack_all, 0, (0, 64)))
    next(stages[1])
    hidden.relay()
    next(stages[0])
    next(stages[1])
    next(stages[1])
    hidden.cross()
    run_stages(stages)
    gn1 = hidden.total()
    value = tokens[...].astype(F32)
    inverse = unit_rows(value)
    normed = value * inverse
    weighted = gn1 * gain[...]
    inner = jnp.mean(weighted * normed, axis=-1, keepdims=True)
    grad_ref[...] = gh1[...] + inverse * (weighted - normed * inner)
    copies.finish()


def scatter_input(part, tokens, gain, gh1, pack, gout, down):
    rows, width = gh1.shape
    shape = pack.shape[2:]
    small = (shape[0] + gout.shape[1], shape[1])
    return pl.pallas_call(
        input_kernel,
        out_shape=[
            jax.ShapeDtypeStruct((rows, width), F32),
            jax.ShapeDtypeStruct((8 * small[0], small[1]), BF16),
            jax.ShapeDtypeStruct((8 * down.shape[0], width), BF16),
        ],
        in_specs=[HBM] + [IN_VMEM] * 3 + [HBM] * 3,
        out_specs=[IN_VMEM] + [HBM] * 2,
        scratch_shapes=[pltpu.VMEM(small, BF16), pltpu.VMEM(gout.shape, BF16)]
        + seq_buffers((rows, width))
        + fsdp_buffers(shape)
        + semaphores(SEQ_COPIES + FSDP_COPIES + 28 + 7, 5),
        compiler_params=params(6),
        name="scatter_input",
    )(part, tokens, gain, gh1, pack, gout, down)


def swap_halves(values):
    lane = lax.broadcasted_iota(jnp.int32, values.shape, 1)
    ahead, behind = pltpu.roll(values, 2 * HD - HD // 2, 1), pltpu.roll(values, HD // 2, 1)
    return jnp.where(lax.rem(lane, HD) < HD // 2, ahead, behind)


def head_means(values):
    low = lanes_low(values.shape)
    first = jnp.sum(jnp.where(low, values, 0.0), axis=1, keepdims=True)
    second = jnp.sum(jnp.where(low, 0.0, values), axis=1, keepdims=True)
    return jnp.where(low, first, second) * (1.0 / HD)


def heads_kernel(x_ref, weight_ref, gain_ref, gains_ref, cos_ref, sin_ref, n1_ref, pre_ref, q_ref, kv_ref):
    def tokens(t, _):
        at = pl.ds(pl.multiple_of(t * 256, 256), 256)
        x = x_ref[at, :].astype(F32)
        n1 = (x * unit_rows(x) * gain_ref[...]).astype(BF16)
        n1_ref[at, :] = n1
        pre = dot_nn(n1, weight_ref[...])
        pre_ref[at, :] = pre
        cosine, sine = cos_ref[at, :], sin_ref[at, :]
        outs = []
        for part in (0, 1):
            values = pre[:, part * 2 * HD : (part + 1) * 2 * HD]
            inverse = lax.rsqrt(head_means(values * values) + EPSILON)
            normed = values * inverse * gains_ref[part : part + 1, :]
            outs.append(normed * cosine + swap_halves(normed) * sine)
        q_ref[at, :] = outs[0].astype(BF16)
        kv_ref[at, :] = jnp.where(lanes_low(outs[1].shape), outs[1], pre[:, 2 * HD :]).astype(BF16)
        return 0

    lax.fori_loop(0, x_ref.shape[0] // 256, tokens, 0)


def project_heads(x, weight, gain, gains, cosine, sine):
    count, width = x.shape
    return pl.pallas_call(
        heads_kernel,
        out_shape=[
            jax.ShapeDtypeStruct((count, width), BF16),
            jax.ShapeDtypeStruct((count, 4 * HD), F32),
            jax.ShapeDtypeStruct((count, 2 * HD), BF16),
            jax.ShapeDtypeStruct((count, 2 * HD), BF16),
        ],
        in_specs=[IN_VMEM] * 6,
        out_specs=[IN_VMEM] * 4,
        compiler_params=pltpu.CompilerParams(vmem_limit_bytes=VMEM),
        name="project_heads",
    )(x, weight, gain, gains, cosine, sine)


def heads_back_kernel(
    x_ref, n1_ref, pre_ref, weight_ref, gains_ref, cos_ref, sin_ref, gq_ref, gkv_ref,
    gn1_ref, gheads_ref, gain_ref, terms_ref, gpre_ref,
):
    count, width = x_ref.shape
    gain_ref[...] = jnp.zeros_like(gain_ref)
    terms_ref[...] = jnp.zeros_like(terms_ref)

    def tokens(t, _):
        at = pl.ds(pl.multiple_of(t * 256, 256), 256)
        cosine, sine = cos_ref[at, :], sin_ref[at, :]
        for part, ref in ((0, gq_ref), (1, gkv_ref)):
            columns = pl.ds(part * 2 * HD, 2 * HD)
            grads = ref[at, :].astype(F32)
            values = pre_ref[at, columns]
            inverse = lax.rsqrt(head_means(values * values) + EPSILON)
            normed = values * inverse
            turned = grads * cosine - swap_halves(grads) * sine
            terms_ref[part : part + 1, :] += jnp.sum(turned * normed, axis=0, keepdims=True)
            weighted = turned * gains_ref[part : part + 1, :]
            back = inverse * (weighted - normed * head_means(weighted * normed))
            if part == 1:
                back = jnp.where(lanes_low(back.shape), back, grads)
            gpre_ref[at, columns] = back.astype(BF16)
        gn1 = dot_nt(gpre_ref[at, :], weight_ref[...])
        gn1_ref[at, :] = gn1.astype(BF16)
        x = x_ref[at, :].astype(F32)
        gain_ref[...] += jnp.sum(gn1 * (x * unit_rows(x)), axis=0, keepdims=True)
        return 0

    lax.fori_loop(0, count // 256, tokens, 0)

    def columns(c, _):
        at = pl.ds(pl.multiple_of(c * 256, 256), 256)
        gheads_ref[at, :] = dot_tn(n1_ref[:, at], gpre_ref[...]).astype(BF16)
        return 0

    lax.fori_loop(0, width // 256, columns, 0)


def heads_back(x, n1, pre, weight, gains, cosine, sine, gq, gkv):
    count, width = x.shape
    return pl.pallas_call(
        heads_back_kernel,
        out_shape=[
            jax.ShapeDtypeStruct((count, width), BF16),
            jax.ShapeDtypeStruct((width, 4 * HD), BF16),
            jax.ShapeDtypeStruct((1, width), F32),
            jax.ShapeDtypeStruct((2, 2 * HD), F32),
        ],
        in_specs=[IN_VMEM] * 9,
        out_specs=[IN_VMEM] * 4,
        scratch_shapes=[pltpu.VMEM((count, 4 * HD), BF16)],
        compiler_params=pltpu.CompilerParams(vmem_limit_bytes=VMEM),
        name="heads_back",
    )(x, n1, pre, weight, gains, cosine, sine, gq, gkv)


def local(
    tokens,
    segments,
    cotangent,
    attention_gain,
    query_gain,
    key_gain,
    query_weight,
    key_weight,
    value_weight,
    out_weight,
    feedforward_gain,
    gate_weight,
    up_weight,
    down_weight,
):
    seq_count = lax.axis_size("seq")
    fsdp_count = lax.axis_size("fsdp")
    fsdp = lax.axis_index("fsdp")
    seq = lax.axis_index("seq")
    rows, width = tokens.shape
    block = rows * seq_count
    hidden = gate_weight.shape[1]
    part = hidden // seq_count
    per_head = (H // KVH) * HD
    block_start = fsdp * block
    take = lax.dynamic_slice_in_dim

    gains = jnp.concatenate([attention_gain, feedforward_gain, query_gain, key_gain])
    heads_weight = jnp.concatenate(
        [
            take(query_weight, seq * per_head, per_head, 1),
            take(key_weight, seq * HD, HD, 1),
            take(value_weight, seq * HD, HD, 1),
        ],
        axis=1,
    )
    gains = jnp.pad(gains[None, :], ((0, 15), (0, heads_weight.shape[1] - gains.shape[0])))
    pieces = down_weight.shape[0] // seq_count
    down_pieces = jnp.pad(
        down_weight.reshape(seq_count, pieces, width), ((0, 0), (0, PIECE - pieces), (0, 0))
    ).reshape(-1, width)
    gate_up = jnp.stack(
        [take(gate_weight, seq * part, part, 1), take(up_weight, seq * part, part, 1)]
    )
    x_block, packs, wo, down_piece = gather(
        "gather_inputs",
        1,
        [(tokens, 0, (0, 64))],
        [(jnp.concatenate([heads_weight, gains]), 0, (0, 48)), (out_weight, 0, (0, 32))],
        pieces=down_pieces,
    )
    packs = packs.reshape(fsdp_count, -1, packs.shape[1])
    heads_weight = packs[:, : width // fsdp_count].reshape(width, -1)
    gains = packs[:, width // fsdp_count].astype(F32)

    shard = width // fsdp_count
    gain_one = gains[:, :shard].reshape(width)
    gain_two = gains[:, shard : 2 * shard].reshape(width)
    qshard = HD // fsdp_count
    gain_q = gains[:, 2 * shard : 2 * shard + qshard].reshape(HD)
    gain_k = gains[:, 2 * shard + qshard : 2 * shard + 2 * qshard].reshape(HD)

    starts = doc_starts(segments)
    labels = jnp.arange(DOCS, dtype=jnp.int32)

    def firsts(ids):
        picked = (ids[:, None] == labels[None, :]).astype(jnp.int32)
        return jnp.sum(picked * starts[None, :], axis=1)

    index = block_start + jnp.arange(block, dtype=jnp.int32)
    positions = index - firsts(take(segments, block_start, block))
    freqs = THETA ** (-2.0 * jnp.arange(HD // 2, dtype=F32) / HD)
    angles = positions.astype(F32)[:, None] * jnp.tile(freqs, 4)[None, :]
    side = jnp.tile(jnp.repeat(jnp.array([-1.0, 1.0], F32), HD // 2), 2)
    cosine, sine = jnp.cos(angles), jnp.sin(angles) * side[None, :]
    head_gains = jnp.stack([jnp.tile(gain_q, 2), jnp.tile(gain_k, 2)])
    shift = (HD**0.5 * LOG2E) * jnp.max(jnp.abs(gain_q)) * jnp.max(jnp.abs(gain_k))
    shift = shift.reshape(1)

    core, chip = fsdp % 2, fsdp // 2
    strip_ids = segments.reshape(fsdp_count // 2, 2, block // STRIP, STRIP)
    strip_ids = lax.dynamic_index_in_dim(strip_ids, core, 1, keepdims=False)
    strip_ids = lax.dynamic_index_in_dim(strip_ids, chip, 1, keepdims=False)
    first = firsts(strip_ids.reshape(-1))
    strip_first = first.reshape(-1, STRIP)
    q_first = (2 * jnp.arange(fsdp_count // 2, dtype=jnp.int32) + core) * block + chip * STRIP
    low = strip_first[:, 0] // KEYS
    high = (q_first + STRIP - 1) // KEYS + 1
    inner_low = jnp.minimum((strip_first[:, STRIP - 1] + KEYS - 1) // KEYS, high)
    inner_high = jnp.maximum((q_first + 1) // KEYS, inner_low)
    ranges = jnp.stack([low, inner_low, inner_high, high, q_first])

    n1, pre, q, kv = project_heads(
        x_block, heads_weight, gain_one[None, :], head_gains, cosine, sine
    )
    dy_block, kv, q = gather(
        "gather_keys",
        2,
        [(cotangent, 0, (0, 64))],
        [(kv, 0, (0, 512))],
        [q],
    )

    ob, o, totals = forward_attention(ranges, shift, q, first[:, None], kv)
    ob_own, h1_own, branch, gh1, gb, gain_two_term, go, g_gate, g_up, g_down = hidden_block(
        ob, wo, tokens, cotangent, gain_two[None, :], gate_up, down_piece, dy_block
    )
    by_core = lambda array: array.reshape(8, 2, -1, array.shape[-1])
    g_out = dot_tn(ob_own, gb).astype(BF16)
    gq, gkv = backward_attention(
        ranges, shift, q, go, o, totals, strip_first[:, None, :], kv
    )
    layer_out, gkv, g_out, g_gate, g_up, gq, g_down = scatter_keys(
        branch.reshape(seq_count, rows, width),
        h1_own,
        by_core(gkv),
        by_core(g_out),
        g_gate,
        g_up,
        gq,
        g_down,
    )
    gn1_partial, g_heads, gain_one_term, head_terms = heads_back(
        x_block, n1, pre, heads_weight, head_gains, cosine, sine, gq, gkv
    )
    gain_q_term = head_terms[0, :HD] + head_terms[0, HD:]
    gain_k_term = head_terms[1, :HD]
    g_heads = g_heads.reshape(fsdp_count, shard, -1)
    terms = jnp.concatenate(
        [
            gain_one_term.reshape(fsdp_count, shard),
            gain_two_term.reshape(fsdp_count, shard),
            gain_q_term.reshape(fsdp_count, qshard),
            gain_k_term.reshape(fsdp_count, qshard),
        ],
        axis=1,
    ).astype(BF16)
    terms = jnp.pad(terms[:, None, :], ((0, 0), (0, 15), (0, g_heads.shape[2] - terms.shape[1])))
    pack = jnp.concatenate([g_heads, terms], axis=1)
    input_grad, packs, g_down = scatter_input(
        gn1_partial.reshape(seq_count, rows, width),
        tokens,
        gain_one[None, :],
        gh1,
        pack.reshape((8, 2) + pack.shape[1:]),
        g_out.reshape(seq_count, -1, pack.shape[2]),
        g_down,
    )
    packs = packs.reshape(seq_count, -1, pack.shape[2])
    g_heads = packs[:, :shard]
    terms = jnp.sum(packs[:, shard].astype(F32), axis=0)
    g_out = packs[:, pack.shape[1] :].astype(F32).reshape(shard, width)
    g_down = g_down.reshape(seq_count, PIECE, width)[:, :pieces].reshape(-1, width)
    columns = lambda a: jnp.transpose(a.reshape(seq_count, shard, part), (1, 0, 2)).reshape(shard, hidden)

    g_query = jnp.transpose(g_heads[:, :, :per_head], (1, 0, 2)).reshape(shard, H * HD)
    g_key = jnp.transpose(g_heads[:, :, per_head : per_head + HD], (1, 0, 2)).reshape(shard, KVH * HD)
    g_value = jnp.transpose(g_heads[:, :, per_head + HD :], (1, 0, 2)).reshape(shard, KVH * HD)

    return (
        layer_out,
        input_grad,
        terms[:shard],
        terms[2 * shard : 2 * shard + qshard],
        terms[2 * shard + qshard : 2 * shard + 2 * qshard],
        g_query.astype(F32),
        g_key.astype(F32),
        g_value.astype(F32),
        g_out,
        terms[shard : 2 * shard],
        columns(g_gate).astype(F32),
        columns(g_up).astype(F32),
        g_down.astype(F32),
    )


def solution(mesh):
    rows = P(("fsdp", "seq"), None)
    matrix = P("fsdp", None)
    vector = P("fsdp")
    in_specs = (rows, P(), rows) + (vector,) * 3 + (matrix,) * 4 + (vector,) + (matrix,) * 3
    out_specs = (rows, rows) + (vector,) * 3 + (matrix,) * 4 + (vector,) + (matrix,) * 3
    return jax.shard_map(local, mesh=mesh, in_specs=in_specs, out_specs=out_specs, check_vma=False)
```

```python
import functools
import math

import jax
import jax.numpy as jnp
from jax import lax
from jax.experimental import pallas as pl
from jax.experimental.pallas import tpu as pltpu
from jax.sharding import PartitionSpec as P

H = 16
KVH = 8
HD = 64
DOCS = 4
EPSILON = 1e-06
THETA = 1000000.0
LOG2E = math.log2(math.e)
F32 = jnp.float32
BF16 = jnp.bfloat16
STRIP = 128
FEED = 256
KEYS = 1024
FORWARD_KEYS = 2048
VMEM = 56 * 1024 * 1024
PIECE = 48


def doc_starts(segments):
    labels = jnp.arange(DOCS, dtype=jnp.int32)
    member = (segments[None, :] == labels[:, None]).astype(jnp.int32)
    lengths = jnp.sum(member, axis=1)
    return jnp.cumsum(lengths) - lengths


def dot_nt(a, b):
    return lax.dot_general(a, b, (((1,), (1,)), ((), ())), preferred_element_type=F32)


def dot_tn(a, b):
    return lax.dot_general(a, b, (((0,), (0,)), ((), ())), preferred_element_type=F32)


def dot_nn(a, b):
    return jnp.dot(a, b, preferred_element_type=F32)


def key_loops(ranges_ref, tile, step):
    low, inner_low, inner_high, high = [ranges_ref[i, tile] for i in range(4)]

    def masked(block, _):
        step(block, True)
        return 0

    def plain(block, _):
        step(block, False)
        return 0

    lax.fori_loop(low, inner_low, masked, 0)
    lax.fori_loop(inner_low, inner_high, plain, 0)
    lax.fori_loop(inner_high, high, masked, 0)


def lanes_low(shape):
    return lax.broadcasted_iota(jnp.int32, shape, 1) < HD


def two_heads(packed, low):
    other = pltpu.roll(packed, HD, 1)
    heads = (packed, other) if low else (other, packed)
    keep = lanes_low(packed.shape) if low else ~lanes_low(packed.shape)
    return jnp.concatenate([jnp.where(keep, head, 0.0) for head in heads], axis=0)


def one_row(heads, low):
    rows = heads.shape[0] // 2
    first, second = heads[:rows], heads[rows:]
    if low:
        second = pltpu.roll(second, HD, 1)
    else:
        first = pltpu.roll(first, HD, 1)
    return jnp.where(lanes_low(first.shape), first, second)


def forward_kernel(
    ranges_ref, shift_ref, query_ref, first_ref, kv_ref, ob_ref, o_ref, totals_ref, total
):
    tile = pl.program_id(0)
    rows = query_ref.shape[0]
    query = two_heads(query_ref[...].astype(F32) * HD**-0.5, True).astype(BF16)
    first = jnp.concatenate([first_ref[...]] * 2, axis=0)
    index = ranges_ref[4, tile] + lax.broadcasted_iota(jnp.int32, (rows, 1), 0)
    index = jnp.concatenate([index, index], axis=0)
    shift = shift_ref[0]
    ones = jnp.ones((FORWARD_KEYS, 2 * HD), BF16)
    total[...] = jnp.zeros_like(total)

    def step(block, masked):
        start = pl.multiple_of(block * FORWARD_KEYS, FORWARD_KEYS)
        kv = kv_ref[pl.ds(start, FORWARD_KEYS), :]
        exps = jnp.exp2(dot_nt(query, kv) * LOG2E - shift)
        if masked:
            keys = start + lax.broadcasted_iota(jnp.int32, (2 * rows, FORWARD_KEYS), 1)
            exps = jnp.where((keys >= first) & (keys <= index), exps, 0.0)
        total[...] += dot_nn(exps.astype(BF16), jnp.concatenate([kv, ones], axis=1))

    key_loops(ranges_ref, tile, step)
    totals = total[:, 2 * HD :]
    o = total[:, : 2 * HD] / totals
    o_ref[0] = o
    totals_ref[0] = totals
    ob_ref[...] = one_row(o, False).astype(BF16)


def forward_attention(ranges, shift, query, first, kv):
    tiles = query.shape[0] // STRIP
    whole = lambda t, *_: (0, 0)
    part = lambda t, *_: (t, 0)
    wide = lambda t, *_: (t, 0, 0)
    return pl.pallas_call(
        forward_kernel,
        grid_spec=pltpu.PrefetchScalarGridSpec(
            num_scalar_prefetch=2,
            grid=(tiles,),
            in_specs=[
                pl.BlockSpec((STRIP, 2 * HD), part),
                pl.BlockSpec((STRIP, 1), part),
                pl.BlockSpec(kv.shape, whole),
            ],
            out_specs=[
                pl.BlockSpec((STRIP, 2 * HD), part),
                pl.BlockSpec((1, 2 * STRIP, 2 * HD), wide),
                pl.BlockSpec((1, 2 * STRIP, 2 * HD), wide),
            ],
            scratch_shapes=[pltpu.VMEM((2 * STRIP, 4 * HD), F32)],
        ),
        out_shape=[
            jax.ShapeDtypeStruct(query.shape, BF16),
            jax.ShapeDtypeStruct((tiles, 2 * STRIP, 2 * HD), F32),
            jax.ShapeDtypeStruct((tiles, 2 * STRIP, 2 * HD), F32),
        ],
        compiler_params=pltpu.CompilerParams(vmem_limit_bytes=VMEM),
        cost_estimate=pl.CostEstimate(
            flops=8 * 10**9, bytes_accessed=8 * 10**6, transcendentals=16 * 10**6
        ),
        name="attention_forward",
    )(ranges, shift, query, first, kv)


def backward_kernel(
    ranges_ref, shift_ref, query_ref, grad_ref, o_ref, totals_ref, first_ref, kv_ref,
    gq_ref, gkv_ref, total, gq,
):
    tile = pl.program_id(0)
    rows = query_ref.shape[0]
    query = two_heads(query_ref[...].astype(F32) * HD**-0.5, True).astype(BF16)
    go = two_heads(grad_ref[...].astype(F32), False)
    totals = totals_ref[0]
    grad = (go / totals).astype(BF16)
    delta = jnp.sum(go * o_ref[0], axis=1, keepdims=True) / totals
    delta = jnp.transpose(delta)[:1]
    both = jnp.concatenate([query, grad], axis=0)
    first = jnp.concatenate([first_ref[0]] * 2, axis=1)
    index = ranges_ref[4, tile] + lax.broadcasted_iota(jnp.int32, (1, rows), 1)
    index = jnp.concatenate([index, index], axis=1)
    shift = shift_ref[0]

    @pl.when(tile == 0)
    def _():
        total[...] = jnp.zeros_like(total)

    gq[...] = jnp.zeros_like(gq)

    def step(block, masked):
        start = pl.multiple_of(block * KEYS, KEYS)
        kv = kv_ref[pl.ds(start, KEYS), :]
        exps = jnp.exp2(dot_nt(kv, query) * LOG2E - shift)
        if masked:
            keys = start + lax.broadcasted_iota(jnp.int32, (KEYS, 2 * rows), 0)
            exps = jnp.where((keys >= first) & (keys <= index), exps, 0.0)
        scores = (exps * (dot_nt(kv, grad) - delta)).astype(BF16)
        gq[...] += dot_tn(scores, kv)
        total[pl.ds(start, KEYS), :] += dot_nn(
            jnp.concatenate([scores, exps.astype(BF16)], axis=1), both
        )

    key_loops(ranges_ref, tile, step)
    gq_ref[...] = (one_row(gq[...], True) * HD**-0.5).astype(BF16)

    @pl.when(tile == pl.num_programs(0) - 1)
    def _():
        gkv_ref[...] = total[...].astype(BF16)


def backward_attention(ranges, shift, query, grad, o, totals, first, kv):
    tiles = query.shape[0] // STRIP
    whole = lambda t, *_: (0, 0)
    part = lambda t, *_: (t, 0)
    wide = lambda t, *_: (t, 0, 0)
    return pl.pallas_call(
        backward_kernel,
        grid_spec=pltpu.PrefetchScalarGridSpec(
            num_scalar_prefetch=2,
            grid=(tiles,),
            in_specs=[
                pl.BlockSpec((STRIP, 2 * HD), part),
                pl.BlockSpec((STRIP, 2 * HD), part),
                pl.BlockSpec((1, 2 * STRIP, 2 * HD), wide),
                pl.BlockSpec((1, 2 * STRIP, 2 * HD), wide),
                pl.BlockSpec((1, 1, STRIP), wide),
                pl.BlockSpec(kv.shape, whole),
            ],
            out_specs=[
                pl.BlockSpec((STRIP, 2 * HD), part),
                pl.BlockSpec(kv.shape, whole),
            ],
            scratch_shapes=[pltpu.VMEM(kv.shape, F32), pltpu.VMEM((2 * STRIP, 2 * HD), F32)],
        ),
        out_shape=[
            jax.ShapeDtypeStruct(query.shape, BF16),
            jax.ShapeDtypeStruct(kv.shape, BF16),
        ],
        compiler_params=pltpu.CompilerParams(vmem_limit_bytes=VMEM),
        cost_estimate=pl.CostEstimate(
            flops=20 * 10**9, bytes_accessed=16 * 10**6, transcendentals=16 * 10**6
        ),
        name="attention_backward",
    )(ranges, shift, query, grad, o, totals, first, kv)


MESH = pl.DeviceIdType.MESH
HBM = pl.BlockSpec(memory_space=pl.ANY)
IN_VMEM = pl.BlockSpec(memory_space=pltpu.VMEM)
RING = 8


def pair_of(value):
    return value + 1 - 2 * lax.rem(value, 2)


def ring_step(index, steps):
    return lax.div(index, RING) * RING + lax.rem(lax.rem(index, RING) + 2 * steps, RING)


class Copies:
    def __init__(self, send, recv, local):
        self.send, self.recv, self.local = send, recv, local
        self.started, self.locals = [], []

    def remote(self, src, dst, peer, recv=None):
        i = len(self.started)
        copy = pltpu.make_async_remote_copy(
            src_ref=src,
            dst_ref=dst,
            send_sem=self.send.at[i],
            recv_sem=self.recv.at[i] if recv is None else recv,
            device_id=peer,
            device_id_type=MESH,
        )
        copy.start()
        self.started.append(copy)
        return copy

    def here(self, src, dst):
        copy = pltpu.make_async_copy(src, dst, self.local.at[len(self.locals)])
        copy.start()
        self.locals.append(copy)
        return copy

    def finish(self):
        for copy in self.started:
            copy.wait_send()


def greet(peers):
    barrier = pltpu.get_barrier_semaphore()
    for peer in peers:
        pl.semaphore_signal(barrier, inc=1, device_id=peer, device_id_type=MESH)
    pl.semaphore_wait(barrier, len(peers))


def slot(ref, axis, size, index, split=None, half=0):
    start = index * size
    where = [pl.ds(0, n) for n in ref.shape]
    where[axis] = pl.ds(pl.multiple_of(start, 16), size)
    if split is not None:
        along, cut = split
        whole = size if along == axis else ref.shape[along]
        base = start if along == axis else 0
        begin, count = (0, cut) if half == 0 else (cut, whole - cut)
        offset = base + begin
        where[along] = pl.ds(pl.multiple_of(offset, 16) if along == axis else offset, count)
    return ref.at[tuple(where)]


def gather_stages(copies, src, out, axis, size, split, me, pair, device, sibling):
    plus, minus = ring_step(me, 1), ring_step(me, 3)
    at = functools.partial(slot, out, axis, size)
    halves = lambda index, half: at(index, split, half)
    to_sibling = []

    def pass_on(index):
        if sibling is not None:
            to_sibling.append(copies.remote(at(index), at(index), device(sibling)))

    def piece(half):
        along, at_row = split
        where = [pl.ds(0, n) for n in src.shape]
        where[along] = pl.ds(0, at_row) if half == 0 else pl.ds(at_row, src.shape[along] - at_row)
        return src.at[tuple(where)]

    def forward(index, half, peer):
        return copies.remote(halves(index, half), halves(index, half), device(peer))

    kept = copies.here(src, at(me))
    first = [copies.remote(piece(half), halves(me, half), device(pair)) for half in (0, 1)]
    ways = ((0, plus), (1, minus), (1, plus), (0, minus))
    near = [copies.remote(piece(half), halves(me, half), device(peer)) for half, peer in ways]
    if sibling is not None:
        to_sibling.append(copies.remote(src, at(me), device(sibling)))
    yield
    near[0].wait_recv()
    far = [forward(minus, 0, plus)]
    near[1].wait_recv()
    far.append(forward(plus, 1, minus))
    near[2].wait_recv()
    pass_on(minus)
    near[3].wait_recv()
    pass_on(plus)
    yield
    first[0].wait_recv()
    up_low, down_low = forward(pair, 0, plus), forward(pair, 0, minus)
    first[1].wait_recv()
    down_high, up_high = forward(pair, 1, minus), forward(pair, 1, plus)
    pass_on(pair)
    yield
    shift = pair - me
    up_low.wait_recv()
    last = [forward(minus + shift, 0, plus)]
    down_high.wait_recv()
    last.append(forward(plus + shift, 1, minus))
    up_high.wait_recv()
    pass_on(minus + shift)
    down_low.wait_recv()
    pass_on(plus + shift)
    yield
    opposite = ring_step(me, 2)
    for copy in far:
        copy.wait_recv()
    pass_on(opposite)
    yield
    for copy in last:
        copy.wait_recv()
    pass_on(opposite + shift)
    yield
    for copy in to_sibling:
        copy.wait_recv()
    kept.wait()


def run_stages(stages):
    live = list(stages)
    while live:
        live = [stage for stage in live if next(stage, stage) is not stage]


class Swap:
    def __init__(self, copies, recv, sem, tag, stays, sends):
        self.copies, self.recv, self.tag, self.stays = copies, recv, tag, stays
        (src, dst, peer), rest = sends[0], sends[1:]
        self.own = pltpu.make_async_remote_copy(
            src_ref=src,
            dst_ref=dst,
            send_sem=sem.at[0],
            recv_sem=recv.at[tag],
            device_id=peer,
            device_id_type=MESH,
        )
        self.kept = pltpu.make_async_copy(src, dst, sem.at[1])

        @pl.when(stays)
        def _():
            self.kept.start()

        @pl.when(jnp.logical_not(stays))
        def _():
            self.own.start()

        self.sample = (src, dst, peer, sem)
        for src, dst, peer in rest:
            copies.remote(src, dst, peer, recv.at[tag])

    def wait(self, landing):
        src, _, peer, sem = self.sample
        for step in range(1, 8):
            sender = lax.rem(self.tag + step, 8)
            pltpu.make_async_remote_copy(
                src_ref=src,
                dst_ref=landing(sender),
                send_sem=sem.at[0],
                recv_sem=self.recv.at[sender],
                device_id=peer,
                device_id_type=MESH,
            ).wait_recv()

        @pl.when(self.stays)
        def _():
            self.kept.wait()

        @pl.when(jnp.logical_not(self.stays))
        def _():
            self.own.wait()


def greet_for_swaps(places, peers):
    barrier = pltpu.get_barrier_semaphore()
    senders, others = places.heads()[1], places.owners()[1]
    peers = peers + senders[1:] + others[1:]
    for peer in peers:
        pl.semaphore_signal(barrier, inc=1, device_id=peer, device_id_type=MESH)

    @pl.when(places.stays)
    def _():
        pl.semaphore_wait(barrier, len(peers))

    @pl.when(jnp.logical_not(places.stays))
    def _():
        for peer in (senders[0], others[0]):
            pl.semaphore_signal(barrier, inc=1, device_id=peer, device_id_type=MESH)
        pl.semaphore_wait(barrier, len(peers) + 2)


class Move:
    def __init__(self, src, dst, peer, stays, sem):
        self.stays = stays
        self.own = pltpu.make_async_remote_copy(
            src_ref=src,
            dst_ref=dst,
            send_sem=sem.at[0],
            recv_sem=sem.at[1],
            device_id=peer,
            device_id_type=MESH,
        )
        self.kept = pltpu.make_async_copy(src, dst, sem.at[2])

        @pl.when(stays)
        def _():
            self.kept.start()

        @pl.when(jnp.logical_not(stays))
        def _():
            self.own.start()

    def wait(self):
        @pl.when(self.stays)
        def _():
            self.kept.wait()

        @pl.when(jnp.logical_not(self.stays))
        def _():
            self.own.wait()


def greet_for_move(places, peers, sender):
    barrier = pltpu.get_barrier_semaphore()
    for peer in peers:
        pl.semaphore_signal(barrier, inc=1, device_id=peer, device_id_type=MESH)

    @pl.when(places.fixed)
    def _():
        pl.semaphore_wait(barrier, len(peers))

    @pl.when(jnp.logical_not(places.fixed))
    def _():
        pl.semaphore_signal(barrier, inc=1, device_id=sender, device_id_type=MESH)
        pl.semaphore_wait(barrier, len(peers) + 1)


def strips_at(ref, index):
    return ref.at[pl.ds(pl.multiple_of(index * STRIP, STRIP), STRIP), :]


def heads_at(ref, index):
    return ref.at[:, pl.ds(pl.multiple_of(index * 2 * HD, 2 * HD), 2 * HD)]


class Places:
    def __init__(self):
        self.seq, self.fsdp = lax.axis_index("seq"), lax.axis_index("fsdp")
        self.core = lax.rem(self.fsdp, 2)
        self.chip = lax.div(self.fsdp, 2)
        self.row = lax.div(self.chip, 4)
        self.col = lax.rem(self.chip, 4)
        self.sibling = pair_of(self.fsdp)
        self.across = lax.rem(self.fsdp + 8, 16)
        self.stays = self.chip == self.seq
        self.piece_to = (self.chip, self.core * 8 + self.seq)
        self.piece_from = (lax.rem(self.fsdp, 8), 2 * self.seq + lax.div(self.fsdp, 8))
        self.fixed = (self.chip == self.seq) & (self.core * 8 + self.seq == self.fsdp)

    def on_seq(self, index):
        return (index, self.fsdp)

    def on_fsdp(self, index):
        return (self.seq, index)

    def other_seq(self, step):
        return lax.rem(self.seq + step, 8)

    def other_chip(self, step):
        return lax.rem(self.row + step // 4, 2) * 4 + lax.rem(self.col + step % 4, 4)

    def gather_peers(self):
        seq = [pair_of(self.seq), ring_step(self.seq, 1), ring_step(self.seq, 3)]
        fsdp = [self.across, ring_step(self.fsdp, 1), ring_step(self.fsdp, 3), self.sibling]
        return [self.on_seq(i) for i in seq] + [self.on_fsdp(i) for i in fsdp]

    def strip_peers(self):
        return [self.on_fsdp(self.other_chip(d) * 2 + self.core) for d in range(1, 8)]

    def owners(self):
        strips = [lax.rem(self.chip + d, 8) for d in range(8)]
        return strips, [(self.chip, strip * 2 + self.core) for strip in strips]

    def heads(self):
        heads = [lax.rem(self.seq + d, 8) for d in range(8)]
        return heads, [(head, self.seq * 2 + self.core) for head in heads]


def params(name_id):
    return pltpu.CompilerParams(
        collective_id=name_id, has_side_effects=True, vmem_limit_bytes=VMEM
    )


def semaphores(remote, local):
    return [
        pltpu.SemaphoreType.DMA((remote,)),
        pltpu.SemaphoreType.DMA((remote,)),
        pltpu.SemaphoreType.DMA((local,)),
    ]


def seq_gather(copies, places, src, out, axis, split):
    size = src.shape[axis]
    return gather_stages(
        copies, src, out, axis, size, split, places.seq, pair_of(places.seq), places.on_seq, None
    )


def fsdp_gather(copies, places, src, out, axis, split):
    size = src.shape[axis]
    return gather_stages(
        copies, src, out, axis, size, split, places.fsdp, places.across, places.on_fsdp, places.sibling
    )


class Strips:
    def __init__(self, copies, places, src, out):
        self.kept = copies.here(strips_at(src, places.chip), strips_at(out, places.chip))
        self.copies = []
        for d in range(1, 8):
            chip = places.other_chip(d)
            peer = places.on_fsdp(chip * 2 + places.core)
            self.copies.append(copies.remote(strips_at(src, chip), strips_at(out, places.chip), peer))

    def wait(self):
        for copy in self.copies:
            copy.wait_recv()
        self.kept.wait()


def gather(name, name_id, seq_items, fsdp_items, strips=(), pieces=None):
    items = seq_items + fsdp_items
    count = len(items)
    every = count + len(strips)
    sources = [item[0] for item in items] + list(strips) + ([] if pieces is None else [pieces])

    def kernel(*refs):
        total = len(sources)
        srcs, outs, rest = refs[:total], refs[total : 2 * total], refs[2 * total :]
        copies, places = Copies(*rest[:3]), Places()
        peers = places.gather_peers() + (places.strip_peers() if strips else [])
        if pieces is None:
            greet(peers)
        else:
            greet_for_move(places, peers, places.piece_from)
        stages = []
        order = list(range(count))
        for i in order[::-1] if strips else order:
            _, axis, split = items[i]
            make = seq_gather if i < len(seq_items) else fsdp_gather
            stages.append(make(copies, places, srcs[i], outs[i], axis, split))
            next(stages[-1])
        moved = [Strips(copies, places, srcs[i], outs[i]) for i in range(count, every)]
        if pieces is not None:
            at = pl.ds(pl.multiple_of(places.seq * PIECE, 16), PIECE)
            moved.append(Move(srcs[-1].at[at], outs[-1], places.piece_to, places.fixed, rest[3]))
        run_stages(stages)
        for item in moved:
            item.wait()
        copies.finish()

    shapes = []
    for i, (array, axis, _) in enumerate(items):
        shape = list(array.shape)
        shape[axis] *= 8 if i < len(seq_items) else 16
        shapes.append(jax.ShapeDtypeStruct(tuple(shape), array.dtype))
    shapes += [jax.ShapeDtypeStruct(array.shape, array.dtype) for array in strips]
    extra = []
    if pieces is not None:
        shapes.append(jax.ShapeDtypeStruct((PIECE,) + pieces.shape[1:], pieces.dtype))
        extra = [pltpu.SemaphoreType.DMA((3,))]
    remote = 14 * len(seq_items) + 22 * len(fsdp_items) + 7 * len(strips)
    return pl.pallas_call(
        kernel,
        out_shape=shapes,
        in_specs=[HBM] * len(sources),
        out_specs=[HBM] * len(sources),
        scratch_shapes=semaphores(remote, every) + extra,
        compiler_params=params(name_id),
        name=name,
    )(*sources)


class RingSum:
    def __init__(self, copies, near, mine, held, cut, index, device):
        self.remote, self.mine, self.device = copies.remote, mine, device
        self.half, self.ring, self.other = held
        self.cut, self.index = cut, index
        self.plus, self.minus, self.pair = near

    def parts(self):
        rows = self.mine.shape[1]
        return pl.ds(0, self.cut), pl.ds(self.cut, rows - self.cut)

    def send(self):
        low, high = self.parts()
        self.first, self.second = [], []
        for flip in (1, 0):
            far, up, down = [self.mine.at[self.index(flip, step)] for step in (2, 1, 3)]
            self.prepare(flip, 2)
            self.first.append(
                (
                    self.remote(far.at[low], self.half.at[flip, low], self.plus),
                    self.remote(far.at[high], self.half.at[flip, high], self.minus),
                )
            )
            self.prepare(flip, 1)
            self.prepare(flip, 3)
            self.second.append(
                [
                    self.remote(up.at[high], self.ring.at[flip, 0, high], self.plus),
                    self.remote(down.at[low], self.ring.at[flip, 1, low], self.minus),
                ]
            )

    def relay(self):
        low, high = self.parts()
        for i, flip in enumerate((1, 0)):
            for copy, step, part, way, peer in (
                (self.first[i][0], 1, low, 0, self.plus),
                (self.first[i][1], 3, high, 1, self.minus),
            ):
                copy.wait_recv()
                at = self.index(flip, step)
                self.mine[at, part] = (
                    self.mine[at, part].astype(F32) + self.half[flip, part].astype(F32)
                ).astype(BF16)
                self.second[i].append(
                    self.remote(self.mine.at[at, part], self.ring.at[flip, way, part], peer)
                )

    def prepare(self, flip, step):
        pass

    def gathered(self, i, flip):
        self.prepare(flip, 0)
        for copy in self.second[i]:
            copy.wait_recv()
        return (
            self.mine[self.index(flip, 0)].astype(F32)
            + self.ring[flip, 0].astype(F32)
            + self.ring[flip, 1].astype(F32)
        )

    def cross(self):
        self.other[0] = self.gathered(0, 1).astype(BF16)
        self.last = self.remote(self.other.at[0], self.other.at[1], self.pair)

    def total(self):
        total = self.gathered(1, 0)
        self.last.wait_recv()
        return total + self.other[1].astype(F32)


def ring_buffers(shape):
    return [
        pltpu.VMEM((2,) + shape, BF16),
        pltpu.VMEM((2, 2) + shape, BF16),
        pltpu.VMEM((2,) + shape, BF16),
    ]


RING_COPIES = 13


class SeqSum(RingSum):
    def __init__(self, copies, places, part, buffers, cut):
        mine, held = buffers[0], buffers[1:]
        seq = places.seq

        def index(flip, step):
            base = ring_step(seq, step)
            return pair_of(base) if flip else base

        near = [places.on_seq(i) for i in (ring_step(seq, 1), ring_step(seq, 3), pair_of(seq))]
        super().__init__(copies, near, mine, held, cut, index, places.on_seq)
        self.kept = copies.here(part, mine)

    def ready(self):
        self.kept.wait()


class FsdpSum(RingSum):
    def __init__(self, copies, places, part, buffers, cut):
        mine, self.theirs, held = buffers[0], buffers[1], buffers[2:]
        fsdp = places.fsdp

        def index(flip, step):
            return lax.rem(places.row + flip, 2) * 4 + lax.rem(places.col + step, 4)

        near = [places.on_fsdp(i) for i in (ring_step(fsdp, 1), ring_step(fsdp, 3), places.across)]
        super().__init__(copies, near, mine, held, cut, index, places.on_fsdp)
        self.others = {
            (flip, step): copies.remote(
                part.at[index(flip, step), 1 - places.core],
                self.theirs.at[index(flip, step)],
                places.on_fsdp(places.sibling),
            )
            for flip in (1, 0)
            for step in (2, 1, 3, 0)
        }
        self.kept = copies.here(part.at[:, places.core], mine)

    def ready(self):
        self.kept.wait()

    def prepare(self, flip, step):
        self.others[flip, step].wait_recv()
        at = self.index(flip, step)
        self.mine[at] = (self.mine[at].astype(F32) + self.theirs[at].astype(F32)).astype(BF16)


def seq_buffers(shape):
    return [pltpu.VMEM((8,) + shape, BF16)] + ring_buffers(shape)


def fsdp_buffers(shape):
    return [pltpu.VMEM((8,) + shape, BF16)] * 2 + ring_buffers(shape)


SEQ_COPIES = RING_COPIES
FSDP_COPIES = RING_COPIES + 8


def unit_rows(values):
    return lax.rsqrt(jnp.mean(values * values, axis=-1, keepdims=True) + EPSILON)


def spread(pieces, part):
    shape = (pieces * PIECE, part)
    row = lax.broadcasted_iota(jnp.int32, shape, 0)
    column = lax.broadcasted_iota(jnp.int32, shape, 1)
    size = part // pieces
    inside = lax.rem(row, PIECE)
    hit = (lax.div(row, PIECE) * size + inside == column) & (inside < size)
    return jnp.where(hit, 1.0, 0.0).astype(BF16)


def hidden_kernel(
    ob, wo, tokens, dy_own, gain, gate_up, down, dy,
    own_ref, h1_ref, branch_ref, gh1_ref, gb_ref, term_ref, go_ref, gate_out, up_out, down_out,
    own, n2, go_own, n2_all, weights, down_pad, down_all, act, ggate, gup, gn2_all, held,
    gate_part, up_part, down_part, *scratch,
):
    sums_at = scratch[:15]
    tags, ends, tags_back, ends_back = scratch[15:19]
    copies, places = Copies(*scratch[19:]), Places()
    others = [places.on_seq(places.other_seq(d)) for d in range(1, 8)]
    greet_for_swaps(places, places.gather_peers() + others)
    rows, width = own.shape
    part = down_all.shape[0]
    pieces = down_pad.shape[0] // PIECE

    strips, owners = places.owners()
    heads, workers = places.heads()
    landing = heads_at(own, places.seq)
    sends = [(strips_at(ob, strip), landing, peer) for strip, peer in zip(strips, owners)]
    swap = Swap(copies, tags, ends, places.seq, places.stays, sends)
    gathers = [
        fsdp_gather(copies, places, gate_up, weights, 1, (1, 32)),
        fsdp_gather(copies, places, down, down_pad, 0, (0, 32)),
    ]
    for stage in gathers:
        next(stage)
    swap.wait(lambda sender: heads_at(own, sender))
    own_ref[...] = own[...]

    def project(j, _):
        at = pl.ds(pl.multiple_of(j * 256, 256), 256)
        h1_ref[:, at] = tokens[:, at].astype(F32) + dot_nn(own[...], wo[:, at])
        return 0

    lax.fori_loop(0, width // 256, project, 0)
    value = h1_ref[...]
    inverse = unit_rows(value)
    n2[...] = (value * inverse * gain[...]).astype(BF16)
    tokens_in = seq_gather(copies, places, n2, n2_all, 0, (0, 64))
    next(tokens_in)
    for _ in range(3):
        for stage in gathers:
            next(stage)
        if _ < 2:
            next(tokens_in)
    run_stages(gathers)
    matrix = spread(pieces, part)

    def pack_down(j, _):
        at = pl.ds(pl.multiple_of(j * 256, 256), 256)
        down_all[:, at] = dot_tn(matrix, down_pad[:, at]).astype(BF16)
        return 0

    lax.fori_loop(0, width // 256, pack_down, 0)

    arrivals = []

    def feed(step):
        base = lax.div(ring_step(places.seq, step), 2) * 2 * rows
        at = pl.ds(pl.multiple_of(base, 2 * rows), 2 * rows)
        values = n2_all[at, :]
        gate = dot_nn(values, weights[0])
        up = dot_nn(values, weights[1])
        gact = dot_nt(dy[at, :], down_all[...])
        sig = jax.nn.sigmoid(gate)
        silu = gate * sig
        act_here = (silu * up).astype(BF16)
        gg = (gact * up * sig * (1.0 + gate * (1.0 - sig))).astype(BF16)
        gu = (gact * silu).astype(BF16)
        act[at, :] = act_here
        ggate[at, :] = gg
        gup[at, :] = gu
        gn2_all[at, :] = (dot_nt(gg, weights[0]) + dot_nt(gu, weights[1])).astype(BF16)
        for flip in (1, 0):
            if step == 0 and flip == 0:
                continue
            peer = ring_step(places.seq, step)
            peer = pair_of(peer) if flip else peer
            arrivals.append(
                copies.remote(
                    gn2_all.at[pl.ds(pl.multiple_of(peer * rows, rows), rows), :],
                    held.at[2 * step + flip],
                    places.on_seq(peer),
                )
            )
        branch_ref[at, :] = dot_nn(act_here, down_all[...]).astype(BF16)

    tokens_in.send(None)
    kept_first = copies.locals[-1]
    kept_first.wait()
    feed(0)
    feed(1)
    feed(3)
    next(tokens_in)
    next(tokens_in)
    feed(2)

    sums = []

    def weight_sum(c, part_ref, grads):
        at = pl.ds(pl.multiple_of(c * 256, 256), 256)
        shape = (2, 2) + part_ref.shape[2:]
        part_ref[pl.ds(c * 2, 2)] = dot_tn(n2_all[:, at], grads[...]).astype(BF16).reshape(shape)
        return 0

    def down_sum(c, _):
        at = pl.ds(pl.multiple_of(c * 256, 256), 256)
        g_down = dot_nn(matrix, dot_tn(act[...], dy[:, at]).astype(BF16)).astype(BF16)
        down_part[:, :, :, at] = g_down.reshape((8, 2, PIECE, 256))
        return 0

    lax.fori_loop(0, width // 256, lambda c, _: weight_sum(c, gate_part, ggate), 0)
    sums.append(FsdpSum(copies, places, gate_part, sums_at[:5], 32))
    lax.fori_loop(0, width // 256, lambda c, _: weight_sum(c, up_part, gup), 0)
    sums.append(FsdpSum(copies, places, up_part, sums_at[5:10], 32))
    sums[0].ready()
    sums[0].send()
    lax.fori_loop(0, width // 256, down_sum, 0)
    sums.append(FsdpSum(copies, places, down_part, sums_at[10:15], 32))
    for item in sums[1:]:
        item.ready()
        item.send()
    for item in sums:
        item.relay()
    gn2 = gn2_all[pl.ds(pl.multiple_of(places.seq * rows, rows), rows), :].astype(F32)
    for copy in arrivals:
        copy.wait_recv()
    for slot_index in range(1, 8):
        gn2 += held[slot_index].astype(F32)
    value = h1_ref[...]
    inverse = unit_rows(value)
    normed = value * inverse
    term_ref[...] = jnp.sum(gn2 * normed, axis=0, keepdims=True)
    weighted = gn2 * gain[...]
    inner = jnp.mean(weighted * normed, axis=-1, keepdims=True)
    gh1 = dy_own[...].astype(F32) + inverse * (weighted - normed * inner)
    gh1_ref[...] = gh1
    gb_ref[...] = gh1.astype(BF16)

    def project_back(j, _):
        begin = pl.multiple_of(j * 256, 256)
        go_own[:, pl.ds(begin, 256)] = dot_nt(gb_ref[...], wo[pl.ds(begin, 256), :]).astype(BF16)
        return 0

    lax.fori_loop(0, width // 256, project_back, 0)
    landing = strips_at(go_ref, places.chip)
    sends = [(heads_at(go_own, head), landing, peer) for head, peer in zip(heads, workers)]
    swap_back = Swap(copies, tags_back, ends_back, places.chip, places.stays, sends)
    for item in sums:
        item.cross()
    for item, out in zip(sums, (gate_out, up_out, down_out)):
        out[...] = item.total().astype(BF16)
    swap_back.wait(lambda sender: strips_at(go_ref, sender))
    copies.finish()


def hidden_block(ob, wo, tokens, dy_own, gain, gate_up, down, dy):
    rows, width = tokens.shape
    shard, part = gate_up.shape[1:]
    slices = [(shard, part), (shard, part), (PIECE, width)]
    block = (8 * rows, width)
    vmem = [(rows, width)] * 3 + [block, (2, width, part), (16 * PIECE, width), (part, width)]
    vmem += [(8 * rows, part)] * 3 + [block, (8, rows, width)]
    vmem += [(8, 2) + shape for shape in slices]
    scratch = [pltpu.VMEM(shape, BF16) for shape in vmem]
    for shape in slices:
        scratch += fsdp_buffers(shape)
    scratch += [pltpu.SemaphoreType.DMA((n,)) for n in (8, 2, 8, 2)]
    return pl.pallas_call(
        hidden_kernel,
        out_shape=[
            jax.ShapeDtypeStruct((rows, width), BF16),
            jax.ShapeDtypeStruct((rows, width), F32),
            jax.ShapeDtypeStruct(block, BF16),
            jax.ShapeDtypeStruct((rows, width), F32),
            jax.ShapeDtypeStruct((rows, width), BF16),
            jax.ShapeDtypeStruct((1, width), F32),
            jax.ShapeDtypeStruct((8 * rows, 128), BF16),
        ]
        + [jax.ShapeDtypeStruct(shape, BF16) for shape in slices],
        in_specs=[HBM] + [IN_VMEM] * 4 + [HBM] * 2 + [IN_VMEM],
        out_specs=[IN_VMEM] * 6 + [HBM] + [IN_VMEM] * 3,
        scratch_shapes=scratch + semaphores(2 * 7 + 14 + 2 * 22 + 7 + 3 * FSDP_COPIES, 6),
        compiler_params=params(4),
        name="scatter_hidden_block",
    )(ob, wo, tokens, dy_own, gain, gate_up, down, dy)


def keys_kernel(
    branch, h1, gkv, gout, gate, up, gq, down,
    layer_ref, gkv_out, gout_out, gate_all, up_all, gq_out, down_out, ends,
    *scratch,
):
    copies, places = Copies(*scratch[14:]), Places()
    greet_for_move(places, places.gather_peers() + places.strip_peers(), places.piece_to)
    moved = Move(down, down_out, places.piece_from, places.fixed, ends)
    stages = [
        seq_gather(copies, places, gate, gate_all, 0, (0, 32)),
        seq_gather(copies, places, up, up_all, 0, (0, 32)),
    ]
    for stage in stages:
        next(stage)
    sums = [
        FsdpSum(copies, places, gkv, scratch[4:9], 512),
        FsdpSum(copies, places, gout, scratch[9:14], 32),
    ]
    hidden = SeqSum(copies, places, branch, scratch[:4], 64)
    items = [hidden] + sums
    for item in items:
        item.ready()
        item.send()
    strips = Strips(copies, places, gq, gq_out)
    for _ in range(2):
        for stage in stages:
            next(stage)
    hidden.relay()
    for item in sums:
        item.relay()
    for stage in stages:
        next(stage)
    for item in items:
        item.cross()
    run_stages(stages)
    for item, out in zip(sums, (gkv_out, gout_out)):
        out[...] = item.total().astype(BF16)
    layer_ref[...] = (h1[...] + hidden.total()).astype(BF16)
    strips.wait()
    moved.wait()
    copies.finish()


def scatter_keys(branch, h1, gkv, gout, gate, up, gq, down):
    rows, width = h1.shape
    shapes = [a.shape[2:] for a in (gkv, gout)]
    scratch = [pltpu.SemaphoreType.DMA((3,))] + seq_buffers((rows, width))
    for shape in shapes:
        scratch += fsdp_buffers(shape)
    wide = [jax.ShapeDtypeStruct((8 * a.shape[0],) + a.shape[1:], BF16) for a in (gate, up)]
    return pl.pallas_call(
        keys_kernel,
        out_shape=[jax.ShapeDtypeStruct((rows, width), BF16)]
        + [jax.ShapeDtypeStruct(shape, BF16) for shape in shapes]
        + wide
        + [jax.ShapeDtypeStruct(gq.shape, BF16), jax.ShapeDtypeStruct(down.shape, BF16)],
        in_specs=[HBM, IN_VMEM] + [HBM] * 6,
        out_specs=[IN_VMEM] * 3 + [HBM] * 4,
        scratch_shapes=scratch + semaphores(SEQ_COPIES + 2 * FSDP_COPIES + 28 + 7, 6),
        compiler_params=params(5),
        name="scatter_keys",
    )(branch, h1, gkv, gout, gate, up, gq, down)


def input_kernel(
    part, tokens, gain, gh1, pack, gout, down,
    grad_ref, pack_all, down_all,
    small, gathered, *scratch,
):
    copies, places = Copies(*scratch[9:]), Places()
    steps = range(1, 8)
    greet(places.gather_peers() + [places.on_seq(places.other_seq(d)) for d in steps])
    packs = FsdpSum(copies, places, pack, scratch[4:9], 48)
    stages = [seq_gather(copies, places, down, down_all, 0, (0, 16))]
    next(stages[0])
    outs = [
        copies.remote(
            gout.at[places.other_seq(d)], gathered.at[d], places.on_seq(places.other_seq(d))
        )
        for d in steps
    ]
    own = copies.here(gout.at[places.seq], gathered.at[0])
    hidden = SeqSum(copies, places, part, scratch[:4], 64)
    packs.ready()
    packs.send()
    hidden.ready()
    hidden.send()
    next(stages[0])
    packs.relay()
    next(stages[0])
    packs.cross()
    own.wait()
    for copy in outs:
        copy.wait_recv()
    rows = pack.shape[2]
    total = gathered[0].astype(F32)
    for d in steps:
        total += gathered[d].astype(F32)
    small[rows:] = total.astype(BF16)
    small[:rows] = packs.total().astype(BF16)
    stages.append(seq_gather(copies, places, small, pack_all, 0, (0, 64)))
    next(stages[1])
    hidden.relay()
    next(stages[0])
    next(stages[1])
    next(stages[1])
    hidden.cross()
    run_stages(stages)
    gn1 = hidden.total()
    value = tokens[...].astype(F32)
    inverse = unit_rows(value)
    normed = value * inverse
    weighted = gn1 * gain[...]
    inner = jnp.mean(weighted * normed, axis=-1, keepdims=True)
    grad_ref[...] = gh1[...] + inverse * (weighted - normed * inner)
    copies.finish()


def scatter_input(part, tokens, gain, gh1, pack, gout, down):
    rows, width = gh1.shape
    shape = pack.shape[2:]
    small = (shape[0] + gout.shape[1], shape[1])
    return pl.pallas_call(
        input_kernel,
        out_shape=[
            jax.ShapeDtypeStruct((rows, width), F32),
            jax.ShapeDtypeStruct((8 * small[0], small[1]), BF16),
            jax.ShapeDtypeStruct((8 * down.shape[0], width), BF16),
        ],
        in_specs=[HBM] + [IN_VMEM] * 3 + [HBM] * 3,
        out_specs=[IN_VMEM] + [HBM] * 2,
        scratch_shapes=[pltpu.VMEM(small, BF16), pltpu.VMEM(gout.shape, BF16)]
        + seq_buffers((rows, width))
        + fsdp_buffers(shape)
        + semaphores(SEQ_COPIES + FSDP_COPIES + 28 + 7, 5),
        compiler_params=params(6),
        name="scatter_input",
    )(part, tokens, gain, gh1, pack, gout, down)


def swap_halves(values):
    lane = lax.broadcasted_iota(jnp.int32, values.shape, 1)
    ahead, behind = pltpu.roll(values, 2 * HD - HD // 2, 1), pltpu.roll(values, HD // 2, 1)
    return jnp.where(lax.rem(lane, HD) < HD // 2, ahead, behind)


def head_means(values):
    low = lanes_low(values.shape)
    first = jnp.sum(jnp.where(low, values, 0.0), axis=1, keepdims=True)
    second = jnp.sum(jnp.where(low, 0.0, values), axis=1, keepdims=True)
    return jnp.where(low, first, second) * (1.0 / HD)


def heads_kernel(x_ref, weight_ref, gain_ref, gains_ref, cos_ref, sin_ref, n1_ref, pre_ref, q_ref, kv_ref):
    def tokens(t, _):
        at = pl.ds(pl.multiple_of(t * 256, 256), 256)
        x = x_ref[at, :].astype(F32)
        n1 = (x * unit_rows(x) * gain_ref[...]).astype(BF16)
        n1_ref[at, :] = n1
        pre = dot_nn(n1, weight_ref[...])
        pre_ref[at, :] = pre
        cosine, sine = cos_ref[at, :], sin_ref[at, :]
        outs = []
        for part in (0, 1):
            values = pre[:, part * 2 * HD : (part + 1) * 2 * HD]
            inverse = lax.rsqrt(head_means(values * values) + EPSILON)
            normed = values * inverse * gains_ref[part : part + 1, :]
            outs.append(normed * cosine + swap_halves(normed) * sine)
        q_ref[at, :] = outs[0].astype(BF16)
        kv_ref[at, :] = jnp.where(lanes_low(outs[1].shape), outs[1], pre[:, 2 * HD :]).astype(BF16)
        return 0

    lax.fori_loop(0, x_ref.shape[0] // 256, tokens, 0)


def project_heads(x, weight, gain, gains, cosine, sine):
    count, width = x.shape
    return pl.pallas_call(
        heads_kernel,
        out_shape=[
            jax.ShapeDtypeStruct((count, width), BF16),
            jax.ShapeDtypeStruct((count, 4 * HD), F32),
            jax.ShapeDtypeStruct((count, 2 * HD), BF16),
            jax.ShapeDtypeStruct((count, 2 * HD), BF16),
        ],
        in_specs=[IN_VMEM] * 6,
        out_specs=[IN_VMEM] * 4,
        compiler_params=pltpu.CompilerParams(vmem_limit_bytes=VMEM),
        name="project_heads",
    )(x, weight, gain, gains, cosine, sine)


def heads_back_kernel(
    x_ref, n1_ref, pre_ref, weight_ref, gains_ref, cos_ref, sin_ref, gq_ref, gkv_ref,
    gn1_ref, gheads_ref, gain_ref, terms_ref, gpre_ref,
):
    count, width = x_ref.shape
    gain_ref[...] = jnp.zeros_like(gain_ref)
    terms_ref[...] = jnp.zeros_like(terms_ref)

    def tokens(t, _):
        at = pl.ds(pl.multiple_of(t * 256, 256), 256)
        cosine, sine = cos_ref[at, :], sin_ref[at, :]
        for part, ref in ((0, gq_ref), (1, gkv_ref)):
            columns = pl.ds(part * 2 * HD, 2 * HD)
            grads = ref[at, :].astype(F32)
            values = pre_ref[at, columns]
            inverse = lax.rsqrt(head_means(values * values) + EPSILON)
            normed = values * inverse
            turned = grads * cosine - swap_halves(grads) * sine
            terms_ref[part : part + 1, :] += jnp.sum(turned * normed, axis=0, keepdims=True)
            weighted = turned * gains_ref[part : part + 1, :]
            back = inverse * (weighted - normed * head_means(weighted * normed))
            if part == 1:
                back = jnp.where(lanes_low(back.shape), back, grads)
            gpre_ref[at, columns] = back.astype(BF16)
        gn1 = dot_nt(gpre_ref[at, :], weight_ref[...])
        gn1_ref[at, :] = gn1.astype(BF16)
        x = x_ref[at, :].astype(F32)
        gain_ref[...] += jnp.sum(gn1 * (x * unit_rows(x)), axis=0, keepdims=True)
        return 0

    lax.fori_loop(0, count // 256, tokens, 0)

    def columns(c, _):
        at = pl.ds(pl.multiple_of(c * 256, 256), 256)
        gheads_ref[at, :] = dot_tn(n1_ref[:, at], gpre_ref[...]).astype(BF16)
        return 0

    lax.fori_loop(0, width // 256, columns, 0)


def heads_back(x, n1, pre, weight, gains, cosine, sine, gq, gkv):
    count, width = x.shape
    return pl.pallas_call(
        heads_back_kernel,
        out_shape=[
            jax.ShapeDtypeStruct((count, width), BF16),
            jax.ShapeDtypeStruct((width, 4 * HD), BF16),
            jax.ShapeDtypeStruct((1, width), F32),
            jax.ShapeDtypeStruct((2, 2 * HD), F32),
        ],
        in_specs=[IN_VMEM] * 9,
        out_specs=[IN_VMEM] * 4,
        scratch_shapes=[pltpu.VMEM((count, 4 * HD), BF16)],
        compiler_params=pltpu.CompilerParams(vmem_limit_bytes=VMEM),
        name="heads_back",
    )(x, n1, pre, weight, gains, cosine, sine, gq, gkv)


def local(
    tokens,
    segments,
    cotangent,
    attention_gain,
    query_gain,
    key_gain,
    query_weight,
    key_weight,
    value_weight,
    out_weight,
    feedforward_gain,
    gate_weight,
    up_weight,
    down_weight,
):
    seq_count = lax.axis_size("seq")
    fsdp_count = lax.axis_size("fsdp")
    fsdp = lax.axis_index("fsdp")
    seq = lax.axis_index("seq")
    rows, width = tokens.shape
    block = rows * seq_count
    hidden = gate_weight.shape[1]
    part = hidden // seq_count
    per_head = (H // KVH) * HD
    block_start = fsdp * block
    take = lax.dynamic_slice_in_dim

    gains = jnp.concatenate([attention_gain, feedforward_gain, query_gain, key_gain])
    heads_weight = jnp.concatenate(
        [
            take(query_weight, seq * per_head, per_head, 1),
            take(key_weight, seq * HD, HD, 1),
            take(value_weight, seq * HD, HD, 1),
        ],
        axis=1,
    )
    gains = jnp.pad(gains[None, :], ((0, 15), (0, heads_weight.shape[1] - gains.shape[0])))
    pieces = down_weight.shape[0] // seq_count
    down_pieces = jnp.pad(
        down_weight.reshape(seq_count, pieces, width), ((0, 0), (0, PIECE - pieces), (0, 0))
    ).reshape(-1, width)
    gate_up = jnp.stack(
        [take(gate_weight, seq * part, part, 1), take(up_weight, seq * part, part, 1)]
    )
    x_block, packs, wo, down_piece = gather(
        "gather_inputs",
        1,
        [(tokens, 0, (0, 64))],
        [(jnp.concatenate([heads_weight, gains]), 0, (0, 48)), (out_weight, 0, (0, 32))],
        pieces=down_pieces,
    )
    packs = packs.reshape(fsdp_count, -1, packs.shape[1])
    heads_weight = packs[:, : width // fsdp_count].reshape(width, -1)
    gains = packs[:, width // fsdp_count].astype(F32)

    shard = width // fsdp_count
    gain_one = gains[:, :shard].reshape(width)
    gain_two = gains[:, shard : 2 * shard].reshape(width)
    qshard = HD // fsdp_count
    gain_q = gains[:, 2 * shard : 2 * shard + qshard].reshape(HD)
    gain_k = gains[:, 2 * shard + qshard : 2 * shard + 2 * qshard].reshape(HD)

    starts = doc_starts(segments)
    labels = jnp.arange(DOCS, dtype=jnp.int32)

    def firsts(ids):
        picked = (ids[:, None] == labels[None, :]).astype(jnp.int32)
        return jnp.sum(picked * starts[None, :], axis=1)

    index = block_start + jnp.arange(block, dtype=jnp.int32)
    positions = index - firsts(take(segments, block_start, block))
    freqs = THETA ** (-2.0 * jnp.arange(HD // 2, dtype=F32) / HD)
    angles = positions.astype(F32)[:, None] * jnp.tile(freqs, 4)[None, :]
    side = jnp.tile(jnp.repeat(jnp.array([-1.0, 1.0], F32), HD // 2), 2)
    cosine, sine = jnp.cos(angles), jnp.sin(angles) * side[None, :]
    head_gains = jnp.stack([jnp.tile(gain_q, 2), jnp.tile(gain_k, 2)])
    shift = (HD**0.5 * LOG2E) * jnp.max(jnp.abs(gain_q)) * jnp.max(jnp.abs(gain_k))
    shift = shift.reshape(1)

    core, chip = fsdp % 2, fsdp // 2
    strip_ids = segments.reshape(fsdp_count // 2, 2, block // STRIP, STRIP)
    strip_ids = lax.dynamic_index_in_dim(strip_ids, core, 1, keepdims=False)
    strip_ids = lax.dynamic_index_in_dim(strip_ids, chip, 1, keepdims=False)
    first = firsts(strip_ids.reshape(-1))
    strip_first = first.reshape(-1, STRIP)
    q_first = (2 * jnp.arange(fsdp_count // 2, dtype=jnp.int32) + core) * block + chip * STRIP

    def key_ranges(size):
        low = strip_first[:, 0] // size
        high = (q_first + STRIP - 1) // size + 1
        inner_low = jnp.minimum((strip_first[:, STRIP - 1] + size - 1) // size, high)
        inner_high = jnp.maximum((q_first + 1) // size, inner_low)
        return jnp.stack([low, inner_low, inner_high, high, q_first])

    n1, pre, q, kv = project_heads(
        x_block, heads_weight, gain_one[None, :], head_gains, cosine, sine
    )
    dy_block, kv, q = gather(
        "gather_keys",
        2,
        [(cotangent, 0, (0, 64))],
        [(kv, 0, (0, 512))],
        [q],
    )

    ob, o, totals = forward_attention(key_ranges(FORWARD_KEYS), shift, q, first[:, None], kv)
    ob_own, h1_own, branch, gh1, gb, gain_two_term, go, g_gate, g_up, g_down = hidden_block(
        ob, wo, tokens, cotangent, gain_two[None, :], gate_up, down_piece, dy_block
    )
    by_core = lambda array: array.reshape(8, 2, -1, array.shape[-1])
    g_out = dot_tn(ob_own, gb).astype(BF16)
    gq, gkv = backward_attention(
        key_ranges(KEYS), shift, q, go, o, totals, strip_first[:, None, :], kv
    )
    layer_out, gkv, g_out, g_gate, g_up, gq, g_down = scatter_keys(
        branch.reshape(seq_count, rows, width),
        h1_own,
        by_core(gkv),
        by_core(g_out),
        g_gate,
        g_up,
        gq,
        g_down,
    )
    gn1_partial, g_heads, gain_one_term, head_terms = heads_back(
        x_block, n1, pre, heads_weight, head_gains, cosine, sine, gq, gkv
    )
    gain_q_term = head_terms[0, :HD] + head_terms[0, HD:]
    gain_k_term = head_terms[1, :HD]
    g_heads = g_heads.reshape(fsdp_count, shard, -1)
    terms = jnp.concatenate(
        [
            gain_one_term.reshape(fsdp_count, shard),
            gain_two_term.reshape(fsdp_count, shard),
            gain_q_term.reshape(fsdp_count, qshard),
            gain_k_term.reshape(fsdp_count, qshard),
        ],
        axis=1,
    ).astype(BF16)
    terms = jnp.pad(terms[:, None, :], ((0, 0), (0, 15), (0, g_heads.shape[2] - terms.shape[1])))
    pack = jnp.concatenate([g_heads, terms], axis=1)
    input_grad, packs, g_down = scatter_input(
        gn1_partial.reshape(seq_count, rows, width),
        tokens,
        gain_one[None, :],
        gh1,
        pack.reshape((8, 2) + pack.shape[1:]),
        g_out.reshape(seq_count, -1, pack.shape[2]),
        g_down,
    )
    packs = packs.reshape(seq_count, -1, pack.shape[2])
    g_heads = packs[:, :shard]
    terms = jnp.sum(packs[:, shard].astype(F32), axis=0)
    g_out = packs[:, pack.shape[1] :].astype(F32).reshape(shard, width)
    g_down = g_down.reshape(seq_count, PIECE, width)[:, :pieces].reshape(-1, width)
    columns = lambda a: jnp.transpose(a.reshape(seq_count, shard, part), (1, 0, 2)).reshape(shard, hidden)

    g_query = jnp.transpose(g_heads[:, :, :per_head], (1, 0, 2)).reshape(shard, H * HD)
    g_key = jnp.transpose(g_heads[:, :, per_head : per_head + HD], (1, 0, 2)).reshape(shard, KVH * HD)
    g_value = jnp.transpose(g_heads[:, :, per_head + HD :], (1, 0, 2)).reshape(shard, KVH * HD)

    return (
        layer_out,
        input_grad,
        terms[:shard],
        terms[2 * shard : 2 * shard + qshard],
        terms[2 * shard + qshard : 2 * shard + 2 * qshard],
        g_query.astype(F32),
        g_key.astype(F32),
        g_value.astype(F32),
        g_out,
        terms[shard : 2 * shard],
        columns(g_gate).astype(F32),
        columns(g_up).astype(F32),
        g_down.astype(F32),
    )


def solution(mesh):
    rows = P(("fsdp", "seq"), None)
    matrix = P("fsdp", None)
    vector = P("fsdp")
    in_specs = (rows, P(), rows) + (vector,) * 3 + (matrix,) * 4 + (vector,) + (matrix,) * 3
    out_specs = (rows, rows) + (vector,) * 3 + (matrix,) * 4 + (vector,) + (matrix,) * 3
    return jax.shard_map(local, mesh=mesh, in_specs=in_specs, out_specs=out_specs, check_vma=False)
```
